32 devices in a mesh: rows: 4 (over y, x), tm: 8 (over z, core).
Axes of the slice: x: 2, y: 2, z: 4, core: 2. Of those that a mesh axis runs over, the one named last changes fastest.
Arguments:
- frames: bfloat16 [4, 4, 1024, 512], P(None, 'rows', 'tm'), may hold values from -6 to 6
- segment_ids: int32 [4, 4, 1024], P(None, 'rows', 'tm'), may hold values from 0 to 16, as said below
- norm_gains: float32 [2, 5, 512], replicated, may hold values from 0.5 to 1.5
- feed_in: bfloat16 [2, 2, 512, 2048], replicated, may hold values from -0.25 to 0.25
- feed_out: bfloat16 [2, 2, 2048, 512], replicated, may hold values from -0.125 to 0.125
- attend_in: bfloat16 [2, 512, 1536], replicated, may hold values from -0.25 to 0.25
- attend_out: bfloat16 [2, 512, 512], replicated, may hold values from -1.5 to 1.5
- point_in: bfloat16 [2, 512, 1024], replicated, may hold values from -0.25 to 0.25
- depthwise: float32 [2, 9, 512], replicated, may hold values from -2 to 2
- stat_mean: float32 [2, 512], replicated, may hold values from -1.75 to 1.75
- stat_var: float32 [2, 512], replicated, may hold values from 0.2 to 2
- batch_scale: float32 [2, 512], replicated, may hold values from 0.5 to 1.5
- batch_shift: float32 [2, 512], replicated, may hold values from -1.75 to 1.75
- point_out: bfloat16 [2, 512, 512], replicated, may hold values from -0.25 to 0.25
- cotangent: bfloat16 [4, 4, 1024, 512], P(None, 'rows', 'tm'), may hold values from -6 to 6
Outputs:
- activations: bfloat16 [4, 4, 1024, 512], P(None, 'rows', 'tm')
- frames_grad: bfloat16 [4, 4, 1024, 512], P(None, 'rows', 'tm')
- gains_grad: float32 [2, 5, 512], P(None, None, 'tm')
- feed_in_grad: float32 [2, 2, 512, 2048], P(None, None, None, 'tm')
- feed_out_grad: float32 [2, 2, 2048, 512], P(None, None, None, 'tm')
- attend_in_grad: float32 [2, 512, 1536], P(None, None, 'tm')
- attend_out_grad: float32 [2, 512, 512], P(None, None, 'tm')
- point_in_grad: float32 [2, 512, 1024], P(None, None, 'tm')
- depthwise_grad: float32 [2, 9, 512], P(None, None, 'tm')
- scale_grad: float32 [2, 512], P(None, 'tm')
- shift_grad: float32 [2, 512], P(None, 'tm')
- point_out_grad: float32 [2, 512, 512], P(None, None, 'tm')
The draws below stay inside these ranges and needn't reach their ends.
Inputs may be any that keep to these rules, and one draw needn't show every extreme that they name: `segment_ids`: along each row the ids never fall and rise by one at a time; every utterance is shorter than 128 frames and lies within two adjacent blocks of 128 frames (frames j * 128 to (j + 2) * 128 - 1 for some j); every boundary between two blocks is crossed by an utterance.
All inputs are finite; a program needn't handle non-finite values.
Results may differ from the reference program's by a relative error of at most 0.023.
Values may be sent and summed in bfloat16 or wider, within the bound.
No kernel may reach another device: no remote copies, remote signals or barrier semaphores. Data moves between devices by JAX's collectives and lax.ppermute only.
A program may use at most 384 MiB of HBM per device.

```python
import math
import jax
import jax.numpy as jnp
from jax import lax

D = 512
FF = 2048
H = 8
HD = 64
KERNEL = 9
HALO = 4
BLK = 128
MB = 4
LAYERS = 2
NR = 4
LEN = 1024


def draw_segment_ids(key, part):
    key = jax.random.fold_in(key, 11)
    first_key, second_key = jax.random.split(key, 2)
    blocks = LEN // BLK
    shape = (MB, NR, blocks, 1)
    early_cut = jax.random.randint(first_key, shape, BLK // 8, 3 * BLK // 8)
    late_cut = jax.random.randint(second_key, shape, 5 * BLK // 8, 7 * BLK // 8)
    offset = jnp.arange(BLK).astype(jnp.int32)[None, None, None, :]
    block_number = jnp.arange(blocks).astype(jnp.int32)[None, None, :, None]
    counted = 2 * block_number + (offset >= early_cut).astype(jnp.int32) + (offset >= late_cut).astype(jnp.int32)
    return counted.reshape(MB, NR, LEN).astype(jnp.int32)


def steps_of(rng, dims, cuts, smallest, largest):
    def one(dim, parts):
        heights = jax.random.uniform(jax.random.fold_in(jax.random.fold_in(rng, 6), dim), (parts,), jnp.float32, smallest / len(cuts), largest / len(cuts))
        return jnp.repeat(jnp.exp(heights), dims[dim] // parts).reshape((-1,) + (1,) * (len(dims) - dim - 1))

    level = one(*cuts[0])
    for cut in cuts[1:]:
        level = level * one(*cut)
    return level


def bell_draw(key, dims, spread, limit, cuts=(), held_as=jnp.bfloat16):
    factor_of = steps_of(key, dims, cuts, -0.22, 0.18) if cuts else 1.0
    values = jax.random.normal(key, dims, jnp.float32) * spread * factor_of
    return jnp.minimum(jnp.maximum(values, -limit), limit).astype(held_as)


def setup_inputs(seed: int = 0) -> dict:
    keys = jax.random.split(jax.random.key(seed), 16)
    frames = bell_draw(keys[0], (MB, NR, LEN, D), 1.0, 6.0, ((1, 4), (2, 8)))
    segment_ids = draw_segment_ids(jax.random.fold_in(keys[15], 71), 0)
    norm_gains = jnp.clip(1.0 + 0.1 * jax.random.normal(keys[2], (LAYERS, 5, D), jnp.float32), 0.5, 1.5)
    feed_in = bell_draw(keys[3], (LAYERS, 2, D, FF), D ** -0.5, 0.25)
    feed_out = bell_draw(keys[4], (LAYERS, 2, FF, D), FF ** -0.5, 0.125)
    attend_in = bell_draw(keys[5], (LAYERS, D, 3 * D), D ** -0.5, 0.25)
    attend_out = bell_draw(keys[6], (LAYERS, D, D), (4 * D // BLK) ** -0.5, 1.5)
    point_in = bell_draw(keys[7], (LAYERS, D, 2 * D), D ** -0.5, 0.25)
    depthwise = bell_draw(keys[8], (LAYERS, KERNEL, D), KERNEL ** -0.5, 2.0, (), jnp.float32)
    stat_mean = bell_draw(keys[9], (LAYERS, D), 0.3, 1.75, (), jnp.float32)
    stat_var = jnp.clip(jnp.exp(jax.random.uniform(keys[10], (LAYERS, D), jnp.float32, math.log(0.2), math.log(2.0))), 0.2, 2.0)
    batch_scale = jnp.clip(1.0 + 0.1 * jax.random.normal(keys[11], (LAYERS, D), jnp.float32), 0.5, 1.5)
    batch_shift = bell_draw(keys[12], (LAYERS, D), 0.3, 1.75, (), jnp.float32)
    point_out = bell_draw(keys[13], (LAYERS, D, D), D ** -0.5, 0.25)
    cotangent = bell_draw(keys[14], (MB, NR, LEN, D), 1.0, 6.0, ((1, 4), (2, 8)))
    return {"frames": frames, "segment_ids": segment_ids, "norm_gains": norm_gains, "feed_in": feed_in, "feed_out": feed_out, "attend_in": attend_in, "attend_out": attend_out, "point_in": point_in, "depthwise": depthwise, "stat_mean": stat_mean, "stat_var": stat_var, "batch_scale": batch_scale, "batch_shift": batch_shift, "point_out": point_out, "cotangent": cotangent}


EPSILON = 1e-05
MASKED = -1e+30
PRECISE = lax.Precision.HIGHEST

@jax.custom_vjp
def low(v):
    return lax.optimization_barrier(v.astype(jnp.bfloat16)).astype(jnp.float32)

@jax.custom_vjp
def low_back(v):
    return v

def low_keep(v):
    return (low(v), None)

def low_pass(kept, grad):
    return (grad,)

def back_keep(v):
    return (v, None)

def back_low(kept, grad):
    return (low(grad),)
low.defvjp(low_keep, low_pass)
low_back.defvjp(back_keep, back_low)

def matmul(left, right):
    return jnp.dot(left, right, precision=PRECISE, preferred_element_type=jnp.float32)

def layer_norm(values, gain):
    centred = values - lax.optimization_barrier(jnp.mean(values, axis=-1, keepdims=True))
    variance = lax.optimization_barrier(jnp.mean(centred * centred, axis=-1, keepdims=True))
    return centred * lax.rsqrt(variance + EPSILON) * gain

def rotate(values, cosine, sine):
    half_dim = values.shape[-1] // 2
    first, second = (values[..., :half_dim], values[..., half_dim:])
    cos_rows, sin_rows = (cosine[:, None, :], sine[:, None, :])
    return jnp.concatenate([first * cos_rows - second * sin_rows, second * cos_rows + first * sin_rows], axis=-1)

def feed_forward(stream, gain, w_in, w_out):
    active = low(layer_norm(stream, gain))
    hidden = low_back(matmul(active, w_in))
    swish = low(jax.nn.silu(hidden))
    return low_back(matmul(swish, w_out))

def attend(stream, gain, w_in, w_out, row_ids, cosine, sine):
    length = stream.shape[0]
    active = low(layer_norm(stream, gain))
    projected = low_back(matmul(active, w_in)).reshape(length, 3, H, HD)
    queries = low(rotate(projected[:, 0], cosine, sine))
    keyed = low(rotate(projected[:, 1], cosine, sine))
    valued = low(projected[:, 2])
    span = math.gcd(length, 512)
    count = length // span
    width = span + 2 * BLK
    key_pad = jnp.pad(keyed, ((BLK, BLK), (0, 0), (0, 0)))
    value_pad = jnp.pad(valued, ((BLK, BLK), (0, 0), (0, 0)))
    id_pad = jnp.pad(row_ids, BLK, constant_values=-1)
    starts = (jnp.arange(count) * span).astype(jnp.int32)

    def one_block(pieces):
        query_block, block_ids, start = pieces
        near_keys = lax.dynamic_slice_in_dim(key_pad, start, width, 0)
        near_values = lax.dynamic_slice_in_dim(value_pad, start, width, 0)
        near_ids = lax.dynamic_slice_in_dim(id_pad, start, width, 0)
        raw = jnp.einsum('qhe,khe->hqk', query_block, near_keys, precision=PRECISE) * HD ** (-0.5)
        same = (block_ids[:, None] == near_ids[None, :])[None]
        scores = low_back(jnp.where(same, raw, MASKED))
        weights = low(jax.nn.softmax(scores, axis=-1))
        return jnp.einsum('hqk,khe->qhe', weights, near_values, precision=PRECISE)
    attended = lax.map(jax.checkpoint(one_block), (queries.reshape(count, span, H, HD), row_ids.reshape(count, span), starts))
    attended = low(low_back(attended.reshape(length, D)))
    return low_back(matmul(attended, w_out))

def convolve(stream, gain, w_in, w_depth, mean_stat, var_stat, bn_gain, bn_bias, w_out, row_ids):
    length = stream.shape[0]
    active = low(layer_norm(stream, gain))
    upper = low_back(matmul(active, w_in))
    gated = low(upper[:, :D] * jax.nn.sigmoid(upper[:, D:]))
    padded = jnp.pad(gated, ((HALO, HALO), (0, 0)))
    pad_ids = jnp.pad(row_ids, HALO, constant_values=-1)
    depth = jnp.zeros_like(gated)
    for offset in range(KERNEL):
        same = (pad_ids[offset:offset + length] == row_ids).astype(gated.dtype)
        depth = depth + w_depth[offset] * padded[offset:offset + length] * same[:, None]
    depth = low_back(depth)
    normed = (depth - mean_stat) * lax.rsqrt(var_stat + EPSILON) * bn_gain + bn_bias
    return low_back(matmul(low(jax.nn.silu(normed)), w_out))

def one_layer(weights, frozen, stream, row_ids, cosine, sine):
    gain_rows, w_feed_in, w_feed_out, w_attend_in, w_attend_out, w_point_in, w_depth, bn_gain, bn_bias, w_point_out = weights
    mean_stat, var_stat = frozen
    stream = stream + 0.5 * feed_forward(stream, gain_rows[0], w_feed_in[0], w_feed_out[0])
    stream = stream + attend(stream, gain_rows[1], w_attend_in, w_attend_out, row_ids, cosine, sine)
    stream = stream + convolve(stream, gain_rows[2], w_point_in, w_depth, mean_stat, var_stat, bn_gain, bn_bias, w_point_out, row_ids)
    stream = stream + 0.5 * feed_forward(stream, gain_rows[3], w_feed_in[1], w_feed_out[1])
    return layer_norm(stream, gain_rows[4])

def forward(params, frozen, stream, row_ids, cosine, sine):
    for layer_index in range(LAYERS):
        weights = tuple((param[layer_index] for param in params))
        stats = tuple((stat[layer_index] for stat in frozen))
        stream = one_layer(weights, stats, stream, row_ids, cosine, sine)
    return stream

def reference(frames, segment_ids, norm_gains, feed_in, feed_out, attend_in, attend_out, point_in, depthwise, stat_mean, stat_var, batch_scale, batch_shift, point_out, cotangent):
    params = tuple((param.astype(jnp.float32) for param in (norm_gains, feed_in, feed_out, attend_in, attend_out, point_in, depthwise, batch_scale, batch_shift, point_out)))
    frozen = (stat_mean.astype(jnp.float32), stat_var.astype(jnp.float32))
    length = frames.shape[2]
    half_dim = HD // 2
    frequency = 10000.0 ** (-jnp.arange(half_dim).astype(jnp.float32) / half_dim)
    indices = jnp.arange(length).astype(jnp.int32)
    rows_in = frames.reshape(-1, length, D).astype(jnp.float32)
    rows_ids = segment_ids.reshape(-1, length)
    rows_grad = cotangent.reshape(-1, length, D).astype(jnp.float32)

    def row_step(totals, pieces):
        stream, row_ids, grad = pieces
        starts_here = jnp.concatenate([jnp.ones((1,), jnp.bool_), row_ids[1:] != row_ids[:-1]])
        opening = lax.cummax(jnp.where(starts_here, indices, 0).astype(jnp.int32), axis=0)
        position = (indices - opening).astype(jnp.float32)
        angle = position[:, None] * frequency[None, :]
        cosine, sine = (jnp.cos(angle), jnp.sin(angle))

        def apply(weights, values):
            return forward(weights, frozen, values, row_ids, cosine, sine)
        result, pull = jax.vjp(apply, params, stream)
        param_grads, input_grad = pull(grad)
        totals = jax.tree.map(jnp.add, totals, param_grads)
        return (totals, (result.astype(jnp.bfloat16), input_grad.astype(jnp.bfloat16)))
    zeros = tuple((jnp.zeros_like(param) for param in params))
    totals, (results, input_grads) = lax.scan(row_step, zeros, (rows_in, rows_ids, rows_grad))
    return (results.reshape(frames.shape), input_grads.reshape(frames.shape)) + tuple(totals)
```

```python
import functools

import jax
import jax.numpy as jnp
import numpy as np
from jax import lax
from jax.experimental import pallas as pl
from jax.experimental.pallas import tpu as pltpu
from jax.sharding import PartitionSpec as P

HD = 64
KERNEL = 9
HALO = 4
EPSILON = 1e-05
MASKED = -1e30
BF = jnp.bfloat16
F32 = jnp.float32
D = 512
FF = 2048
BLK = 128
ROW_CHOICES = (640, 1024)
CAP = ROW_CHOICES[-1]
LANES = 256
PAIRS = D // 128
VMEM_LIMIT = 60 * 2**20
ANY = pl.BlockSpec(memory_space=pl.ANY)
VMEM = pl.BlockSpec(memory_space=pltpu.VMEM)
SMEM = pl.BlockSpec(memory_space=pltpu.SMEM)


def shifted(array, axis, by):
    size = lax.axis_size(axis)
    pairs = [(i, i + by) for i in range(size) if 0 <= i + by < size]
    return lax.ppermute(array, axis, pairs)


def struct(shape, dtype):
    return jax.ShapeDtypeStruct(shape, dtype)


def call(body, ins, outs, scratch, args, flops=0, moved=0, name="kernel"):
    return pl.pallas_call(
        body,
        out_shape=[s for s, _ in outs],
        in_specs=ins,
        out_specs=[b for _, b in outs],
        scratch_shapes=scratch,
        compiler_params=pltpu.CompilerParams(vmem_limit_bytes=VMEM_LIMIT),
        cost_estimate=pl.CostEstimate(flops=int(flops), bytes_accessed=int(moved), transcendentals=0),
        name=name,
    )(*args)


def dot_nn(a, b):
    return jnp.dot(a, b, preferred_element_type=F32)


def dot_nt(a, b):
    return lax.dot_general(a, b, (((1,), (1,)), ((), ())), preferred_element_type=F32)


def dot_tn(a, b):
    return lax.dot_general(a, b, (((0,), (0,)), ((), ())), preferred_element_type=F32)


def sigmoid(v):
    return 0.5 + 0.5 * jnp.tanh(0.5 * v)


def normalise(x):
    c = x - jnp.mean(x, axis=-1, keepdims=True)
    inv = lax.rsqrt(jnp.mean(c * c, axis=-1, keepdims=True) + EPSILON)
    return c * inv, inv


def norm_back(grad, xhat, inv, gain):
    w = grad * gain
    return inv * (
        w - jnp.mean(w, axis=-1, keepdims=True) - xhat * jnp.mean(w * xhat, axis=-1, keepdims=True)
    )


def fold(v):
    return jnp.sum(v.reshape(v.shape[0] // 8, 8, v.shape[1]), axis=0)


def total(v):
    return jnp.sum(v, axis=0, keepdims=True)


def by_rows(n_ref, body):
    low = 0
    for rows in ROW_CHOICES:
        n = n_ref[0]
        cond = n > low
        if rows != CAP:
            cond = cond & (n <= rows)

        @pl.when(cond)
        def _(rows=rows):
            body(rows)

        low = rows


def blocks(rows, step, init=None, size=128):
    def wrapped(i, carry):
        at = pl.ds(pl.multiple_of(i * size, size), size)
        return step(i, at, carry)

    return lax.fori_loop(0, rows // size, wrapped, init if init is not None else jnp.int32(0))


def rope_tables():
    half = HD // 2
    freq = np.power(np.float32(10000.0), -(np.arange(half).astype(np.float32) / np.float32(half)))
    angle = np.arange(BLK).astype(np.float32)[:, None] * freq.astype(np.float32)[None, :]
    cos = np.cos(angle.astype(np.float64))
    sin = np.sin(angle.astype(np.float64))
    full = (np.concatenate([cos] * 4, axis=1), np.concatenate([-sin, sin] * 2, axis=1))
    parts = []
    for table in full:
        rest = table
        for _ in range(3):
            piece = rest.astype(jnp.bfloat16)
            parts.append(piece)
            rest = rest - piece.astype(np.float64)
    return np.stack(parts)


def pack_body(keep_ref, key_ref, keyc_ref, win_ref, tab_ref, x_ref, p_ref, cos_ref, sin_ref, kb_ref, kr_ref, dest_s, pos_s):
    count = keep_ref.shape[1]
    win = count // 4
    keep = keep_ref[...]
    before = (
        lax.broadcasted_iota(jnp.int32, (count, count), 0) < lax.broadcasted_iota(jnp.int32, (count, count), 1)
    ).astype(F32).astype(BF)
    dest = dot_nn(jnp.broadcast_to(keep, (8, count)).astype(BF), before)
    dest_s[...] = jnp.where(jnp.broadcast_to(keep, (8, count)) > 0.5, dest, -1.0)
    earlier = lax.broadcasted_iota(jnp.int32, (win, win), 0) < lax.broadcasted_iota(jnp.int32, (win, win), 1)
    for m in range(4):
        at = pl.ds(m * win, win)
        same = (keyc_ref[at, :] == key_ref[:, at]) & earlier
        pos_s[:, at] = jnp.broadcast_to(jnp.sum(jnp.where(same, 1.0, 0.0), axis=0, keepdims=True), (8, win))
    kr_ref[...] = jnp.full(kr_ref.shape, -1.0, F32)

    def step(i, at, carry):
        row = (lax.broadcasted_iota(jnp.int32, (BLK, count), 0) + i * BLK).astype(F32)
        pick = jnp.where(dest_s[0:1, :] == row, 1.0, 0.0)
        p = pick.astype(BF)
        p_ref[at, :] = p
        x_ref[at, :] = dot_nn(p, win_ref[...])
        key = jnp.broadcast_to(jnp.sum(pick * key_ref[...], axis=1, keepdims=True), (BLK, BLK))
        kb_ref[at, :] = key
        kr_ref[:, pl.ds(pl.multiple_of(i * BLK + BLK, BLK), BLK)] = key.T[0:8]
        pos = jnp.sum(pick * pos_s[0:1, :], axis=1, keepdims=True)
        hot = (lax.broadcasted_iota(jnp.int32, (BLK, BLK), 1).astype(F32) == pos).astype(F32).astype(BF)
        cos_ref[at, :] = dot_nn(hot, tab_ref[0]) + dot_nn(hot, tab_ref[1]) + dot_nn(hot, tab_ref[2])
        sin_ref[at, :] = dot_nn(hot, tab_ref[3]) + dot_nn(hot, tab_ref[4]) + dot_nn(hot, tab_ref[5])
        return carry

    blocks(count, step)


def pack(keep, key, window):
    count = keep.shape[0]
    return call(
        pack_body,
        [VMEM] * 5,
        [
            (struct((CAP, D), F32), VMEM),
            (struct((CAP, count), BF), VMEM),
            (struct((CAP, 128), F32), VMEM),
            (struct((CAP, 128), F32), VMEM),
            (struct((CAP, 128), F32), VMEM),
            (struct((8, CAP + 2 * BLK), F32), VMEM),
        ],
        [pltpu.VMEM((8, count), F32), pltpu.VMEM((8, count), F32)],
        (keep[None, :], key[None, :], key[:, None], window, jnp.asarray(rope_tables(), dtype=BF)),
        flops=2 * count * count * D,
        moved=8 * 2**20,
        name="pack",
    )


def lane_low(shape):
    return lax.broadcasted_iota(jnp.int32, shape, 1) % HD < HD // 2


def swap_halves(v):
    return jnp.where(lane_low(v.shape), pltpu.roll(v, 128 - HD // 2, 1), pltpu.roll(v, HD // 2, 1))


def stacked(v):
    first = lax.broadcasted_iota(jnp.int32, v.shape, 1) < HD
    zero = jnp.zeros_like(v)
    return jnp.concatenate([jnp.where(first, v, zero), jnp.where(first, zero, v)], axis=0)


def unstacked(v):
    half = v.shape[0] // 2
    first = lax.broadcasted_iota(jnp.int32, (half, 128), 1) < HD
    return jnp.where(first, v[:half], v[half:])


def norm_into(x_ref, gain, a_ref, rows):
    def step(i, at, carry):
        xhat, _ = normalise(x_ref[at, :])
        a_ref[at, :] = (xhat * gain).astype(BF)
        return carry

    blocks(rows, step)


def forward_body(
    n_ref, x0_ref, cos_ref, sin_ref, kb_ref, kr_ref, gains_ref, taps_ref, mean_ref, var_ref, scale_ref, shift_ref,
    fin_h, fout_h, ain_h, aout_h, pin_h, pout_h,
    act_ref, xs_h, hs_h, q_h, kv_h, at_h, o_h, u_h, z_h,
    fin, fout, ain, aout, pin, pout, xb, hb, qb, kvb, ab, ob, ub, zb, a_s, gp, kp, w_sem, s_sem,
):
    layers = gains_ref.shape[0]
    weights = [
        (fin_h, (0,), fin.at[0]), (fout_h, (0,), fout.at[0]), (ain_h, (), ain), (aout_h, (), aout),
        (pin_h, (), pin), (pout_h, (), pout), (fin_h, (1,), fin.at[1]), (fout_h, (1,), fout.at[1]),
    ]

    def weight_copy(i, l):
        src, sub, dst = weights[i]
        return pltpu.make_async_copy(src.at[(l,) + sub], dst, w_sem.at[i])

    for i in range(len(weights)):
        weight_copy(i, 0).start()

    def run(rows):
        tiles = rows // BLK
        top = pl.ds(0, rows)
        saves = [(xb.at[i, top], lambda l, i=i: xs_h.at[l, i, top]) for i in range(5)]
        saves += [(hb.at[k, top], lambda l, k=k: hs_h.at[l, k, top]) for k in range(2)]
        saves += [
            (qb.at[top], lambda l: q_h.at[l, top]),
            (kvb.at[pl.ds(0, rows + 2 * BLK)], lambda l: kv_h.at[l, pl.ds(0, rows + 2 * BLK)]),
            (ab.at[pl.ds(0, tiles)], lambda l: at_h.at[l, pl.ds(0, tiles)]),
            (ob.at[top], lambda l: o_h.at[l, top]),
            (ub.at[top], lambda l: u_h.at[l, top]),
            (zb.at[top], lambda l: z_h.at[l, top]),
        ]

        def save(i, l):
            src, dst = saves[i]
            return pltpu.make_async_copy(src, dst(l), s_sem.at[i])

        def settle(i, l):
            @pl.when(l > 0)
            def _():
                save(i, l - 1).wait()

        def use(i, l):
            weight_copy(i, l).wait()

        def next_weight(i, l):
            @pl.when(l + 1 < layers)
            def _():
                weight_copy(i, l + 1).start()

        kvb[pl.ds(0, BLK), :] = jnp.zeros((BLK, 2 * D), BF)
        kvb[pl.ds(rows + BLK, BLK), :] = jnp.zeros((BLK, 2 * D), BF)
        gp[pl.ds(0, 8), :] = jnp.zeros((8, D), F32)
        gp[pl.ds(rows + 8, 8), :] = jnp.zeros((8, D), F32)
        kp[pl.ds(0, 8), :] = jnp.full((8, 128), -1.0, F32)
        kp[pl.ds(rows + 8, 8), :] = jnp.full((8, 128), -1.0, F32)

        def fill(i, at, carry):
            kp[pl.ds(pl.multiple_of(i * BLK + 8, 8), BLK), :] = kb_ref[at, :]
            xb[0, at, :] = x0_ref[at, :]
            return carry

        blocks(rows, fill)

        def feed(l, k, src, dst, gain, wi):
            settle(5 + k, l)
            settle(dst, l)

            def first(i, at, carry):
                x = xb[src, at, :]
                xhat, _ = normalise(x)
                a_s[at, :] = (xhat * gain).astype(BF)
                xb[dst, at, :] = x
                return carry

            blocks(rows, first)
            use(wi, l)
            use(wi + 1, l)

            def chunk(c, carry):
                cols = pl.ds(pl.multiple_of(c * 512, 512), 512)
                h = dot_nn(a_s[top, :], fin[k, :, cols])
                hb[k, top, cols] = h.astype(BF)
                s = (h * sigmoid(h)).astype(BF)
                xb[dst, top, :] = xb[dst, top, :] + 0.5 * dot_nn(s, fout[k, cols, :])
                return carry

            lax.fori_loop(0, FF // 512, chunk, jnp.int32(0))
            next_weight(wi, l)
            next_weight(wi + 1, l)
            save(5 + k, l).start()
            save(dst, l).start()

        def layer(l, carry):
            gains = [gains_ref[l, pl.ds(i, 1), :] for i in range(5)]
            save(0, l).start()
            feed(l, 0, 0, 1, gains[0], 0)

            norm_into(xb.at[1], gains[1], a_s, rows)
            settle(7, l)
            settle(8, l)
            settle(9, l)
            settle(10, l)
            use(2, l)
            for part in range(3):
                proj = dot_nn(a_s[top, :], ain[:, part * D : (part + 1) * D])
                for p in range(PAIRS):
                    lanes = slice(p * 128, (p + 1) * 128)
                    v = proj[:, lanes]
                    if part < 2:
                        v = v * cos_ref[top, :] + swap_halves(v) * sin_ref[top, :]
                    if part == 0:
                        qb[top, lanes] = (v * HD**-0.5).astype(BF)
                    elif part == 1:
                        kvb[pl.ds(BLK, rows), lanes] = v.astype(BF)
                    else:
                        kvb[pl.ds(BLK, rows), D + p * 128 : D + (p + 1) * 128] = v.astype(BF)
            next_weight(2, l)

            def tile(t, at, c):
                near = pl.ds(pl.multiple_of(t * BLK, BLK), 3 * BLK)
                same = kb_ref[at, 0:1] == kr_ref[0:1, near]
                same = jnp.concatenate([same, same], axis=0)
                for p in range(PAIRS):
                    lanes = slice(p * 128, (p + 1) * 128)
                    s = dot_nt(stacked(qb[at, lanes]), kvb[near, lanes])
                    s = jnp.where(same, s, MASKED)
                    e = jnp.exp(s - jnp.max(s, axis=-1, keepdims=True))
                    e = e / jnp.sum(e, axis=-1, keepdims=True)
                    low = e.astype(BF)
                    ab[t, p] = low
                    o = dot_nn(low, kvb[near, D + p * 128 : D + (p + 1) * 128])
                    ob[at, lanes] = unstacked(o).astype(BF)
                return c

            blocks(rows, tile)
            settle(2, l)
            use(3, l)
            xb[2, top, :] = xb[1, top, :] + dot_nn(ob[top, :], aout[...])
            next_weight(3, l)
            for i in (7, 8, 9, 10, 2):
                save(i, l).start()

            norm_into(xb.at[2], gains[2], a_s, rows)
            settle(11, l)
            settle(12, l)
            use(4, l)
            for half in range(2):
                lanes = slice(half * 256, (half + 1) * 256)
                up1 = dot_nn(a_s[top, :], pin[:, half * 256 : (half + 1) * 256])
                up2 = dot_nn(a_s[top, :], pin[:, D + half * 256 : D + (half + 1) * 256])
                ub[top, lanes] = up1.astype(BF)
                ub[top, D + half * 256 : D + (half + 1) * 256] = up2.astype(BF)
                gp[pl.ds(8, rows), lanes] = (up1 * sigmoid(up2)).astype(BF).astype(F32)
            next_weight(4, l)
            rs = lax.rsqrt(var_ref[pl.ds(l, 1), :] + EPSILON)
            mean = mean_ref[pl.ds(l, 1), :]
            scale = scale_ref[pl.ds(l, 1), :]
            shift = shift_ref[pl.ds(l, 1), :]

            def conv(t, at, c):
                wide = pl.ds(pl.multiple_of(t * BLK, BLK), BLK + 16)
                keys = kp[wide, :]
                own = keys[8 : 8 + BLK]
                masks = [keys[4 + o : 4 + o + BLK] == own for o in range(KERNEL)]
                for p in range(PAIRS):
                    lanes = slice(p * 128, (p + 1) * 128)
                    g = gp[wide, lanes]
                    z = jnp.zeros((BLK, 128), F32)
                    for o in range(KERNEL):
                        w = taps_ref[l, o : o + 1, lanes]
                        z = z + jnp.where(masks[o], w * g[4 + o : 4 + o + BLK], 0.0)
                    zb[at, lanes] = z
                    b = (z - mean[:, lanes]) * rs[:, lanes] * scale[:, lanes] + shift[:, lanes]
                    a_s[at, lanes] = (b * sigmoid(b)).astype(BF)
                return c

            blocks(rows, conv)
            settle(3, l)
            use(5, l)
            xb[3, top, :] = xb[2, top, :] + dot_nn(a_s[top, :], pout[...])
            next_weight(5, l)
            for i in (11, 12, 3):
                save(i, l).start()

            feed(l, 1, 3, 4, gains[3], 6)
            save(0, l).wait()

            def last(i, at, c):
                xhat, _ = normalise(xb[4, at, :])
                y = xhat * gains[4]
                xb[0, at, :] = y
                act_ref[at, :] = y.astype(BF)
                return c

            blocks(rows, last)
            return carry

        lax.fori_loop(0, layers, layer, jnp.int32(0))
        for i in range(1, len(saves)):
            save(i, layers - 1).wait()
        if rows < CAP:
            act_ref[pl.ds(rows, CAP - rows), :] = jnp.zeros((CAP - rows, D), BF)

    by_rows(n_ref, run)


def forward(n, x0, cos, sin, kb, kr, small, mats):
    layers = small[0].shape[0]
    outs = [
        (struct((CAP, D), BF), VMEM),
        (struct((layers, 5, CAP, D), F32), ANY),
        (struct((layers, 2, CAP, FF), BF), ANY),
        (struct((layers, CAP, D), BF), ANY),
        (struct((layers, CAP + 2 * BLK, 2 * D), BF), ANY),
        (struct((layers, CAP // BLK, PAIRS, 2 * BLK, 3 * BLK), BF), ANY),
        (struct((layers, CAP, D), BF), ANY),
        (struct((layers, CAP, 2 * D), BF), ANY),
        (struct((layers, CAP, D), F32), ANY),
    ]
    vm = pltpu.VMEM
    scratch = [
        vm((2, D, FF), BF), vm((2, FF, D), BF), vm((D, 3 * D), BF), vm((D, D), BF), vm((D, 2 * D), BF), vm((D, D), BF),
        vm((5, CAP, D), F32), vm((2, CAP, FF), BF), vm((CAP, D), BF), vm((CAP + 2 * BLK, 2 * D), BF),
        vm((CAP // BLK, PAIRS, 2 * BLK, 3 * BLK), BF), vm((CAP, D), BF), vm((CAP, 2 * D), BF), vm((CAP, D), F32),
        vm((CAP, D), BF), vm((CAP + 16, D), F32), vm((CAP + 16, 128), F32),
        pltpu.SemaphoreType.DMA((8,)), pltpu.SemaphoreType.DMA((13,)),
    ]
    return call(
        forward_body,
        [SMEM] + [VMEM] * 11 + [ANY] * 6,
        outs,
        scratch,
        (n, x0, cos, sin, kb, kr, *small, *mats),
        flops=2 * 640 * 12e6,
        moved=60 * 2**20,
        name="forward",
    )


def place(keep_ref, send_ref, core, at, pair):
    even = core == 0
    keep_ref[at] = jnp.where(even, pair[0], pair[1]).astype(BF)
    send_ref[at] = jnp.where(even, pair[1], pair[0]).astype(BF)


def feed_back_body(l, k, n_ref, core_ref, g_ref, gains_ref, xs_h, hs_h, fin_h, fout_h, *rest):
    final = k == 1
    out_ref, keep_ref, send_ref, small_ref, x_s, x4_s, h_s, fin, fout, gl_s, a_s, da_s, sem = rest
    core = core_ref[0]
    gain = gains_ref[l, pl.ds(3 if final else 0, 1), :]
    gain4 = gains_ref[l, pl.ds(4, 1), :]

    def run(rows):
        top = pl.ds(0, rows)
        copies = [
            pltpu.make_async_copy(xs_h.at[l, 3 if final else 0, top], x_s.at[top], sem.at[0]),
            pltpu.make_async_copy(hs_h.at[l, k, top], h_s.at[top], sem.at[2]),
            pltpu.make_async_copy(fout_h.at[l, k], fout, sem.at[3]),
            pltpu.make_async_copy(fin_h.at[l, k], fin, sem.at[4]),
        ]
        if final:
            copies.insert(0, pltpu.make_async_copy(xs_h.at[l, 4, top], x4_s.at[top], sem.at[1]))
        for c in copies:
            c.start()
        if final:
            copies[0].wait()
        copies[-4].wait()

        def first(i, at, carry):
            g = g_ref[at, :]
            if final:
                xhat, inv = normalise(x4_s[at, :])
                carry = carry + fold(g * xhat)
                g = norm_back(g, xhat, inv, gain4)
            out_ref[at, :] = g
            gl_s[at, :] = (0.5 * g).astype(BF)
            xhat, _ = normalise(x_s[at, :])
            a_s[at, :] = (xhat * gain).astype(BF)
            da_s[at, :] = jnp.zeros((BLK, D), F32)
            return carry

        gain4_grad = blocks(rows, first, jnp.zeros((8, D), F32))
        for c in copies[-3:]:
            c.wait()

        def chunk(c, carry):
            cols = pl.ds(pl.multiple_of(c * 512, 512), 512)
            h = h_s[top, cols].astype(F32)
            sig = sigmoid(h)
            s = (h * sig).astype(BF)
            ds = dot_nt(gl_s[top, :], fout[cols, :])
            dh = (ds * (sig * (1.0 + h * (1.0 - sig)))).astype(BF)
            dwi = dot_tn(a_s[top, :], dh)
            place(keep_ref, send_ref, core, (c, pl.ds(0, D), slice(None)), (dwi[:, :LANES], dwi[:, LANES:]))
            dwo = dot_tn(gl_s[top, :], s)
            for z in range(4):
                for b in range(2):
                    pair = [
                        dwo[z * 128 + q * 64 : z * 128 + q * 64 + 64, b * LANES : (b + 1) * LANES] for q in range(2)
                    ]
                    at = pl.ds(pl.multiple_of(D + (2 * c + b) * 64, 64), 64)
                    place(keep_ref, send_ref, core, (z, at, slice(None)), pair)
            da_s[top, :] = da_s[top, :] + dot_nt(dh, fin[:, cols])
            return carry

        lax.fori_loop(0, FF // 512, chunk, jnp.int32(0))

        def last(i, at, carry):
            xhat, inv = normalise(x_s[at, :])
            da = da_s[at, :]
            out_ref[at, :] = out_ref[at, :] + norm_back(da, xhat, inv, gain)
            return carry + fold(da * xhat)

        gain_grad = blocks(rows, last, jnp.zeros((8, D), F32))
        small_ref[0:1, :] = total(gain_grad)
        small_ref[1:2, :] = total(gain4_grad)
        if rows < CAP:
            out_ref[pl.ds(rows, CAP - rows), :] = jnp.zeros((CAP - rows, D), F32)

    by_rows(n_ref, run)


def feed_back(l, k, n, core, g, gains, xs, hs, fin, fout):
    vm = pltpu.VMEM
    return call(
        functools.partial(feed_back_body, l, k),
        [SMEM, SMEM, VMEM, VMEM] + [ANY] * 4,
        [
            (struct((CAP, D), F32), VMEM),
            (struct((4, 1024, LANES), BF), VMEM),
            (struct((4, 1024, LANES), BF), VMEM),
            (struct((8, D), F32), VMEM),
        ],
        [
            vm((CAP, D), F32), vm((CAP, D), F32), vm((CAP, FF), BF), vm((D, FF), BF), vm((FF, D), BF),
            vm((CAP, D), BF), vm((CAP, D), BF), vm((CAP, D), F32), pltpu.SemaphoreType.DMA((5,)),
        ],
        (n, core, g, gains, xs, hs, fin, fout),
        flops=8 * 640 * D * FF,
        moved=16 * 2**20,
        name=f"feed_back_{l}_{k}",
    )


def conv_back_body(
    l, n_ref, core_ref, g_ref, kb_ref, gains_ref, taps_ref, mean_ref, var_ref, scale_ref, shift_ref,
    xs_h, u_h, z_h, pin_h, pout_h,
    out_ref, keep_ref, send_ref, small_ref,
    x_s, u_s, z_s, pin, pout, gl_s, a_s, e_s, de_s, gp, dzp, kp, du_s, sem,
):
    core = core_ref[0]
    gain = gains_ref[l, pl.ds(2, 1), :]
    rs = lax.rsqrt(var_ref[pl.ds(l, 1), :] + EPSILON)
    mean = mean_ref[pl.ds(l, 1), :]
    scale = scale_ref[pl.ds(l, 1), :]
    shift = shift_ref[pl.ds(l, 1), :]

    def run(rows):
        top = pl.ds(0, rows)
        copies = [
            pltpu.make_async_copy(pout_h.at[l], pout, sem.at[0]),
            pltpu.make_async_copy(z_h.at[l, top], z_s.at[top], sem.at[1]),
            pltpu.make_async_copy(u_h.at[l, top], u_s.at[top], sem.at[2]),
            pltpu.make_async_copy(xs_h.at[l, 2, top], x_s.at[top], sem.at[3]),
            pltpu.make_async_copy(pin_h.at[l], pin, sem.at[4]),
        ]
        for c in copies:
            c.start()
        for ref, width, value in ((gp, D, 0.0), (dzp, D, 0.0), (kp, 128, -1.0)):
            ref[pl.ds(0, 8), :] = jnp.full((8, width), value, F32)
            ref[pl.ds(rows + 8, 8), :] = jnp.full((8, width), value, F32)

        def low(i, at, carry):
            gl_s[at, :] = g_ref[at, :].astype(BF)
            kp[pl.ds(pl.multiple_of(i * BLK + 8, 8), BLK), :] = kb_ref[at, :]
            return carry

        blocks(rows, low)
        copies[0].wait()
        de_s[top, :] = dot_nt(gl_s[top, :], pout[...])
        for c in copies[1:]:
            c.wait()

        def first(i, at, carry):
            scale_grad, shift_grad = carry
            inner = pl.ds(pl.multiple_of(i * BLK + 8, 8), BLK)
            hat = (z_s[at, :] - mean) * rs
            b = hat * scale + shift
            sig = sigmoid(b)
            e_s[at, :] = (b * sig).astype(BF)
            db = de_s[at, :] * (sig * (1.0 + b * (1.0 - sig)))
            dzp[inner, :] = (db * scale * rs).astype(BF).astype(F32)
            u1 = u_s[at, pl.ds(0, D)].astype(F32)
            u2 = u_s[at, pl.ds(D, D)].astype(F32)
            gp[inner, :] = (u1 * sigmoid(u2)).astype(BF).astype(F32)
            xhat, _ = normalise(x_s[at, :])
            a_s[at, :] = (xhat * gain).astype(BF)
            return (scale_grad + fold(db * hat), shift_grad + fold(db))

        zero = jnp.zeros((8, D), F32)
        scale_grad, shift_grad = blocks(rows, first, (zero, zero))
        small_ref[...] = jnp.zeros(small_ref.shape, F32)
        small_ref[1:2, :] = total(scale_grad)
        small_ref[2:3, :] = total(shift_grad)

        for p in range(PAIRS):
            lanes = slice(p * 128, (p + 1) * 128)

            def taps(t, at, carry, lanes=lanes, p=p):
                wide = pl.ds(pl.multiple_of(t * BLK, BLK), BLK + 16)
                keys = kp[wide, :]
                own = keys[8 : 8 + BLK]
                g = gp[wide, lanes]
                dz = dzp[wide, lanes]
                dz_own = dz[8 : 8 + BLK]
                dg = jnp.zeros((BLK, 128), F32)
                sums = []
                for o in range(KERNEL):
                    mask = keys[4 + o : 4 + o + BLK] == own
                    sums.append(carry[o] + fold(jnp.where(mask, dz_own * g[4 + o : 4 + o + BLK], 0.0)))
                    w = taps_ref[l, KERNEL - 1 - o : KERNEL - o, lanes]
                    dg = dg + jnp.where(mask, w * dz[4 + o : 4 + o + BLK], 0.0)
                u1 = u_s[at, lanes].astype(F32)
                sig = sigmoid(u_s[at, D + p * 128 : D + (p + 1) * 128].astype(F32))
                du_s[at, lanes] = (dg * sig).astype(BF)
                du_s[at, D + p * 128 : D + (p + 1) * 128] = (dg * u1 * sig * (1.0 - sig)).astype(BF)
                return tuple(sums)

            sums = blocks(rows, taps, tuple(jnp.zeros((8, 128), F32) for _ in range(KERNEL)))
            for o in range(KERNEL):
                small_ref[8 + o : 9 + o, lanes] = total(sums[o])

        for z in range(4):
            dwi = dot_tn(a_s[top, :], du_s[top, z * 256 : (z + 1) * 256])
            pair = [
                jnp.concatenate(
                    [dwi[: D // 2, q * 128 : (q + 1) * 128], dwi[D // 2 :, q * 128 : (q + 1) * 128]], axis=1
                )
                for q in range(2)
            ]
            place(keep_ref, send_ref, core, (z, pl.ds(0, 256), slice(None)), pair)
        dwo = dot_tn(gl_s[top, :], e_s[top, :])
        for z in range(4):
            for b in range(2):
                pair = [dwo[z * 128 + q * 64 : z * 128 + q * 64 + 64, b * LANES : (b + 1) * LANES] for q in range(2)]
                place(keep_ref, send_ref, core, (z, pl.ds(256 + b * 64, 64), slice(None)), pair)
        de_s[top, :] = dot_nt(du_s[top, :], pin[...])

        def last(i, at, carry):
            xhat, inv = normalise(x_s[at, :])
            da = de_s[at, :]
            out_ref[at, :] = g_ref[at, :] + norm_back(da, xhat, inv, gain)
            return carry + fold(da * xhat)

        small_ref[0:1, :] = total(blocks(rows, last, zero))

    by_rows(n_ref, run)


def conv_back(l, n, core, g, kb, small, xs, u, z, pin, pout):
    vm = pltpu.VMEM
    return call(
        functools.partial(conv_back_body, l),
        [SMEM, SMEM] + [VMEM] * 8 + [ANY] * 5,
        [
            (struct((CAP, D), F32), VMEM),
            (struct((4, 384, LANES), BF), VMEM),
            (struct((4, 384, LANES), BF), VMEM),
            (struct((24, D), F32), VMEM),
        ],
        [
            vm((CAP, D), F32), vm((CAP, 2 * D), BF), vm((CAP, D), F32), vm((D, 2 * D), BF), vm((D, D), BF),
            vm((CAP, D), BF), vm((CAP, D), BF), vm((CAP, D), BF), vm((CAP, D), F32), vm((CAP + 16, D), F32),
            vm((CAP + 16, D), F32), vm((CAP + 16, 128), F32), vm((CAP, 2 * D), BF), pltpu.SemaphoreType.DMA((5,)),
        ],
        (n, core, g, kb, *small, xs, u, z, pin, pout),
        flops=12 * 640 * D * D,
        moved=12 * 2**20,
        name=f"conv_back_{l}",
    )


def attend_back_body(
    l, n_ref, core_ref, g_ref, cos_ref, sin_ref, gains_ref,
    xs_h, q_h, kv_h, at_h, o_h, ain_h, aout_h,
    out_ref, keep_ref, send_ref, small_ref,
    x_s, q_s, kv_s, at_s, o_s, ain, aout, gl_s, a_s, do_s, dq_s, dkv_s, dp_s, da_s, sem,
):
    core = core_ref[0]
    gain = gains_ref[l, pl.ds(1, 1), :]

    def run(rows):
        tiles = rows // BLK
        top = pl.ds(0, rows)
        wide = pl.ds(0, rows + 2 * BLK)
        copies = [
            pltpu.make_async_copy(aout_h.at[l], aout, sem.at[0]),
            pltpu.make_async_copy(o_h.at[l, top], o_s.at[top], sem.at[1]),
            pltpu.make_async_copy(q_h.at[l, top], q_s.at[top], sem.at[2]),
            pltpu.make_async_copy(kv_h.at[l, wide], kv_s.at[wide], sem.at[3]),
            pltpu.make_async_copy(at_h.at[l, pl.ds(0, tiles)], at_s.at[pl.ds(0, tiles)], sem.at[4]),
            pltpu.make_async_copy(xs_h.at[l, 1, top], x_s.at[top], sem.at[5]),
            pltpu.make_async_copy(ain_h.at[l], ain, sem.at[6]),
        ]
        for c in copies:
            c.start()

        def low(i, at, carry):
            gl_s[at, :] = g_ref[at, :].astype(BF)
            return carry

        blocks(rows, low)

        def clear(i, at, carry):
            dkv_s[at, :] = jnp.zeros((BLK, 2 * D), F32)
            return carry

        blocks(rows + 2 * BLK, clear)
        copies[0].wait()
        do_s[top, :] = dot_nt(gl_s[top, :], aout[...]).astype(BF)
        for c in copies[1:]:
            c.wait()

        def tile(t, at, carry):
            near = pl.ds(pl.multiple_of(t * BLK, BLK), 3 * BLK)
            for p in range(PAIRS):
                lanes = slice(p * 128, (p + 1) * 128)
                vlanes = slice(D + p * 128, D + (p + 1) * 128)
                do = stacked(do_s[at, lanes])
                o = o_s[at, lanes].astype(F32)
                delta = jnp.sum(do.astype(F32) * jnp.concatenate([o, o], axis=0), axis=-1, keepdims=True)
                weights = at_s[t, p]
                da = dot_nt(do, kv_s[near, vlanes])
                ds = (weights.astype(F32) * (da - delta)).astype(BF)
                dq_s[at, lanes] = unstacked(dot_nn(ds, kv_s[near, lanes])) * HD**-0.5
                dkv_s[near, lanes] = dkv_s[near, lanes] + dot_tn(ds, stacked(q_s[at, lanes]))
                dkv_s[near, vlanes] = dkv_s[near, vlanes] + dot_tn(weights, do)
            return carry

        blocks(rows, tile)

        def turn(i, at, carry):
            inner = pl.ds(pl.multiple_of(i * BLK + BLK, BLK), BLK)
            cos, sin = cos_ref[at, :], sin_ref[at, :]
            for p in range(PAIRS):
                lanes = slice(p * 128, (p + 1) * 128)
                dq = dq_s[at, lanes]
                dk = dkv_s[inner, lanes]
                dp_s[at, lanes] = (dq * cos - swap_halves(dq) * sin).astype(BF)
                dp_s[at, D + p * 128 : D + (p + 1) * 128] = (dk * cos - swap_halves(dk) * sin).astype(BF)
                dp_s[at, 2 * D + p * 128 : 2 * D + (p + 1) * 128] = dkv_s[
                    inner, D + p * 128 : D + (p + 1) * 128
                ].astype(BF)
            xhat, _ = normalise(x_s[at, :])
            a_s[at, :] = (xhat * gain).astype(BF)
            return carry

        blocks(rows, turn)

        for z in range(4):
            dwi = dot_tn(dp_s[top, z * 384 : (z + 1) * 384], a_s[top, :])
            for b in range(2):
                pair = [dwi[q * 192 : (q + 1) * 192, b * LANES : (b + 1) * LANES] for q in range(2)]
                place(keep_ref, send_ref, core, (z, pl.ds(b * 192, 192), slice(None)), pair)
        dwo = dot_tn(gl_s[top, :], o_s[top, :])
        for z in range(4):
            for b in range(2):
                pair = [dwo[z * 128 + q * 64 : z * 128 + q * 64 + 64, b * LANES : (b + 1) * LANES] for q in range(2)]
                place(keep_ref, send_ref, core, (z, pl.ds(384 + b * 64, 64), slice(None)), pair)
        da_s[top, :] = dot_nt(dp_s[top, :], ain[...])

        def last(i, at, carry):
            xhat, inv = normalise(x_s[at, :])
            da = da_s[at, :]
            out_ref[at, :] = g_ref[at, :] + norm_back(da, xhat, inv, gain)
            return carry + fold(da * xhat)

        small_ref[0:1, :] = total(blocks(rows, last, jnp.zeros((8, D), F32)))

    by_rows(n_ref, run)


def attend_back(l, n, core, g, cos, sin, gains, xs, q, kv, at, o, ain, aout):
    vm = pltpu.VMEM
    return call(
        functools.partial(attend_back_body, l),
        [SMEM, SMEM] + [VMEM] * 4 + [ANY] * 7,
        [
            (struct((CAP, D), F32), VMEM),
            (struct((4, 512, LANES), BF), VMEM),
            (struct((4, 512, LANES), BF), VMEM),
            (struct((8, D), F32), VMEM),
        ],
        [
            vm((CAP, D), F32), vm((CAP, D), BF), vm((CAP + 2 * BLK, 2 * D), BF),
            vm((CAP // BLK, PAIRS, 2 * BLK, 3 * BLK), BF), vm((CAP, D), BF), vm((D, 3 * D), BF), vm((D, D), BF),
            vm((CAP, D), BF), vm((CAP, D), BF), vm((CAP, D), BF), vm((CAP, D), F32),
            vm((CAP + 2 * BLK, 2 * D), F32), vm((CAP, 3 * D), BF), vm((CAP, D), F32), pltpu.SemaphoreType.DMA((7,)),
        ],
        (n, core, g, cos, sin, gains, xs, q, kv, at, o, ain, aout),
        flops=16 * 640 * D * D,
        moved=20 * 2**20,
        name=f"attend_back_{l}",
    )


def add(*terms):
    acc = terms[0].astype(F32)
    for term in terms[1:]:
        acc = acc + term.astype(F32)
    return acc.astype(BF)


def split_xy_body(sizes, place_ref, *refs):
    count = len(sizes)
    keeps, gots = refs[:count], refs[count : 2 * count]
    a_keep, a_send, b_keep, b_send = refs[2 * count :]
    x, y = place_ref[0], place_ref[1]
    off = 0
    for keep, got, n in zip(keeps, gots, sizes):
        at = pl.ds(off, n)

        def one(z, carry, keep=keep, got=got, at=at):
            for j in range(2):
                a_keep[z, j, at] = add(keep[z, 0, j, x], got[z, 0, j, x])
                a_send[z, j, at] = add(keep[z, 0, j, 1 - x], got[z, 0, j, 1 - x])
                b_keep[z, j, at] = add(keep[z, 1, y, j], got[z, 1, y, j])
                b_send[z, j, at] = add(keep[z, 1, 1 - y, j], got[z, 1, 1 - y, j])
            return carry

        lax.fori_loop(0, 4, one, jnp.int32(0))
        off += n


def split_yx_body(place_ref, a_keep, a_got, b_keep, b_got, a2_keep, a2_send, b2_keep, b2_send):
    x, y = place_ref[0], place_ref[1]

    def one(z, carry):
        a2_keep[z] = add(a_keep[z, y], a_got[z, y])
        a2_send[z] = add(a_keep[z, 1 - y], a_got[z, 1 - y])
        b2_keep[z] = add(b_keep[z, x], b_got[z, x])
        b2_send[z] = add(b_keep[z, 1 - x], b_got[z, 1 - x])
        return carry

    lax.fori_loop(0, 4, one, jnp.int32(0))


def split_z_body(place_ref, a_keep, a_got, b_keep, b_got, own, one, two, three):
    z = place_ref[2]
    for k, ref in enumerate((own, one, two, three)):
        at = lax.rem(z + k, 4)
        ref[0] = add(a_keep[at], a_got[at])
        ref[1] = add(b_keep[at], b_got[at])


def sum_four_body(a, b, c, d, out):
    out[...] = add(a[...], b[...], c[...], d[...])


def row_pairs(bit):
    return [(i, i ^ bit) for i in range(4)]


def summed_group(spot, keeps, sends):
    core_pairs = [(i, i ^ 1) for i in range(8)]
    gots = [lax.ppermute(s, "tm", core_pairs) for s in sends]
    sizes = [k.shape[1] // 8 for k in keeps]
    n = sum(sizes)
    shaped = lambda v: v.reshape(4, 2, 2, 2, v.shape[1] // 8, LANES)
    quarter = struct((4, 2, n, LANES), BF)
    moved = 6 * 4 * 2 * n * LANES * 2
    a_keep, a_send, b_keep, b_send = call(
        functools.partial(split_xy_body, sizes),
        [SMEM] + [VMEM] * (2 * len(sizes)),
        [(quarter, VMEM)] * 4,
        [],
        (spot, *map(shaped, keeps), *map(shaped, gots)),
        moved=2 * moved,
        name="split_xy",
    )
    a_got = lax.ppermute(a_send, "rows", row_pairs(1))
    b_got = lax.ppermute(b_send, "rows", row_pairs(2))
    eighth = struct((4, n, LANES), BF)
    a_keep, a_send, b_keep, b_send = call(
        split_yx_body,
        [SMEM] + [VMEM] * 4,
        [(eighth, VMEM)] * 4,
        [],
        (spot, a_keep, a_got, b_keep, b_got),
        moved=moved,
        name="split_yx",
    )
    a_got = lax.ppermute(a_send, "rows", row_pairs(2))
    b_got = lax.ppermute(b_send, "rows", row_pairs(1))
    piece = struct((2, n, LANES), BF)
    own, *others = call(
        split_z_body,
        [SMEM] + [VMEM] * 4,
        [(piece, VMEM)] * 4,
        [],
        (spot, a_keep, a_got, b_keep, b_got),
        moved=moved // 2,
        name="split_z",
    )
    gots = [
        lax.ppermute(v, "tm", [(i, (i + 2 * k) % 8) for i in range(8)]) for k, v in zip((1, 2, 3), others)
    ]
    mine = call(
        sum_four_body,
        [VMEM] * 4,
        [(piece, VMEM)],
        [],
        (own, *gots),
        moved=moved // 4,
        name="sum_four",
    )[0]
    others = [lax.ppermute(mine, "rows", row_pairs(bit)) for bit in (1, 2, 3)]
    me = 2 * spot[1] + spot[0]
    by_bit = jnp.stack([mine, *others])
    by_owner = jnp.stack([lax.dynamic_index_in_dim(by_bit, jnp.bitwise_xor(me, r), 0, False) for r in range(4)])
    whole = jnp.swapaxes(by_owner, 0, 1)
    out = []
    off = 0
    for size in sizes:
        out.append(whole[:, :, off : off + size].reshape(8 * size, LANES))
        off += size
    return out


def rows_of(chunk, blocks_of):
    r = chunk.shape[0] // blocks_of
    return jnp.swapaxes(chunk.reshape(blocks_of, r, LANES), 0, 1).reshape(r, blocks_of * LANES)


def feed_parts(chunk):
    return chunk[:D], rows_of(chunk[D:], FF // LANES).T


def conv_parts(chunk):
    point_in = jnp.concatenate([chunk[:256, :128], chunk[:256, 128:]], axis=0)
    return point_in, rows_of(chunk[256:], 2).T


def attend_parts(chunk):
    return rows_of(chunk[:384], 2).T, rows_of(chunk[384:], 2).T


def per_device(
    frames, segment_ids, norm_gains, feed_in, feed_out, attend_in, attend_out, point_in, depthwise, stat_mean,
    stat_var, batch_scale, batch_shift, point_out, cotangent,
):
    batches, row_count, frame_count, model_dim = frames.shape
    layers = norm_gains.shape[0]
    tm_size = lax.axis_size("tm")
    rows_size = lax.axis_size("rows")
    tm = lax.axis_index("tm")
    row = lax.axis_index("rows")
    fast = tm_size == 8 and rows_size == 4
    half = batches // 2

    ids = segment_ids[:, 0] + 1
    below = shifted(ids, "tm", 1)
    above = shifted(ids, "tm", -1)

    def windows(own):
        pairs = own.reshape((half, 2) + own.shape[1:])
        from_above = shifted(pairs[:, 0], "tm", -1)
        from_below = shifted(pairs[:, 1], "tm", 1)
        even = jnp.concatenate([pairs[:, 0], from_above], axis=1)
        odd = jnp.concatenate([from_below, pairs[:, 1]], axis=1)
        return jnp.stack([even, odd], axis=1).reshape((batches * 2 * frame_count,) + own.shape[2:])

    pair_ids = ids.reshape(half, 2, frame_count)
    pair_below = below.reshape(half, 2, frame_count)
    pair_above = above.reshape(half, 2, frame_count)
    even_keep = jnp.concatenate(
        [pair_ids[:, 0] != pair_below[:, 0, -1:], pair_above[:, 0] == pair_ids[:, 0, -1:]], axis=1
    )
    odd_keep = jnp.concatenate(
        [pair_below[:, 1] == pair_ids[:, 1, :1], pair_ids[:, 1] != pair_above[:, 1, :1]], axis=1
    )
    even_ids = jnp.concatenate([pair_ids[:, 0], pair_above[:, 0]], axis=1)
    odd_ids = jnp.concatenate([pair_below[:, 1], pair_ids[:, 1]], axis=1)
    keep = jnp.stack([even_keep, odd_keep], axis=1).reshape(-1)
    win_ids = jnp.stack([even_ids, odd_ids], axis=1).reshape(batches, 2 * frame_count)
    key = (win_ids + 4096 * jnp.arange(batches, dtype=jnp.int32)[:, None]).reshape(-1).astype(F32)
    n = jnp.sum(keep.astype(jnp.int32)).reshape(1)

    x0, chooser, cos, sin, kb, kr = pack(keep.astype(F32), key, windows(frames[:, 0]))
    small = (norm_gains, depthwise, stat_mean, stat_var, batch_scale, batch_shift)
    mats = (feed_in, feed_out, attend_in, attend_out, point_in, point_out)
    act, xs, hs, q, kv, at, o, u, z = forward(n, x0, cos, sin, kb, kr, small, mats)

    def unpacked(packed):
        spread = lax.dot_general(
            chooser, packed, (((0,), (0,)), ((), ())), preferred_element_type=F32
        ).astype(BF).reshape(half, 2, 2, frame_count, model_dim)
        from_below = shifted(spread[:, 0, 1], "tm", 1)
        from_above = shifted(spread[:, 1, 0], "tm", -1)
        even = spread[:, 0, 0] + from_below
        odd = spread[:, 1, 1] + from_above
        return jnp.stack([even, odd], axis=1).reshape(batches, 1, frame_count, model_dim)

    activations = unpacked(act)
    g = jnp.dot(chooser, windows(cotangent[:, 0]), preferred_element_type=F32)

    if fast:
        spot = jnp.stack([row % 2, row // 2, tm // 2]).astype(jnp.int32)
        core = (tm % 2).astype(jnp.int32).reshape(1)
    else:
        spot = None
        core = jnp.zeros((1,), jnp.int32)

    members = {}
    smalls = {}
    for l in reversed(range(layers)):
        g, keep_b, send_b, smalls[l, "f1"] = feed_back(l, 1, n, core, g, norm_gains, xs, hs, feed_in, feed_out)
        members[l, "f1"] = (keep_b, send_b)
        g, keep_b, send_b, smalls[l, "c"] = conv_back(l, n, core, g, kb, small, xs, u, z, point_in, point_out)
        members[l, "c"] = (keep_b, send_b)
        g, keep_b, send_b, smalls[l, "a"] = attend_back(
            l, n, core, g, cos, sin, norm_gains, xs, q, kv, at, o, attend_in, attend_out
        )
        members[l, "a"] = (keep_b, send_b)
        g, keep_b, send_b, smalls[l, "f0"] = feed_back(l, 0, n, core, g, norm_gains, xs, hs, feed_in, feed_out)
        members[l, "f0"] = (keep_b, send_b)
    frames_grad = unpacked(g.astype(BF))

    small_rows = []
    for l in range(layers):
        f0, a, c, f1 = (smalls[l, name] for name in ("f0", "a", "c", "f1"))
        small_rows += [f0[0:1], a[0:1], c[0:1], f1[0:1], f1[1:2], c[8 : 8 + KERNEL], c[1:3]]
    per_layer = 5 + KERNEL + 2
    small_all = jnp.concatenate(small_rows, axis=0)

    if fast:
        chunks = small_all.reshape(layers * per_layer, 4, 2, D // 8)
        chunks = jnp.moveaxis(chunks, 0, 2).reshape(4, 2, -1, LANES)
        chunks = jnp.pad(chunks, ((0, 0), (0, 0), (0, 128 - chunks.shape[2]), (0, 0))).astype(BF)
        members["small"] = (
            lax.dynamic_index_in_dim(chunks, core[0], 1, False),
            lax.dynamic_index_in_dim(chunks, 1 - core[0], 1, False),
        )
        groups = []
        for l in reversed(range(layers)):
            groups.append([(l, "f1"), (l, "c"), (l, "a")])
            groups.append([(l, "f0")] + (["small"] if l == 0 else []))
        done = {}
        for names in groups:
            parts = summed_group(spot, [members[m][0] for m in names], [members[m][1] for m in names])
            done.update(zip(names, parts))
        pick = lambda name, split: [split(done[l, name]) for l in range(layers)]
        f0, a, c, f1 = (
            pick("f0", feed_parts), pick("a", attend_parts), pick("c", conv_parts), pick("f1", feed_parts)
        )
        fin = jnp.stack([jnp.stack([f0[l][0], f1[l][0]]) for l in range(layers)])
        fout = jnp.stack([jnp.stack([f0[l][1], f1[l][1]]) for l in range(layers)])
        ain, aout = (jnp.stack([a[l][i] for l in range(layers)]) for i in range(2))
        pin, pout = (jnp.stack([c[l][i] for l in range(layers)]) for i in range(2))
        mats_out = [v.astype(F32) for v in (fin, fout, ain, aout, pin, pout)]
        lines = layers * per_layer * (D // 8) // LANES
        small_out = done["small"][:lines].reshape(layers, per_layer, D // 8).astype(F32)
    else:
        def natural(name, l):
            even, odd = members[l, name]
            return jnp.stack([even, odd], axis=1).astype(F32).reshape(8, -1, LANES)

        def wide(v, count):
            r = v.shape[1] // count
            return jnp.swapaxes(v.reshape(8, count, r, LANES), 1, 2).reshape(8 * r, count * LANES)

        def over_all(v, dim):
            v = lax.psum_scatter(v, "tm", scatter_dimension=dim, tiled=True)
            return lax.psum(v, "rows")

        fin, fout, ain, aout, pin, pout = [], [], [], [], [], []
        for l in range(layers):
            f = [natural("f0", l), natural("f1", l)]
            fin.append(jnp.stack([jnp.moveaxis(v[:, :D], 0, 1).reshape(D, FF) for v in f]))
            fout.append(jnp.stack([wide(v[:, D:], FF // LANES).T for v in f]))
            v = natural("a", l)
            ain.append(wide(v[:, :384], 2).T)
            aout.append(wide(v[:, 384:], 2).T)
            v = natural("c", l)
            top = jnp.concatenate([v[:, :256, :128], v[:, :256, 128:]], axis=1)
            pin.append(jnp.moveaxis(top, 0, 1).reshape(D, 2 * D))
            pout.append(wide(v[:, 256:], 2).T)
        mats_out = [over_all(jnp.stack(v), jnp.stack(v).ndim - 1) for v in (fin, fout, ain, aout, pin, pout)]
        small_out = over_all(small_all, 1).reshape(layers, per_layer, -1)

    fin, fout, ain, aout, pin, pout = mats_out
    return (
        activations,
        frames_grad,
        small_out[:, :5],
        fin,
        fout,
        ain,
        aout,
        pin,
        small_out[:, 5 : 5 + KERNEL],
        small_out[:, 5 + KERNEL],
        small_out[:, 6 + KERNEL],
        pout,
    )


def solution(mesh):
    rep = P()
    in_specs = (
        P(None, "rows", "tm", None), P(None, "rows", "tm"), rep, rep, rep, rep, rep, rep, rep, rep, rep, rep, rep, rep,
        P(None, "rows", "tm", None),
    )
    out_specs = (
        P(None, "rows", "tm", None), P(None, "rows", "tm", None), P(None, None, "tm"), P(None, None, None, "tm"),
        P(None, None, None, "tm"), P(None, None, "tm"), P(None, None, "tm"), P(None, None, "tm"),
        P(None, None, "tm"), P(None, "tm"), P(None, "tm"), P(None, None, "tm"),
    )
    return jax.shard_map(per_device, mesh=mesh, in_specs=in_specs, out_specs=out_specs, check_vma=False)
```

```python
import functools

import jax
import jax.numpy as jnp
import numpy as np
from jax import lax
from jax.experimental import pallas as pl
from jax.experimental.pallas import tpu as pltpu
from jax.sharding import PartitionSpec as P

HD = 64
KERNEL = 9
HALO = 4
EPSILON = 1e-05
MASKED = -1e30
BF = jnp.bfloat16
F32 = jnp.float32
D = 512
FF = 2048
BLK = 128
ROW_CHOICES = (640, 1024)
CAP = ROW_CHOICES[-1]
LANES = 256
SMALL_ROWS = 128
TAIL_WORK = 3e10
PAIRS = D // 128
VMEM_LIMIT = 60 * 2**20
ANY = pl.BlockSpec(memory_space=pl.ANY)
VMEM = pl.BlockSpec(memory_space=pltpu.VMEM)
SMEM = pl.BlockSpec(memory_space=pltpu.SMEM)


def shifted(array, axis, by):
    size = lax.axis_size(axis)
    pairs = [(i, i + by) for i in range(size) if 0 <= i + by < size]
    return lax.ppermute(array, axis, pairs)


def struct(shape, dtype):
    return jax.ShapeDtypeStruct(shape, dtype)


def call(body, ins, outs, scratch, args, flops=0, moved=0, name="kernel", deps=()):
    count = len(ins)

    def inner(*refs):
        body(*refs[:count], *refs[count + len(deps) :])

    return pl.pallas_call(
        inner,
        out_shape=[s for s, _ in outs],
        in_specs=list(ins) + [ANY] * len(deps),
        out_specs=[b for _, b in outs],
        scratch_shapes=scratch,
        compiler_params=pltpu.CompilerParams(vmem_limit_bytes=VMEM_LIMIT),
        cost_estimate=pl.CostEstimate(flops=int(flops), bytes_accessed=int(moved), transcendentals=0),
        name=name,
    )(*args, *deps)


def dot_nn(a, b):
    return jnp.dot(a, b, preferred_element_type=F32)


def dot_nt(a, b):
    return lax.dot_general(a, b, (((1,), (1,)), ((), ())), preferred_element_type=F32)


def dot_tn(a, b):
    return lax.dot_general(a, b, (((0,), (0,)), ((), ())), preferred_element_type=F32)


def sigmoid(v):
    return 0.5 + 0.5 * jnp.tanh(0.5 * v)


def normalise(x):
    c = x - jnp.mean(x, axis=-1, keepdims=True)
    inv = lax.rsqrt(jnp.mean(c * c, axis=-1, keepdims=True) + EPSILON)
    return c * inv, inv


def norm_back(grad, xhat, inv, gain):
    w = grad * gain
    return inv * (
        w - jnp.mean(w, axis=-1, keepdims=True) - xhat * jnp.mean(w * xhat, axis=-1, keepdims=True)
    )


def fold(v):
    return jnp.sum(v.reshape(v.shape[0] // 8, 8, v.shape[1]), axis=0)


def total(v):
    return jnp.sum(v, axis=0, keepdims=True)


def by_rows(n_ref, body):
    low = 0
    for rows in ROW_CHOICES:
        n = n_ref[0]
        cond = n > low
        if rows != CAP:
            cond = cond & (n <= rows)

        @pl.when(cond)
        def _(rows=rows):
            body(rows)

        low = rows


def blocks(rows, step, init=None, size=128):
    def wrapped(i, carry):
        at = pl.ds(pl.multiple_of(i * size, size), size)
        return step(i, at, carry)

    return lax.fori_loop(0, rows // size, wrapped, init if init is not None else jnp.int32(0))


def each(count, rows, step):
    if rows == ROW_CHOICES[0]:
        for i in range(count):
            step(i)
    else:

        def wrapped(i, carry):
            step(i)
            return carry

        lax.fori_loop(0, count, wrapped, jnp.int32(0))


def cut(i, size):
    return pl.ds(i * size, size) if isinstance(i, int) else pl.ds(pl.multiple_of(i * size, size), size)


def rope_tables():
    half = HD // 2
    freq = np.power(np.float32(10000.0), -(np.arange(half).astype(np.float32) / np.float32(half)))
    angle = np.arange(BLK).astype(np.float32)[:, None] * freq.astype(np.float32)[None, :]
    cos = np.cos(angle.astype(np.float64))
    sin = np.sin(angle.astype(np.float64))
    full = (np.concatenate([cos] * 4, axis=1), np.concatenate([-sin, sin] * 2, axis=1))
    parts = []
    for table in full:
        rest = table
        for _ in range(3):
            piece = rest.astype(jnp.bfloat16)
            parts.append(piece)
            rest = rest - piece.astype(np.float64)
    return np.stack(parts)


def pack_body(
    ids_ref, frames_ref, cot_ref, below_ref, above_ref, tab_ref,
    x_ref, g_ref, p_ref, cos_ref, sin_ref, kb_ref, kr_ref, n_ref,
    keep_s, key_s, dest_s, pos_s, win_s, cot_s,
):
    batches = ids_ref.shape[0]
    half = batches // 2
    shown = (8, BLK)
    below_ids = below_ref[pl.ds(4 * BLK, 16), :].astype(F32)[0:1]
    above_ids = above_ref[pl.ds(4 * BLK, 16), :].astype(F32)[0:1]
    for m in range(batches):
        own = ids_ref[m : m + 1, :]
        below = below_ids[:, m * BLK : (m + 1) * BLK]
        above = above_ids[:, m * BLK : (m + 1) * BLK]
        i = m // 2
        mine = pl.ds(m * BLK, BLK)
        theirs = (pl.ds(i * BLK, BLK), pl.ds((half + i) * BLK, BLK))
        if m % 2 == 0:
            pieces = ((own, own != below[:, BLK - 1 : BLK]), (above, above == own[:, BLK - 1 : BLK]))
            frames = ((frames_ref, mine, cot_ref, mine), (above_ref, theirs[0], above_ref, theirs[1]))
        else:
            pieces = ((below, below == own[:, 0:1]), (own, own != above[:, 0:1]))
            frames = ((below_ref, theirs[0], below_ref, theirs[1]), (frames_ref, mine, cot_ref, mine))
        for j in range(2):
            at = pl.ds((2 * m + j) * BLK, BLK)
            key_s[:, at] = jnp.broadcast_to(pieces[j][0] + 4096.0 * m, shown)
            keep_s[:, at] = jnp.broadcast_to(jnp.where(pieces[j][1], 1.0, 0.0), shown)
            src, rows, cot, cot_rows = frames[j]
            win_s[at, :] = src[rows, :]
            cot_s[at, :] = cot[cot_rows, :]
    square = (BLK, BLK)
    earlier = lax.broadcasted_iota(jnp.int32, square, 0) < lax.broadcasted_iota(jnp.int32, square, 1)
    ramp = earlier.astype(F32).astype(BF)
    before = jnp.zeros((8, 1), F32)
    for j in range(2 * batches):
        at = pl.ds(j * BLK, BLK)
        keep = keep_s[:, at]
        dest_s[:, at] = jnp.where(keep > 0.5, before + dot_nn(keep.astype(BF), ramp), -1.0)
        before = before + jnp.sum(keep, axis=1, keepdims=True)
    n_ref[0] = (jnp.sum(before) * 0.125 + 0.5).astype(jnp.int32)
    for m in range(batches):
        first, second = pl.ds(2 * m * BLK, BLK), pl.ds((2 * m + 1) * BLK, BLK)
        cols = [jnp.broadcast_to(key_s[0:1, at], square).T for at in (first, second)]
        count = lambda mask: jnp.broadcast_to(jnp.sum(jnp.where(mask, 1.0, 0.0), axis=0, keepdims=True), shown)
        pos_s[:, first] = count((cols[0] == key_s[0:1, first]) & earlier)
        pos_s[:, second] = count(cols[0] == key_s[0:1, second]) + count((cols[1] == key_s[0:1, second]) & earlier)
    kr_ref[...] = jnp.full(kr_ref.shape, -1.0, F32)
    rows_all = 2 * batches * BLK

    def step(i, at, carry):
        row = (lax.broadcasted_iota(jnp.int32, (BLK, rows_all), 0) + i * BLK).astype(F32)
        pick = jnp.where(dest_s[0:1, :] == row, 1.0, 0.0)
        p = pick.astype(BF)
        p_ref[at, :] = p
        x_ref[at, :] = dot_nn(p, win_s[...])
        g_ref[at, :] = dot_nn(p, cot_s[...])
        key = jnp.broadcast_to(jnp.sum(pick * key_s[0:1, :], axis=1, keepdims=True), square)
        kb_ref[at, :] = key
        kr_ref[:, pl.ds(pl.multiple_of(i * BLK + BLK, BLK), BLK)] = key.T[0:8]
        pos = jnp.sum(pick * pos_s[0:1, :], axis=1, keepdims=True)
        hot = (lax.broadcasted_iota(jnp.int32, square, 1).astype(F32) == pos).astype(F32).astype(BF)
        cos_ref[at, :] = dot_nn(hot, tab_ref[0]) + dot_nn(hot, tab_ref[1]) + dot_nn(hot, tab_ref[2])
        sin_ref[at, :] = dot_nn(hot, tab_ref[3]) + dot_nn(hot, tab_ref[4]) + dot_nn(hot, tab_ref[5])
        return carry

    blocks(rows_all, step)


def pack(ids, frames, cotangent, below, above):
    vm = pltpu.VMEM
    return call(
        pack_body,
        [VMEM] * 6,
        [
            (struct((CAP, D), F32), VMEM),
            (struct((CAP, D), F32), VMEM),
            (struct((CAP, CAP), BF), VMEM),
            (struct((CAP, 128), F32), VMEM),
            (struct((CAP, 128), F32), VMEM),
            (struct((CAP, 128), F32), VMEM),
            (struct((8, CAP + 2 * BLK), F32), VMEM),
            (struct((1,), jnp.int32), SMEM),
        ],
        [vm((8, CAP), F32), vm((8, CAP), F32), vm((8, CAP), F32), vm((8, CAP), F32), vm((CAP, D), BF), vm((CAP, D), BF)],
        (ids, frames, cotangent, below, above, jnp.asarray(rope_tables(), dtype=BF)),
        flops=4 * CAP * CAP * D,
        moved=12 * 2**20,
        name="pack",
    )


def lane_low(shape):
    return lax.broadcasted_iota(jnp.int32, shape, 1) % HD < HD // 2


def swap_halves(v):
    return jnp.where(lane_low(v.shape), pltpu.roll(v, 128 - HD // 2, 1), pltpu.roll(v, HD // 2, 1))


def stacked(v):
    first = lax.broadcasted_iota(jnp.int32, v.shape, 1) < HD
    zero = jnp.zeros_like(v)
    return jnp.concatenate([jnp.where(first, v, zero), jnp.where(first, zero, v)], axis=0)


def unstacked(v):
    half = v.shape[0] // 2
    first = lax.broadcasted_iota(jnp.int32, (half, 128), 1) < HD
    return jnp.where(first, v[:half], v[half:])


def norm_into(x_ref, gain, a_ref, rows):
    def step(i, at, carry):
        xhat, _ = normalise(x_ref[at, :])
        a_ref[at, :] = (xhat * gain).astype(BF)
        return carry

    blocks(rows, step)


def forward_body(
    n_ref, x0_ref, cos_ref, sin_ref, kb_ref, kr_ref, gains_ref, taps_ref, mean_ref, var_ref, scale_ref, shift_ref,
    fin_h, fout_h, ain_h, aout_h, pin_h, pout_h,
    act_ref, xs_h, hs_h, q_h, kv_h, at_h, o_h, u_h, z_h,
    fin, fout, ain, aout, pin, pout, xb, hb, qb, kvb, ab, ob, ub, zb, a_s, gp, kp, w_sem, s_sem,
):
    layers = gains_ref.shape[0]
    weights = [
        (fin_h, (0,), fin.at[0]), (fout_h, (0,), fout.at[0]), (ain_h, (), ain), (aout_h, (), aout),
        (pin_h, (), pin), (pout_h, (), pout), (fin_h, (1,), fin.at[1]), (fout_h, (1,), fout.at[1]),
    ]

    def weight_copy(i, l):
        src, sub, dst = weights[i]
        return pltpu.make_async_copy(src.at[(l,) + sub], dst, w_sem.at[i])

    for i in range(len(weights)):
        weight_copy(i, 0).start()

    def run(rows):
        tiles = rows // BLK
        top = pl.ds(0, rows)
        saves = [(xb.at[i, top], lambda l, i=i: xs_h.at[l, i, top]) for i in range(5)]
        saves += [(hb.at[k, top], lambda l, k=k: hs_h.at[l, k, top]) for k in range(2)]
        saves += [
            (qb.at[top], lambda l: q_h.at[l, top]),
            (kvb.at[pl.ds(0, rows + 2 * BLK)], lambda l: kv_h.at[l, pl.ds(0, rows + 2 * BLK)]),
            (ab.at[pl.ds(0, tiles)], lambda l: at_h.at[l, pl.ds(0, tiles)]),
            (ob.at[top], lambda l: o_h.at[l, top]),
            (ub.at[top], lambda l: u_h.at[l, top]),
            (zb.at[top], lambda l: z_h.at[l, top]),
        ]

        def save(i, l):
            src, dst = saves[i]
            return pltpu.make_async_copy(src, dst(l), s_sem.at[i])

        def settle(i, l):
            @pl.when(l > 0)
            def _():
                save(i, l - 1).wait()

        def use(i, l):
            weight_copy(i, l).wait()

        def next_weight(i, l):
            @pl.when(l + 1 < layers)
            def _():
                weight_copy(i, l + 1).start()

        kvb[pl.ds(0, BLK), :] = jnp.zeros((BLK, 2 * D), BF)
        kvb[pl.ds(rows + BLK, BLK), :] = jnp.zeros((BLK, 2 * D), BF)
        gp[:, pl.ds(0, 8), :] = jnp.zeros((PAIRS, 8, 128), F32)
        gp[:, pl.ds(rows + 8, 8), :] = jnp.zeros((PAIRS, 8, 128), F32)
        kp[pl.ds(0, 8), :] = jnp.full((8, 128), -1.0, F32)
        kp[pl.ds(rows + 8, 8), :] = jnp.full((8, 128), -1.0, F32)

        def fill(i, at, carry):
            kp[pl.ds(pl.multiple_of(i * BLK + 8, 8), BLK), :] = kb_ref[at, :]
            xb[0, at, :] = x0_ref[at, :]
            return carry

        blocks(rows, fill)

        def feed(l, k, src, dst, gain, wi):
            settle(5 + k, l)
            settle(dst, l)

            def first(i, at, carry):
                x = xb[src, at, :]
                xhat, _ = normalise(x)
                a_s[at, :] = (xhat * gain).astype(BF)
                xb[dst, at, :] = x
                return carry

            blocks(rows, first)
            use(wi, l)
            use(wi + 1, l)

            def chunk(c):
                cols = cut(c, 512)
                h = dot_nn(a_s[top, :], fin[k, :, cols])
                hb[k, top, cols] = h.astype(BF)
                s = (h * sigmoid(h)).astype(BF)
                xb[dst, top, :] = xb[dst, top, :] + 0.5 * dot_nn(s, fout[k, cols, :])

            each(FF // 512, rows, chunk)
            next_weight(wi, l)
            next_weight(wi + 1, l)
            save(5 + k, l).start()
            save(dst, l).start()

        def layer(l, carry):
            gains = [gains_ref[l, pl.ds(i, 1), :] for i in range(5)]
            save(0, l).start()
            feed(l, 0, 0, 1, gains[0], 0)

            norm_into(xb.at[1], gains[1], a_s, rows)
            settle(7, l)
            settle(8, l)
            settle(9, l)
            settle(10, l)
            use(2, l)
            for part in range(3):
                proj = dot_nn(a_s[top, :], ain[:, part * D : (part + 1) * D])
                for p in range(PAIRS):
                    lanes = slice(p * 128, (p + 1) * 128)
                    v = proj[:, lanes]
                    if part < 2:
                        v = v * cos_ref[top, :] + swap_halves(v) * sin_ref[top, :]
                    if part == 0:
                        qb[top, lanes] = (v * HD**-0.5).astype(BF)
                    elif part == 1:
                        kvb[pl.ds(BLK, rows), lanes] = v.astype(BF)
                    else:
                        kvb[pl.ds(BLK, rows), D + p * 128 : D + (p + 1) * 128] = v.astype(BF)
            next_weight(2, l)

            def tile(t, at, c):
                near = pl.ds(pl.multiple_of(t * BLK, BLK), 3 * BLK)
                same = kb_ref[at, 0:1] == kr_ref[0:1, near]
                same = jnp.concatenate([same, same], axis=0)
                for p in range(PAIRS):
                    lanes = slice(p * 128, (p + 1) * 128)
                    s = dot_nt(stacked(qb[at, lanes]), kvb[near, lanes])
                    s = jnp.where(same, s, MASKED)
                    e = jnp.exp(s - jnp.max(s, axis=-1, keepdims=True))
                    low = (e * (1.0 / jnp.sum(e, axis=-1, keepdims=True))).astype(BF)
                    ab[t, p] = low
                    o = dot_nn(low, kvb[near, D + p * 128 : D + (p + 1) * 128])
                    ob[at, lanes] = unstacked(o).astype(BF)
                return c

            blocks(rows, tile)
            settle(2, l)
            use(3, l)
            xb[2, top, :] = xb[1, top, :] + dot_nn(ob[top, :], aout[...])
            next_weight(3, l)
            for i in (7, 8, 9, 10, 2):
                save(i, l).start()

            norm_into(xb.at[2], gains[2], a_s, rows)
            settle(11, l)
            settle(12, l)
            use(4, l)
            for half in range(2):
                lanes = slice(half * 256, (half + 1) * 256)
                up1 = dot_nn(a_s[top, :], pin[:, half * 256 : (half + 1) * 256])
                up2 = dot_nn(a_s[top, :], pin[:, D + half * 256 : D + (half + 1) * 256])
                ub[top, lanes] = up1.astype(BF)
                ub[top, D + half * 256 : D + (half + 1) * 256] = up2.astype(BF)
                gated = (up1 * sigmoid(up2)).astype(BF).astype(F32)
                for q in range(2):
                    gp[2 * half + q, pl.ds(8, rows), :] = gated[:, q * 128 : (q + 1) * 128]
            next_weight(4, l)
            rs = lax.rsqrt(var_ref[pl.ds(l, 1), :] + EPSILON)
            mean = mean_ref[pl.ds(l, 1), :]
            scale = scale_ref[pl.ds(l, 1), :]
            shift = shift_ref[pl.ds(l, 1), :]

            def conv(t, at, c):
                near = [pl.ds(t * BLK + 4 + o, BLK) for o in range(KERNEL)]
                own = kb_ref[at, :]
                masks = [kp[near[o], :] == own for o in range(KERNEL)]
                for p in range(PAIRS):
                    lanes = slice(p * 128, (p + 1) * 128)
                    z = jnp.zeros((BLK, 128), F32)
                    for o in range(KERNEL):
                        w = taps_ref[l, o : o + 1, lanes]
                        z = z + jnp.where(masks[o], w * gp[p, near[o], :], 0.0)
                    zb[at, lanes] = z
                    b = (z - mean[:, lanes]) * rs[:, lanes] * scale[:, lanes] + shift[:, lanes]
                    a_s[at, lanes] = (b * sigmoid(b)).astype(BF)
                return c

            blocks(rows, conv)
            settle(3, l)
            use(5, l)
            xb[3, top, :] = xb[2, top, :] + dot_nn(a_s[top, :], pout[...])
            next_weight(5, l)
            for i in (11, 12, 3):
                save(i, l).start()

            feed(l, 1, 3, 4, gains[3], 6)
            save(0, l).wait()

            def last(i, at, c):
                xhat, _ = normalise(xb[4, at, :])
                y = xhat * gains[4]
                xb[0, at, :] = y
                act_ref[at, :] = y.astype(BF)
                return c

            blocks(rows, last)
            return carry

        lax.fori_loop(0, layers, layer, jnp.int32(0))
        for i in range(1, len(saves)):
            save(i, layers - 1).wait()
        if rows < CAP:
            act_ref[pl.ds(rows, CAP - rows), :] = jnp.zeros((CAP - rows, D), BF)

    by_rows(n_ref, run)


def forward(n, x0, cos, sin, kb, kr, small, mats):
    layers = small[0].shape[0]
    outs = [
        (struct((CAP, D), BF), VMEM),
        (struct((layers, 5, CAP, D), F32), ANY),
        (struct((layers, 2, CAP, FF), BF), ANY),
        (struct((layers, CAP, D), BF), ANY),
        (struct((layers, CAP + 2 * BLK, 2 * D), BF), ANY),
        (struct((layers, CAP // BLK, PAIRS, 2 * BLK, 3 * BLK), BF), ANY),
        (struct((layers, CAP, D), BF), ANY),
        (struct((layers, CAP, 2 * D), BF), ANY),
        (struct((layers, CAP, D), F32), ANY),
    ]
    vm = pltpu.VMEM
    scratch = [
        vm((2, D, FF), BF), vm((2, FF, D), BF), vm((D, 3 * D), BF), vm((D, D), BF), vm((D, 2 * D), BF), vm((D, D), BF),
        vm((5, CAP, D), F32), vm((2, CAP, FF), BF), vm((CAP, D), BF), vm((CAP + 2 * BLK, 2 * D), BF),
        vm((CAP // BLK, PAIRS, 2 * BLK, 3 * BLK), BF), vm((CAP, D), BF), vm((CAP, 2 * D), BF), vm((CAP, D), F32),
        vm((CAP, D), BF), vm((PAIRS, CAP + 16, 128), F32), vm((CAP + 16, 128), F32),
        pltpu.SemaphoreType.DMA((8,)), pltpu.SemaphoreType.DMA((13,)),
    ]
    return call(
        forward_body,
        [SMEM] + [VMEM] * 11 + [ANY] * 6,
        outs,
        scratch,
        (n, x0, cos, sin, kb, kr, *small, *mats),
        flops=2 * 640 * 12e6,
        moved=60 * 2**20,
        name="forward",
    )


class Out:
    def __init__(self, core, buf, kept_h, sent_h, sem):
        self.core = core
        self.buf = buf
        self.homes = (kept_h, sent_h)
        self.sem = sem

    def put(self, at, pair):
        self.buf[(self.core,) + at] = pair[0].astype(BF)
        self.buf[(1 - self.core,) + at] = pair[1].astype(BF)

    def copies(self, slot, at):
        return [
            pltpu.make_async_copy(self.buf.at[(i,) + at], home.at[at], self.sem.at[2 * slot + i])
            for i, home in enumerate(self.homes)
        ]

    def send(self, slot, at):
        for c in self.copies(slot, at):
            c.start()

    def wait(self, slot, at):
        for c in self.copies(slot, at):
            c.wait()


def transposed_out(out, dwo, first):
    for z in range(4):
        for b in range(dwo.shape[1] // LANES):
            pair = [dwo[z * 128 + q * 64 : z * 128 + q * 64 + 64, b * LANES : (b + 1) * LANES] for q in range(2)]
            out.put((z, first(b), slice(None)), pair)


def feed_back_body(l, k, others, n_ref, core_ref, gains_ref, *refs):
    final = k == 1
    small_refs, (g_h, xs_h, hs_h, fin_h, fout_h, *rest) = refs[:others], refs[others:]
    out_h, keep_h, send_h, small_ref, g_s, x_s, x4_s, h_s, fin, fout, gl_s, a_s, da_s, buf, sem, osem = rest
    gain = gains_ref[l, pl.ds(3 if final else 0, 1), :]
    gain4 = gains_ref[l, pl.ds(4, 1), :]
    out = Out(core_ref[0], buf, keep_h, send_h, osem)
    every = pl.ds(0, 4)

    def run(rows):
        top = pl.ds(0, rows)
        g_in = pltpu.make_async_copy(g_h.at[top], g_s.at[top], sem.at[0])
        x_in = pltpu.make_async_copy(xs_h.at[l, 3 if final else 0, top], x_s.at[top], sem.at[1])
        x4_in = pltpu.make_async_copy(xs_h.at[l, 4, top], x4_s.at[top], sem.at[2])

        def chunk_in(c):
            cols = cut(c, 512)
            return [
                pltpu.make_async_copy(hs_h.at[l, k, top, cols], h_s.at[top, cols], sem.at[3 + 3 * c]),
                pltpu.make_async_copy(fout_h.at[l, k, cols], fout.at[cols], sem.at[4 + 3 * c]),
                pltpu.make_async_copy(fin_h.at[l, k, :, cols], fin.at[:, cols], sem.at[5 + 3 * c]),
            ]

        starts = [g_in, x4_in, x_in] if final else [g_in, x_in]
        for c in range(4):
            starts += chunk_in(c)
        for c in starts:
            c.start()
        g_in.wait()
        if final:
            x4_in.wait()
        x_in.wait()

        def first(i, at, carry):
            g = g_s[at, :]
            if final:
                xhat, inv = normalise(x4_s[at, :])
                carry = carry + fold(g * xhat)
                g = norm_back(g, xhat, inv, gain4)
                g_s[at, :] = g
            gl_s[at, :] = (0.5 * g).astype(BF)
            xhat, _ = normalise(x_s[at, :])
            a_s[at, :] = (xhat * gain).astype(BF)
            da_s[at, :] = jnp.zeros((BLK, D), F32)
            return carry

        gain4_grad = blocks(rows, first, jnp.zeros((8, D), F32))

        def low_rows(c):
            return pl.ds(D + c * 128, 128) if isinstance(c, int) else pl.ds(pl.multiple_of(D + c * 128, 128), 128)

        def spots(c):
            return (c, pl.ds(0, D)), (every, low_rows(c))

        def chunk(c):
            cols = cut(c, 512)
            for copy in chunk_in(c):
                copy.wait()
            h = h_s[top, cols].astype(F32)
            sig = sigmoid(h)
            s = (h * sig).astype(BF)
            ds = dot_nt(gl_s[top, :], fout[cols, :])
            dh = (ds * (sig * (1.0 + h * (1.0 - sig)))).astype(BF)
            dwi = dot_tn(a_s[top, :], dh)
            out.put((c, pl.ds(0, D), slice(None)), (dwi[:, :LANES], dwi[:, LANES:]))
            dwo = dot_tn(gl_s[top, :], s)
            step = lambda b: (D + (2 * c + b) * 64)
            transposed_out(
                out, dwo,
                lambda b: pl.ds(step(b), 64) if isinstance(c, int) else pl.ds(pl.multiple_of(step(b), 64), 64),
            )
            for i, at in enumerate(spots(c)):
                out.send(2 * c + i, at)
            da_s[top, :] = da_s[top, :] + dot_nt(dh, fin[:, cols])

        each(FF // 512, rows, chunk)

        def last(i, at, carry):
            xhat, inv = normalise(x_s[at, :])
            da = da_s[at, :]
            g_s[at, :] = g_s[at, :] + norm_back(da, xhat, inv, gain)
            return carry + fold(da * xhat)

        gain_grad = blocks(rows, last, jnp.zeros((8, D), F32))
        g_out = pltpu.make_async_copy(g_s.at[top], out_h.at[top], sem.at[0])
        g_out.start()
        small_ref[0:1, :] = total(gain_grad)
        small_ref[1:2, :] = total(gain4_grad)
        if others:
            low_spot = (every, pl.ds(1024, SMALL_ROWS))
            buf[:, :, pl.ds(1024, SMALL_ROWS), :] = jnp.zeros((2, 4, SMALL_ROWS, LANES), BF)
            rows_all = jnp.concatenate([small_ref[...]] + [ref[...] for ref in small_refs], axis=0)
            lines = SMALL_ROWS // 4
            rows_all = jnp.concatenate([rows_all, jnp.zeros((4 * lines - rows_all.shape[0], D), F32)], axis=0)
            for z in range(4):
                pair = []
                for q in range(2):
                    own = rows_all[:, z * 128 + q * 64 : z * 128 + q * 64 + 64]
                    pair.append(jnp.concatenate([own[i * lines : (i + 1) * lines] for i in range(4)], axis=1))
                out.put((z, pl.ds(1024, lines), slice(None)), pair)
            out.send(8, low_spot)
            out.wait(8, low_spot)
        for c in range(4):
            for i, at in enumerate(spots(c)):
                out.wait(2 * c + i, at)
        g_out.wait()

    by_rows(n_ref, run)


def feed_back(l, k, n, core, g, gains, xs, hs, fin, fout, deps=(), smalls=()):
    vm = pltpu.VMEM
    lines = 1024 + (SMALL_ROWS if smalls else 0)
    return call(
        functools.partial(feed_back_body, l, k, len(smalls)),
        [SMEM, SMEM, VMEM] + [VMEM] * len(smalls) + [ANY] * 5,
        [
            (struct((CAP, D), F32), ANY),
            (struct((4, lines, LANES), BF), ANY),
            (struct((4, lines, LANES), BF), ANY),
            (struct((8, D), F32), VMEM),
        ],
        [
            vm((CAP, D), F32), vm((CAP, D), F32), vm((CAP, D), F32), vm((CAP, FF), BF), vm((D, FF), BF),
            vm((FF, D), BF), vm((CAP, D), BF), vm((CAP, D), BF), vm((CAP, D), F32),
            vm((2, 4, lines, LANES), BF),
            pltpu.SemaphoreType.DMA((15,)), pltpu.SemaphoreType.DMA((18,)),
        ],
        (n, core, gains, *smalls, g, xs, hs, fin, fout),
        flops=8 * 640 * D * FF,
        moved=16 * 2**20,
        name=f"feed_back_{l}_{k}",
        deps=deps,
    )


def conv_back_body(
    l, n_ref, core_ref, kb_ref, gains_ref, taps_ref, mean_ref, var_ref, scale_ref, shift_ref,
    g_h, xs_h, u_h, z_h, pin_h, pout_h,
    out_h, keep_h, send_h, small_ref,
    g_s, x_s, u_s, z_s, pin, pout, gl_s, a_s, e_s, de_s, gp, dzp, kp, du_s, buf, sem, osem,
):
    gain = gains_ref[l, pl.ds(2, 1), :]
    rs = lax.rsqrt(var_ref[pl.ds(l, 1), :] + EPSILON)
    mean = mean_ref[pl.ds(l, 1), :]
    scale = scale_ref[pl.ds(l, 1), :]
    shift = shift_ref[pl.ds(l, 1), :]
    out = Out(core_ref[0], buf, keep_h, send_h, osem)
    every = pl.ds(0, 4)

    def run(rows):
        top = pl.ds(0, rows)
        copies = [
            pltpu.make_async_copy(g_h.at[top], g_s.at[top], sem.at[0]),
            pltpu.make_async_copy(pout_h.at[l], pout, sem.at[1]),
            pltpu.make_async_copy(z_h.at[l, top], z_s.at[top], sem.at[2]),
            pltpu.make_async_copy(u_h.at[l, top], u_s.at[top], sem.at[3]),
            pltpu.make_async_copy(xs_h.at[l, 2, top], x_s.at[top], sem.at[4]),
            pltpu.make_async_copy(pin_h.at[l], pin, sem.at[5]),
        ]
        for c in copies:
            c.start()
        for ref in (gp, dzp):
            ref[:, pl.ds(0, 8), :] = jnp.zeros((PAIRS, 8, 128), F32)
            ref[:, pl.ds(rows + 8, 8), :] = jnp.zeros((PAIRS, 8, 128), F32)
        kp[pl.ds(0, 8), :] = jnp.full((8, 128), -1.0, F32)
        kp[pl.ds(rows + 8, 8), :] = jnp.full((8, 128), -1.0, F32)
        copies[0].wait()

        def low(i, at, carry):
            gl_s[at, :] = g_s[at, :].astype(BF)
            kp[pl.ds(pl.multiple_of(i * BLK + 8, 8), BLK), :] = kb_ref[at, :]
            return carry

        blocks(rows, low)
        for c in copies[1:4]:
            c.wait()
        de_s[top, :] = dot_nt(gl_s[top, :], pout[...])
        copies[4].wait()

        def first(i, at, carry):
            scale_grad, shift_grad = carry
            inner = pl.ds(pl.multiple_of(i * BLK + 8, 8), BLK)
            hat = (z_s[at, :] - mean) * rs
            b = hat * scale + shift
            sig = sigmoid(b)
            e_s[at, :] = (b * sig).astype(BF)
            db = de_s[at, :] * (sig * (1.0 + b * (1.0 - sig)))
            dz = (db * scale * rs).astype(BF).astype(F32)
            u1 = u_s[at, pl.ds(0, D)].astype(F32)
            u2 = u_s[at, pl.ds(D, D)].astype(F32)
            gated = (u1 * sigmoid(u2)).astype(BF).astype(F32)
            for p in range(PAIRS):
                dzp[p, inner, :] = dz[:, p * 128 : (p + 1) * 128]
                gp[p, inner, :] = gated[:, p * 128 : (p + 1) * 128]
            xhat, _ = normalise(x_s[at, :])
            a_s[at, :] = (xhat * gain).astype(BF)
            return (scale_grad + fold(db * hat), shift_grad + fold(db))

        zero = jnp.zeros((8, D), F32)
        scale_grad, shift_grad = blocks(rows, first, (zero, zero))
        small_ref[...] = jnp.zeros(small_ref.shape, F32)
        small_ref[1:2, :] = total(scale_grad)
        small_ref[2:3, :] = total(shift_grad)
        dwo = dot_tn(gl_s[top, :], e_s[top, :])
        transposed_out(out, dwo, lambda b: pl.ds(256 + b * 64, 64))
        low_spot = (every, pl.ds(256, 128))
        out.send(0, low_spot)

        for p in range(PAIRS):
            lanes = slice(p * 128, (p + 1) * 128)

            def taps(t, at, carry, lanes=lanes, p=p):
                own = kb_ref[at, :]
                dz_own = dzp[p, pl.ds(pl.multiple_of(t * BLK + 8, 8), BLK), :]
                dg = jnp.zeros((BLK, 128), F32)
                sums = []
                for o in range(KERNEL):
                    near = pl.ds(t * BLK + 4 + o, BLK)
                    mask = kp[near, :] == own
                    sums.append(carry[o] + fold(jnp.where(mask, dz_own * gp[p, near, :], 0.0)))
                    w = taps_ref[l, KERNEL - 1 - o : KERNEL - o, lanes]
                    dg = dg + jnp.where(mask, w * dzp[p, near, :], 0.0)
                u1 = u_s[at, lanes].astype(F32)
                sig = sigmoid(u_s[at, D + p * 128 : D + (p + 1) * 128].astype(F32))
                du_s[at, lanes] = (dg * sig).astype(BF)
                du_s[at, D + p * 128 : D + (p + 1) * 128] = (dg * u1 * sig * (1.0 - sig)).astype(BF)
                return tuple(sums)

            sums = blocks(rows, taps, tuple(jnp.zeros((8, 128), F32) for _ in range(KERNEL)))
            for o in range(KERNEL):
                small_ref[8 + o : 9 + o, lanes] = total(sums[o])

        for half in range(2):
            dwi = dot_tn(a_s[top, :], du_s[top, half * 512 : (half + 1) * 512])
            for q in range(2):
                pair = [
                    jnp.concatenate([dwi[: D // 2, at : at + 128], dwi[D // 2 :, at : at + 128]], axis=1)
                    for at in (q * 256, q * 256 + 128)
                ]
                out.put((2 * half + q, pl.ds(0, 256), slice(None)), pair)
        high_spot = (every, pl.ds(0, 256))
        out.send(1, high_spot)
        copies[5].wait()
        de_s[top, :] = dot_nt(du_s[top, :], pin[...])

        def last(i, at, carry):
            xhat, inv = normalise(x_s[at, :])
            da = de_s[at, :]
            g_s[at, :] = g_s[at, :] + norm_back(da, xhat, inv, gain)
            return carry + fold(da * xhat)

        small_ref[0:1, :] = total(blocks(rows, last, zero))
        g_out = pltpu.make_async_copy(g_s.at[top], out_h.at[top], sem.at[0])
        g_out.start()
        out.wait(0, low_spot)
        out.wait(1, high_spot)
        g_out.wait()

    by_rows(n_ref, run)


def conv_back(l, n, core, g, kb, small, xs, u, z, pin, pout, deps=()):
    vm = pltpu.VMEM
    return call(
        functools.partial(conv_back_body, l),
        [SMEM, SMEM] + [VMEM] * 7 + [ANY] * 6,
        [
            (struct((CAP, D), F32), ANY),
            (struct((4, 384, LANES), BF), ANY),
            (struct((4, 384, LANES), BF), ANY),
            (struct((24, D), F32), VMEM),
        ],
        [
            vm((CAP, D), F32), vm((CAP, D), F32), vm((CAP, 2 * D), BF), vm((CAP, D), F32), vm((D, 2 * D), BF),
            vm((D, D), BF), vm((CAP, D), BF), vm((CAP, D), BF), vm((CAP, D), BF), vm((CAP, D), F32),
            vm((PAIRS, CAP + 16, 128), F32), vm((PAIRS, CAP + 16, 128), F32), vm((CAP + 16, 128), F32),
            vm((CAP, 2 * D), BF), vm((2, 4, 384, LANES), BF),
            pltpu.SemaphoreType.DMA((6,)), pltpu.SemaphoreType.DMA((4,)),
        ],
        (n, core, kb, *small, g, xs, u, z, pin, pout),
        flops=12 * 640 * D * D,
        moved=12 * 2**20,
        name=f"conv_back_{l}",
        deps=deps,
    )


def attend_back_body(
    l, n_ref, core_ref, cos_ref, sin_ref, gains_ref,
    g_h, xs_h, q_h, kv_h, at_h, o_h, ain_h, aout_h,
    out_h, keep_h, send_h, small_ref,
    g_s, x_s, q_s, kv_s, at_s, o_s, ain, aout, gl_s, a_s, do_s, dq_s, dkv_s, dp_s, da_s, buf, sem, osem,
):
    out = Out(core_ref[0], buf, keep_h, send_h, osem)
    every = pl.ds(0, 4)
    gain = gains_ref[l, pl.ds(1, 1), :]

    def run(rows):
        tiles = rows // BLK
        top = pl.ds(0, rows)
        wide = pl.ds(0, rows + 2 * BLK)
        copies = [
            pltpu.make_async_copy(aout_h.at[l], aout, sem.at[0]),
            pltpu.make_async_copy(o_h.at[l, top], o_s.at[top], sem.at[1]),
            pltpu.make_async_copy(q_h.at[l, top], q_s.at[top], sem.at[2]),
            pltpu.make_async_copy(kv_h.at[l, wide], kv_s.at[wide], sem.at[3]),
            pltpu.make_async_copy(xs_h.at[l, 1, top], x_s.at[top], sem.at[5]),
            pltpu.make_async_copy(ain_h.at[l], ain, sem.at[6]),
        ]
        copies = [pltpu.make_async_copy(g_h.at[top], g_s.at[top], sem.at[7])] + copies

        def weights_in(t):
            return pltpu.make_async_copy(at_h.at[l, t], at_s.at[t], sem.at[8 + t])

        for c in copies[:5]:
            c.start()
        for t in range(tiles):
            weights_in(t).start()
        for c in copies[5:]:
            c.start()
        copies[0].wait()

        def low(i, at, carry):
            gl_s[at, :] = g_s[at, :].astype(BF)
            return carry

        blocks(rows, low)

        def clear(i, at, carry):
            dkv_s[at, :] = jnp.zeros((BLK, 2 * D), F32)
            return carry

        blocks(rows + 2 * BLK, clear)
        copies[1].wait()
        do_s[top, :] = dot_nt(gl_s[top, :], aout[...]).astype(BF)
        for c in copies[2:5]:
            c.wait()

        def tile(t, at, carry):
            near = pl.ds(pl.multiple_of(t * BLK, BLK), 3 * BLK)
            weights_in(t).wait()
            for p in range(PAIRS):
                lanes = slice(p * 128, (p + 1) * 128)
                vlanes = slice(D + p * 128, D + (p + 1) * 128)
                do = stacked(do_s[at, lanes])
                o = o_s[at, lanes].astype(F32)
                delta = jnp.sum(do.astype(F32) * jnp.concatenate([o, o], axis=0), axis=-1, keepdims=True)
                weights = at_s[t, p]
                da = dot_nt(do, kv_s[near, vlanes])
                ds = (weights.astype(F32) * (da - delta)).astype(BF)
                dq_s[at, lanes] = unstacked(dot_nn(ds, kv_s[near, lanes])) * HD**-0.5
                dkv_s[near, lanes] = dkv_s[near, lanes] + dot_tn(ds, stacked(q_s[at, lanes]))
                dkv_s[near, vlanes] = dkv_s[near, vlanes] + dot_tn(weights, do)
            return carry

        blocks(rows, tile)
        copies[5].wait()

        def turn(i, at, carry):
            inner = pl.ds(pl.multiple_of(i * BLK + BLK, BLK), BLK)
            cos, sin = cos_ref[at, :], sin_ref[at, :]
            for p in range(PAIRS):
                lanes = slice(p * 128, (p + 1) * 128)
                dq = dq_s[at, lanes]
                dk = dkv_s[inner, lanes]
                dp_s[at, lanes] = (dq * cos - swap_halves(dq) * sin).astype(BF)
                dp_s[at, D + p * 128 : D + (p + 1) * 128] = (dk * cos - swap_halves(dk) * sin).astype(BF)
                dp_s[at, 2 * D + p * 128 : 2 * D + (p + 1) * 128] = dkv_s[
                    inner, D + p * 128 : D + (p + 1) * 128
                ].astype(BF)
            xhat, _ = normalise(x_s[at, :])
            a_s[at, :] = (xhat * gain).astype(BF)
            return carry

        blocks(rows, turn)

        dwo = dot_tn(gl_s[top, :], o_s[top, :])
        transposed_out(out, dwo, lambda b: pl.ds(384 + b * 64, 64))
        low_spot = (every, pl.ds(384, 128))
        out.send(0, low_spot)
        for half in range(2):
            dwi = dot_tn(dp_s[top, half * 768 : (half + 1) * 768], a_s[top, :])
            for q in range(2):
                for b in range(2):
                    pair = [
                        dwi[q * 384 + r * 192 : q * 384 + (r + 1) * 192, b * LANES : (b + 1) * LANES] for r in range(2)
                    ]
                    out.put((2 * half + q, pl.ds(b * 192, 192), slice(None)), pair)
        high_spot = (every, pl.ds(0, 384))
        out.send(1, high_spot)
        copies[6].wait()
        da_s[top, :] = dot_nt(dp_s[top, :], ain[...])

        def last(i, at, carry):
            xhat, inv = normalise(x_s[at, :])
            da = da_s[at, :]
            g_s[at, :] = g_s[at, :] + norm_back(da, xhat, inv, gain)
            return carry + fold(da * xhat)

        small_ref[0:1, :] = total(blocks(rows, last, jnp.zeros((8, D), F32)))
        g_out = pltpu.make_async_copy(g_s.at[top], out_h.at[top], sem.at[7])
        g_out.start()
        out.wait(0, low_spot)
        out.wait(1, high_spot)
        g_out.wait()

    by_rows(n_ref, run)


def attend_back(l, n, core, g, cos, sin, gains, xs, q, kv, at, o, ain, aout, deps=()):
    vm = pltpu.VMEM
    return call(
        functools.partial(attend_back_body, l),
        [SMEM, SMEM] + [VMEM] * 3 + [ANY] * 8,
        [
            (struct((CAP, D), F32), ANY),
            (struct((4, 512, LANES), BF), ANY),
            (struct((4, 512, LANES), BF), ANY),
            (struct((8, D), F32), VMEM),
        ],
        [
            vm((CAP, D), F32), vm((CAP, D), F32), vm((CAP, D), BF), vm((CAP + 2 * BLK, 2 * D), BF),
            vm((CAP // BLK, PAIRS, 2 * BLK, 3 * BLK), BF), vm((CAP, D), BF), vm((D, 3 * D), BF), vm((D, D), BF),
            vm((CAP, D), BF), vm((CAP, D), BF), vm((CAP, D), BF), vm((CAP, D), F32),
            vm((CAP + 2 * BLK, 2 * D), F32), vm((CAP, 3 * D), BF), vm((CAP, D), F32),
            vm((2, 4, 512, LANES), BF),
            pltpu.SemaphoreType.DMA((8 + CAP // BLK,)), pltpu.SemaphoreType.DMA((4,)),
        ],
        (n, core, cos, sin, gains, g, xs, q, kv, at, o, ain, aout),
        flops=16 * 640 * D * D,
        moved=20 * 2**20,
        name=f"attend_back_{l}",
        deps=deps,
    )


def add(*terms):
    acc = terms[0].astype(F32)
    for term in terms[1:]:
        acc = acc + term.astype(F32)
    return acc.astype(BF)


def spot_of(place_ref):
    x, y, core = place_ref[0], place_ref[1], place_ref[3]
    even = core == 0
    return jnp.where(even, x, y), jnp.where(even, y, x), 1 + core, 2 - core


def split_first_body(sizes, place_ref, *refs):
    count = len(sizes)
    keeps, gots = refs[:count], refs[count : 2 * count]
    kept, sent = refs[2 * count :]
    first, _, by_first, by_second = spot_of(place_ref)
    off = 0
    for keep, got, n in zip(keeps, gots, sizes):
        at = pl.ds(off, n)

        def one(z, carry, keep=keep, got=got, at=at):
            for j in range(2):
                own = first * by_first + j * by_second
                other = (1 - first) * by_first + j * by_second
                kept[z, j, at] = add(keep[z, own], got[z, own])
                sent[z, j, at] = add(keep[z, other], got[z, other])
            return carry

        lax.fori_loop(0, 4, one, jnp.int32(0))
        off += n


def split_second_body(place_ref, keep, got, kept, sent):
    _, second, _, _ = spot_of(place_ref)

    def one(z, carry):
        kept[z] = add(keep[z, second], got[z, second])
        sent[z] = add(keep[z, 1 - second], got[z, 1 - second])
        return carry

    lax.fori_loop(0, 4, one, jnp.int32(0))


def split_z_body(plan, place_ref, *refs):
    ins, outs = refs[:-4], refs[-4:]
    z = place_ref[2]
    for k, ref in enumerate(outs):
        at = lax.rem(z + k, 4)
        off = used = 0
        for count, n in plan:
            terms = [r[at] for r in ins[used : used + count]]
            ref[pl.ds(off, n), :] = add(*terms) if count > 1 else terms[0]
            used += count
            off += n


def row_pairs(bit):
    return [(i, i ^ bit) for i in range(4)]


def along(axis):
    return [(r * 8 + t, (r ^ (1 << ((t + axis) % 2))) * 8 + t) for r in range(4) for t in range(8)]


def sum_cores_body(sizes, *refs):
    count = len(sizes)
    keeps, gots, out = refs[:count], refs[count : 2 * count], refs[2 * count]
    off = 0
    for keep, got, n in zip(keeps, gots, sizes):
        at = pl.ds(off, n)

        def one(z, carry, keep=keep, got=got, at=at):
            for j in range(4):
                out[j, z, at] = add(keep[z, j], got[z, j])
            return carry

        lax.fori_loop(0, 4, one, jnp.int32(0))
        off += n


class Group:
    def __init__(self, spot, members):
        self.spot = spot
        self.keeps = [keep for _, keep, _ in members]
        self.sizes = [keep.shape[1] // 4 for keep in self.keeps]
        self.names = [name for name, _, _ in members]
        self.n = sum(self.sizes)
        self.bytes = 16 * self.n * LANES * 2
        self.gots = [got for _, _, got in members]

    def cores(self):
        shaped = lambda v: v.reshape(4, 4, v.shape[1] // 4, LANES)
        return (*map(shaped, self.keeps), *map(shaped, self.gots))

    def offload(self, deps):
        both = call(
            functools.partial(sum_cores_body, self.sizes),
            [VMEM] * (2 * len(self.sizes)),
            [(struct((4, 4, self.n, LANES), BF), VMEM)],
            [],
            self.cores(),
            moved=3 * self.bytes,
            name="sum_cores",
            deps=deps,
        )[0]
        part = lax.psum_scatter(both, "rows", scatter_dimension=0, tiled=True)
        self.terms = [part.reshape(4, self.n, LANES)]
        return [both]

    def first(self, deps, work=0):
        self.kept, sent = call(
            functools.partial(split_first_body, self.sizes),
            [SMEM] + [VMEM] * (2 * len(self.sizes)),
            [(struct((4, 2, self.n, LANES), BF), VMEM)] * 2,
            [],
            (self.spot, *self.cores()),
            moved=3 * self.bytes,
            name="split_first",
            flops=work,
            deps=deps,
        )
        self.got = lax.ppermute(sent, ("rows", "tm"), along(0))
        return [self.kept]

    def second(self, deps, work=0):
        self.kept, sent = call(
            split_second_body,
            [SMEM] + [VMEM] * 2,
            [(struct((4, self.n, LANES), BF), VMEM)] * 2,
            [],
            (self.spot, self.kept, self.got),
            moved=3 * self.bytes // 2,
            name="split_second",
            flops=work,
            deps=deps,
        )
        self.terms = [self.kept, lax.ppermute(sent, ("rows", "tm"), along(1))]
        return [self.kept]


def merge_body(*refs):
    *ins, out = refs
    off = 0
    for ref in ins:
        n = ref.shape[1]
        out[:, pl.ds(off, n), :] = ref[...]
        off += n


def offloaded_rest(groups, deps):
    n = sum(group.n for group in groups)
    part = call(
        merge_body,
        [VMEM] * len(groups),
        [(struct((4, n, LANES), BF), VMEM)],
        [],
        [group.terms[0] for group in groups],
        moved=16 * n * LANES,
        name="merge",
        deps=deps,
    )[0]
    mine = lax.psum_scatter(
        part, "tm", scatter_dimension=0, tiled=True, axis_index_groups=[[0, 2, 4, 6], [1, 3, 5, 7]]
    )
    mine = mine.reshape(part.shape[1:])
    return mine, lax.all_gather(mine, "rows", axis=0, tiled=True)


def along_z(spot, groups, deps, work=0):
    ins = [term for group in groups for term in group.terms]
    n = sum(group.n for group in groups)
    own, *others = call(
        functools.partial(split_z_body, [(len(group.terms), group.n) for group in groups]),
        [SMEM] + [VMEM] * len(ins),
        [(struct((n, LANES), BF), VMEM)] * 4,
        [],
        (spot, *ins),
        moved=16 * n * LANES * 2,
        name="split_z",
        flops=work,
        deps=deps,
    )
    return [own] + [
        lax.ppermute(v, "tm", [(i, (i + 2 * k) % 8) for i in range(8)]) for k, v in zip((1, 2, 3), others)
    ]


def join_body(plan, *refs):
    *ins, out = refs
    off = at = 0
    for count, n in plan:
        out[pl.ds(at, n), :] = add(*(ref[...] for ref in ins[off : off + count])) if count > 1 else ins[off][...]
        off += count
        at += n


def gathered(lists, deps):
    ins = [term for terms in lists for term in terms]
    plan = [(len(terms), terms[0].shape[0]) for terms in lists]
    n = sum(rows for _, rows in plan)
    mine = call(
        functools.partial(join_body, plan),
        [VMEM] * len(ins),
        [(struct((n, LANES), BF), VMEM)],
        [],
        ins,
        moved=6 * n * LANES,
        name="join",
        deps=deps,
    )[0]
    return [mine] + [lax.ppermute(mine, "rows", row_pairs(bit)) for bit in (1, 2, 3)]


def finish_body(members, by_bit, me_ref, *refs):
    count = 4 if by_bit else 1
    chunks = refs[:count]
    fin_h, fout_h, ain_h, aout_h, pin_h, pout_h, small_h = refs[-13:-6]
    whole, fout, ain, pin, narrow, sem = refs[-6:]
    me = me_ref[0]
    rows = sum(n for _, _, n in members)
    off = 0
    waits = []
    for i, (l, name, n) in enumerate(members):
        for j in range(4):
            if by_bit:
                owner = pl.multiple_of(jnp.bitwise_xor(me, j) * n, n)
                whole[i, pl.ds(owner, n), :] = chunks[j][pl.ds(off, n), :].astype(F32)
            else:
                whole[i, pl.ds(j * n, n), :] = chunks[0][pl.ds(j * rows + off, n), :].astype(F32)
        off += n
        if name in ("f0", "f1"):
            k = int(name == "f1")
            for b in range(FF // LANES):
                fout[i, :, pl.ds(b * LANES, LANES)] = whole[i, pl.ds(D + b * 64, 64), :]
            jobs = [(whole.at[i, pl.ds(0, D)], fin_h.at[l, k]), (fout.at[i], fout_h.at[l, k])]
            if 4 * n > 1024:
                jobs.append((whole.at[i, pl.ds(1024, SMALL_ROWS // 4)], small_h))
        elif name == "c":
            pin[i, pl.ds(0, 256), :] = whole[i, pl.ds(0, 256), 0:128]
            pin[i, pl.ds(256, 256), :] = whole[i, pl.ds(0, 256), 128:256]
            for b in range(2):
                narrow[i, :, pl.ds(b * LANES, LANES)] = whole[i, pl.ds(256 + b * 64, 64), :]
            jobs = [(pin.at[i], pin_h.at[l]), (narrow.at[i], pout_h.at[l])]
        else:
            for b in range(2):
                ain[i, :, pl.ds(b * LANES, LANES)] = whole[i, pl.ds(b * 192, 192), :]
                narrow[i, :, pl.ds(b * LANES, LANES)] = whole[i, pl.ds(384 + b * 64, 64), :]
            jobs = [(ain.at[i], ain_h.at[l]), (narrow.at[i], aout_h.at[l])]
        for j, (src, dst) in enumerate(jobs):
            c = pltpu.make_async_copy(src, dst, sem.at[3 * i + j])
            c.start()
            waits.append(c)
    for c in waits:
        c.wait()


def finish(layers, me, groups, chunks, before, deps=()):
    members = [(*name, size) for group in groups for name, size in zip(group.names, group.sizes)]
    count = len(members)
    shapes = [
        (layers, 2, D, FF // 8), (layers, 2, D // 8, FF), (layers, 3 * D // 8, D), (layers, D // 8, D),
        (layers, D, 2 * D // 8), (layers, D // 8, D), (SMALL_ROWS // 4, LANES),
    ]
    vm = pltpu.VMEM

    def body(*refs):
        finish_body(members, len(chunks) == 4, *refs)

    return pl.pallas_call(
        body,
        out_shape=[struct(shape, F32) for shape in shapes],
        in_specs=[SMEM] + [VMEM] * len(chunks) + [ANY] * (len(before) + len(deps)),
        out_specs=[ANY] * 7,
        scratch_shapes=[
            vm((count, 1024 + SMALL_ROWS, LANES), F32), vm((count, 64, FF), F32), vm((count, 192, D), F32),
            vm((count, D, 128), F32), vm((count, 64, D), F32), pltpu.SemaphoreType.DMA((3 * count,)),
        ],
        input_output_aliases={1 + len(chunks) + i: i for i in range(len(before))},
        compiler_params=pltpu.CompilerParams(vmem_limit_bytes=VMEM_LIMIT),
        name="finish",
    )(me, *chunks, *before, *deps)


def per_device(
    frames, segment_ids, norm_gains, feed_in, feed_out, attend_in, attend_out, point_in, depthwise, stat_mean,
    stat_var, batch_scale, batch_shift, point_out, cotangent,
):
    batches, row_count, frame_count, model_dim = frames.shape
    layers = norm_gains.shape[0]
    tm_size = lax.axis_size("tm")
    rows_size = lax.axis_size("rows")
    tm = lax.axis_index("tm")
    row = lax.axis_index("rows")
    fast = tm_size == 8 and rows_size == 4
    half = batches // 2

    ids = segment_ids[:, 0] + 1
    id_rows = jnp.broadcast_to(ids.reshape(1, -1).astype(BF), (16, batches * frame_count))
    parts_of = lambda v, odd: v.reshape(half, 2, frame_count, model_dim)[:, odd].reshape(-1, model_dim)
    message = lambda odd: jnp.concatenate([parts_of(frames, odd), parts_of(cotangent, odd), id_rows], axis=0)
    above = shifted(message(0), "tm", -1)
    below = shifted(message(1), "tm", 1)
    flat = lambda v: v.reshape(batches * frame_count, model_dim)
    x0, g, chooser, cos, sin, kb, kr, n = pack(ids.astype(F32), flat(frames), flat(cotangent), below, above)
    small = (norm_gains, depthwise, stat_mean, stat_var, batch_scale, batch_shift)
    mats = (feed_in, feed_out, attend_in, attend_out, point_in, point_out)
    act, xs, hs, q, kv, at, o, u, z = forward(n, x0, cos, sin, kb, kr, small, mats)

    def unpacked(packed):
        spread = lax.dot_general(
            chooser, packed, (((0,), (0,)), ((), ())), preferred_element_type=F32
        ).astype(BF).reshape(half, 2, 2, frame_count, model_dim)
        from_below = shifted(spread[:, 0, 1], "tm", 1)
        from_above = shifted(spread[:, 1, 0], "tm", -1)
        even = spread[:, 0, 0] + from_below
        odd = spread[:, 1, 1] + from_above
        return jnp.stack([even, odd], axis=1).reshape(batches, 1, frame_count, model_dim)

    activations = unpacked(act)

    if fast:
        spot = jnp.stack([row % 2, row // 2, tm // 2, tm % 2]).astype(jnp.int32)
        core = (tm % 2).astype(jnp.int32).reshape(1)
    else:
        spot = None
        core = jnp.zeros((1,), jnp.int32)

    members = {}
    smalls = {}
    parts = {
        "f1": lambda l: (feed_back, l, 1, n, core, g, norm_gains, xs, hs, feed_in, feed_out),
        "c": lambda l: (conv_back, l, n, core, g, kb, small, xs, u, z, point_in, point_out),
        "a": lambda l: (attend_back, l, n, core, g, cos, sin, norm_gains, xs, q, kv, at, o, attend_in, attend_out),
        "f0": lambda l: (feed_back, l, 0, n, core, g, norm_gains, xs, hs, feed_in, feed_out),
    }
    order = [(l, name) for l in range(layers) for name in ("f0", "a", "c", "f1")]

    def back(l, name, deps=(), **more):
        nonlocal g
        kernel, *args = parts[name](l)
        g, kept, sent, smalls[l, name] = kernel(*args, deps=deps, **more)
        members[l, name] = ((l, name), kept, sent)

    crossed = {}

    def begin(l, name):
        crossed[l, name] = lax.ppermute(members[l, name][2], "tm", [(i, i ^ 1) for i in range(8)])

    def group(*names):
        for name in names:
            if name not in crossed:
                begin(*name)
        return Group(spot, [(name, members[name][1], crossed[name]) for name in names])

    if fast:
        me = (2 * spot[1] + spot[0]).reshape(1)
        back(1, "f1")
        begin(1, "f1")
        back(1, "c")
        one = group((1, "f1"), (1, "c"))
        made = one.offload([])
        back(1, "a", made)
        begin(1, "a")
        back(1, "f0")
        two = group((1, "a"), (1, "f0"))
        made = two.offload([])
        back(0, "f1", made + one.terms)
        begin(0, "f1")
        back(0, "c")
        begin(0, "c")
        three = group((0, "f1"))
        made = three.first([g])
        mine_early, all_early = offloaded_rest([one, two], made)
        back(0, "a", made + two.terms)
        four = group((0, "c"), (0, "a"))
        made = three.second([g])
        made += four.first(made)
        back(0, "f0", made + [mine_early], smalls=[smalls[name] for name in order[1:]])
        five = group((0, "f0"))
        z_three = along_z(spot, [three], [g], TAIL_WORK)
        made = five.first(z_three[:1])
        made = four.second(made)
        z_four = along_z(spot, [four], made)
        made = five.second(z_four[:1])
        outs = finish(layers, me, [one, two], [all_early], [], made)
        chunks_mid = gathered([z_three, z_four], outs[:1])
        z_five = along_z(spot, [five], chunks_mid[:1])
        chunks_late = gathered([z_five], [])
        outs = finish(layers, me, [three, four], chunks_mid, outs, chunks_late[:1])
        *mats_out, small_out = finish(layers, me, [five], chunks_late, outs)
        mats_out = [
            v.swapaxes(-1, -2) if turned else v for v, turned in zip(mats_out, (False, True, True, True, False, True))
        ]
        lines = small_out.reshape(-1, 4, 64).swapaxes(0, 1).reshape(-1, 64)
        starts = {name: 0 for name in order}
        at_row = 0
        for name in order:
            starts[name] = at_row
            at_row += smalls[name].shape[0]
        pieces = lambda name, first, count: [
            lines[starts[l, name] + first : starts[l, name] + first + count] for l in range(layers)
        ]
    else:
        for l in reversed(range(layers)):
            for name in ("f1", "c", "a", "f0"):
                back(l, name)
        pieces = None
    filled = lax.broadcasted_iota(jnp.int32, g.shape, 0) < n[0]
    frames_grad = unpacked(jnp.where(filled, g, 0.0).astype(BF))

    if not fast:
        mats_out, lines_of = general_sums(layers, members, smalls, order)
        pieces = lambda name, first, count: [lines_of[l, name][first : first + count] for l in range(layers)]
    gains_out = jnp.stack(
        [
            jnp.concatenate(rows, axis=0)
            for rows in zip(
                pieces("f0", 0, 1), pieces("a", 0, 1), pieces("c", 0, 1), pieces("f1", 0, 1), pieces("f1", 1, 1)
            )
        ]
    )
    fin, fout, ain, aout, pin, pout = mats_out
    return (
        activations,
        frames_grad,
        gains_out,
        fin,
        fout,
        ain,
        aout,
        pin,
        jnp.stack(pieces("c", 8, KERNEL)),
        jnp.concatenate(pieces("c", 1, 1), axis=0),
        jnp.concatenate(pieces("c", 2, 1), axis=0),
        pout,
    )


def general_sums(layers, members, smalls, order):
    def natural(l, name):
        _, even, odd = members[l, name]
        return jnp.stack([even, odd], axis=1).astype(F32).reshape(8, -1, LANES)

    def wide(v, count):
        r = v.shape[1] // count
        return jnp.swapaxes(v.reshape(8, count, r, LANES), 1, 2).reshape(8 * r, count * LANES)

    def over_all(v):
        v = lax.psum_scatter(v, "tm", scatter_dimension=v.ndim - 1, tiled=True)
        return lax.psum(v, "rows")

    fin, fout, ain, aout, pin, pout = [], [], [], [], [], []
    for l in range(layers):
        f = [natural(l, "f0"), natural(l, "f1")]
        fin.append(jnp.stack([jnp.moveaxis(v[:, :D], 0, 1).reshape(D, FF) for v in f]))
        fout.append(jnp.stack([wide(v[:, D:], FF // LANES).T for v in f]))
        v = natural(l, "a")
        ain.append(wide(v[:, :384], 2).T)
        aout.append(wide(v[:, 384:], 2).T)
        v = natural(l, "c")
        top = jnp.concatenate([v[:, :256, :128], v[:, :256, 128:]], axis=1)
        pin.append(jnp.moveaxis(top, 0, 1).reshape(D, 2 * D))
        pout.append(wide(v[:, 256:], 2).T)
    mats_out = [over_all(jnp.stack(v)) for v in (fin, fout, ain, aout, pin, pout)]
    small_all = over_all(jnp.concatenate([smalls[name] for name in order], axis=0))
    lines_of = {}
    at = 0
    for name in order:
        rows = smalls[name].shape[0]
        lines_of[name] = small_all[at : at + rows]
        at += rows
    return mats_out, lines_of


def solution(mesh):
    rep = P()
    in_specs = (
        P(None, "rows", "tm", None), P(None, "rows", "tm"), rep, rep, rep, rep, rep, rep, rep, rep, rep, rep, rep, rep,
        P(None, "rows", "tm", None),
    )
    out_specs = (
        P(None, "rows", "tm", None), P(None, "rows", "tm", None), P(None, None, "tm"), P(None, None, None, "tm"),
        P(None, None, None, "tm"), P(None, None, "tm"), P(None, None, "tm"), P(None, None, "tm"),
        P(None, None, "tm"), P(None, "tm"), P(None, "tm"), P(None, None, "tm"),
    )
    return jax.shard_map(per_device, mesh=mesh, in_specs=in_specs, out_specs=out_specs, check_vma=False)
```

```python
import functools

import jax
import jax.numpy as jnp
import numpy as np
from jax import lax
from jax.experimental import pallas as pl
from jax.experimental.pallas import tpu as pltpu
from jax.sharding import PartitionSpec as P

HD = 64
KERNEL = 9
HALO = 4
EPSILON = 1e-05
MASKED = -1e30
BF = jnp.bfloat16
F32 = jnp.float32
D = 512
FF = 2048
BLK = 128
ROW_CHOICES = (640, 1024)
CAP = ROW_CHOICES[-1]
LANES = 256
SMALL_ROWS = 128
TAIL_WORK = 3e10
PAIRS = D // 128
VMEM_LIMIT = 60 * 2**20
VMEM_SMALL = 24 * 2**20
ANY = pl.BlockSpec(memory_space=pl.ANY)
VMEM = pl.BlockSpec(memory_space=pltpu.VMEM)
SMEM = pl.BlockSpec(memory_space=pltpu.SMEM)


def shifted(array, axis, by):
    size = lax.axis_size(axis)
    pairs = [(i, i + by) for i in range(size) if 0 <= i + by < size]
    return lax.ppermute(array, axis, pairs)


def struct(shape, dtype):
    return jax.ShapeDtypeStruct(shape, dtype)


def call(body, ins, outs, scratch, args, flops=0, moved=0, name="kernel", deps=(), vmem=VMEM_LIMIT):
    count = len(ins)

    def inner(*refs):
        body(*refs[:count], *refs[count + len(deps) :])

    return pl.pallas_call(
        inner,
        out_shape=[s for s, _ in outs],
        in_specs=list(ins) + [ANY] * len(deps),
        out_specs=[b for _, b in outs],
        scratch_shapes=scratch,
        compiler_params=pltpu.CompilerParams(vmem_limit_bytes=vmem),
        cost_estimate=pl.CostEstimate(flops=int(flops), bytes_accessed=int(moved), transcendentals=0),
        name=name,
    )(*args, *deps)


def dot_nn(a, b):
    return jnp.dot(a, b, preferred_element_type=F32)


def dot_nt(a, b):
    return lax.dot_general(a, b, (((1,), (1,)), ((), ())), preferred_element_type=F32)


def dot_tn(a, b):
    return lax.dot_general(a, b, (((0,), (0,)), ((), ())), preferred_element_type=F32)


def sigmoid(v):
    return 0.5 + 0.5 * jnp.tanh(0.5 * v)


def normalise(x):
    c = x - jnp.mean(x, axis=-1, keepdims=True)
    inv = lax.rsqrt(jnp.mean(c * c, axis=-1, keepdims=True) + EPSILON)
    return c * inv, inv


def norm_back(grad, xhat, inv, gain):
    w = grad * gain
    return inv * (
        w - jnp.mean(w, axis=-1, keepdims=True) - xhat * jnp.mean(w * xhat, axis=-1, keepdims=True)
    )


def fold(v):
    return jnp.sum(v.reshape(v.shape[0] // 8, 8, v.shape[1]), axis=0)


def total(v):
    return jnp.sum(v, axis=0, keepdims=True)


def by_rows(n_ref, body):
    low = 0
    for rows in ROW_CHOICES:
        n = n_ref[0]
        cond = n > low
        if rows != CAP:
            cond = cond & (n <= rows)

        @pl.when(cond)
        def _(rows=rows):
            body(rows)

        low = rows


def blocks(rows, step, init=None, size=128):
    def wrapped(i, carry):
        at = pl.ds(pl.multiple_of(i * size, size), size)
        return step(i, at, carry)

    start = init if init is not None else jnp.int32(0)
    return lax.fori_loop(0, rows // size, wrapped, start, unroll=rows == ROW_CHOICES[0])


def each(count, rows, step):
    if rows == ROW_CHOICES[0]:
        for i in range(count):
            step(i)
    else:

        def wrapped(i, carry):
            step(i)
            return carry

        lax.fori_loop(0, count, wrapped, jnp.int32(0))


def cut(i, size):
    return pl.ds(i * size, size) if isinstance(i, int) else pl.ds(pl.multiple_of(i * size, size), size)


def rope_tables():
    half = HD // 2
    freq = np.power(np.float32(10000.0), -(np.arange(half).astype(np.float32) / np.float32(half)))
    angle = np.arange(BLK).astype(np.float32)[:, None] * freq.astype(np.float32)[None, :]
    cos = np.cos(angle.astype(np.float64))
    sin = np.sin(angle.astype(np.float64))
    full = (np.concatenate([cos] * 4, axis=1), np.concatenate([-sin, sin] * 2, axis=1))
    parts = []
    for table in full:
        rest = table
        for _ in range(3):
            piece = rest.astype(jnp.bfloat16)
            parts.append(piece)
            rest = rest - piece.astype(np.float64)
    return np.stack(parts)


def pack_body(
    ids_ref, frames_ref, cot_ref, below_ref, above_ref, tab_ref,
    x_ref, g_ref, p_ref, cos_ref, sin_ref, kb_ref, kr_ref, n_ref,
    keep_s, key_s, dest_s, pos_s, win_s, cot_s,
):
    batches = ids_ref.shape[0]
    half = batches // 2
    shown = (8, BLK)
    below_ids = below_ref[pl.ds(4 * BLK, 16), :].astype(F32)[0:1]
    above_ids = above_ref[pl.ds(4 * BLK, 16), :].astype(F32)[0:1]
    for m in range(batches):
        own = ids_ref[m : m + 1, :]
        below = below_ids[:, m * BLK : (m + 1) * BLK]
        above = above_ids[:, m * BLK : (m + 1) * BLK]
        i = m // 2
        mine = pl.ds(m * BLK, BLK)
        theirs = (pl.ds(i * BLK, BLK), pl.ds((half + i) * BLK, BLK))
        if m % 2 == 0:
            pieces = ((own, own != below[:, BLK - 1 : BLK]), (above, above == own[:, BLK - 1 : BLK]))
            frames = ((frames_ref, mine, cot_ref, mine), (above_ref, theirs[0], above_ref, theirs[1]))
        else:
            pieces = ((below, below == own[:, 0:1]), (own, own != above[:, 0:1]))
            frames = ((below_ref, theirs[0], below_ref, theirs[1]), (frames_ref, mine, cot_ref, mine))
        for j in range(2):
            at = pl.ds((2 * m + j) * BLK, BLK)
            key_s[:, at] = jnp.broadcast_to(pieces[j][0] + 4096.0 * m, shown)
            keep_s[:, at] = jnp.broadcast_to(jnp.where(pieces[j][1], 1.0, 0.0), shown)
            src, rows, cot, cot_rows = frames[j]
            win_s[at, :] = src[rows, :]
            cot_s[at, :] = cot[cot_rows, :]
    square = (BLK, BLK)
    earlier = lax.broadcasted_iota(jnp.int32, square, 0) < lax.broadcasted_iota(jnp.int32, square, 1)
    ramp = earlier.astype(F32).astype(BF)
    before = jnp.zeros((8, 1), F32)
    for j in range(2 * batches):
        at = pl.ds(j * BLK, BLK)
        keep = keep_s[:, at]
        dest_s[:, at] = jnp.where(keep > 0.5, before + dot_nn(keep.astype(BF), ramp), -1.0)
        before = before + jnp.sum(keep, axis=1, keepdims=True)
    n = (jnp.sum(before) * 0.125 + 0.5).astype(jnp.int32)
    n_ref[0] = n
    for m in range(batches):
        first, second = pl.ds(2 * m * BLK, BLK), pl.ds((2 * m + 1) * BLK, BLK)
        cols = [jnp.broadcast_to(key_s[0:1, at], square).T for at in (first, second)]
        count = lambda mask: jnp.broadcast_to(jnp.sum(jnp.where(mask, 1.0, 0.0), axis=0, keepdims=True), shown)
        pos_s[:, first] = count((cols[0] == key_s[0:1, first]) & earlier)
        pos_s[:, second] = count(cols[0] == key_s[0:1, second]) + count((cols[1] == key_s[0:1, second]) & earlier)
    kr_ref[...] = jnp.full(kr_ref.shape, -1.0, F32)
    rows_all = 2 * batches * BLK

    def step(i, at):
        row = (lax.broadcasted_iota(jnp.int32, (BLK, rows_all), 0) + i * BLK).astype(F32)
        pick = jnp.where(dest_s[0:1, :] == row, 1.0, 0.0)
        p = pick.astype(BF)
        p_ref[at, :] = p
        x_ref[at, :] = dot_nn(p, win_s[...])
        g_ref[at, :] = dot_nn(p, cot_s[...])
        key = jnp.broadcast_to(jnp.sum(pick * key_s[0:1, :], axis=1, keepdims=True), square)
        kb_ref[at, :] = key
        kr_ref[:, pl.ds(i * BLK + BLK, BLK)] = key.T[0:8]
        pos = jnp.sum(pick * pos_s[0:1, :], axis=1, keepdims=True)
        hot = (lax.broadcasted_iota(jnp.int32, square, 1).astype(F32) == pos).astype(F32).astype(BF)
        cos_ref[at, :] = dot_nn(hot, tab_ref[0]) + dot_nn(hot, tab_ref[1]) + dot_nn(hot, tab_ref[2])
        sin_ref[at, :] = dot_nn(hot, tab_ref[3]) + dot_nn(hot, tab_ref[4]) + dot_nn(hot, tab_ref[5])

    for i in range(rows_all // BLK):
        at = pl.ds(i * BLK, BLK)
        if i * BLK < ROW_CHOICES[0]:
            step(i, at)
        else:

            @pl.when(n > ROW_CHOICES[0])
            def _(i=i, at=at):
                step(i, at)

            @pl.when(n <= ROW_CHOICES[0])
            def _(at=at):
                p_ref[at, :] = jnp.zeros((BLK, rows_all), BF)


def pack(ids, frames, cotangent, below, above):
    vm = pltpu.VMEM
    return call(
        pack_body,
        [VMEM] * 6,
        [
            (struct((CAP, D), F32), VMEM),
            (struct((CAP, D), F32), VMEM),
            (struct((CAP, CAP), BF), VMEM),
            (struct((CAP, 128), F32), VMEM),
            (struct((CAP, 128), F32), VMEM),
            (struct((CAP, 128), F32), VMEM),
            (struct((8, CAP + 2 * BLK), F32), VMEM),
            (struct((1,), jnp.int32), SMEM),
        ],
        [vm((8, CAP), F32), vm((8, CAP), F32), vm((8, CAP), F32), vm((8, CAP), F32), vm((CAP, D), BF), vm((CAP, D), BF)],
        (ids, frames, cotangent, below, above, jnp.asarray(rope_tables(), dtype=BF)),
        flops=4 * CAP * CAP * D,
        moved=12 * 2**20,
        name="pack",
    )


def lane_low(shape):
    return lax.broadcasted_iota(jnp.int32, shape, 1) % HD < HD // 2


def swap_halves(v):
    return jnp.where(lane_low(v.shape), pltpu.roll(v, 128 - HD // 2, 1), pltpu.roll(v, HD // 2, 1))


def stacked(v):
    first = lax.broadcasted_iota(jnp.int32, v.shape, 1) < HD
    zero = jnp.zeros_like(v)
    return jnp.concatenate([jnp.where(first, v, zero), jnp.where(first, zero, v)], axis=0)


def unstacked(v):
    half = v.shape[0] // 2
    first = lax.broadcasted_iota(jnp.int32, (half, 128), 1) < HD
    return jnp.where(first, v[:half], v[half:])


def norm_into(x_ref, gain, a_ref, rows):
    def step(i, at, carry):
        xhat, _ = normalise(x_ref[at, :])
        a_ref[at, :] = (xhat * gain).astype(BF)
        return carry

    blocks(rows, step)


def forward_body(
    n_ref, x0_ref, cos_ref, sin_ref, kb_ref, kr_ref, gains_ref, taps_ref, mean_ref, var_ref, scale_ref, shift_ref,
    fin_h, fout_h, ain_h, aout_h, pin_h, pout_h,
    act_ref, xs_h, hs_h, q_h, kv_h, at_h, o_h, u_h, z_h,
    fin, fout, ain, aout, pin, pout, xb, hb, qb, kvb, ab, ob, ub, zb, a_s, gp, kp, w_sem, s_sem,
):
    layers = gains_ref.shape[0]
    weights = [
        (fin_h, (0,), fin.at[0]), (fout_h, (0,), fout.at[0]), (ain_h, (), ain), (aout_h, (), aout),
        (pin_h, (), pin), (pout_h, (), pout), (fin_h, (1,), fin.at[1]), (fout_h, (1,), fout.at[1]),
    ]

    def weight_copy(i, l):
        src, sub, dst = weights[i]
        return pltpu.make_async_copy(src.at[(l,) + sub], dst, w_sem.at[i])

    for i in (0, 1):
        weight_copy(i, 0).start()

    def run(rows):
        tiles = rows // BLK
        top = pl.ds(0, rows)
        saves = [(xb.at[i, top], lambda l, i=i: xs_h.at[l, i, top]) for i in range(5)]
        saves += [(hb.at[k, top], lambda l, k=k: hs_h.at[l, k, top]) for k in range(2)]
        saves += [
            (qb.at[top], lambda l: q_h.at[l, top]),
            (kvb.at[pl.ds(0, rows + 2 * BLK)], lambda l: kv_h.at[l, pl.ds(0, rows + 2 * BLK)]),
            (ab.at[pl.ds(0, tiles)], lambda l: at_h.at[l, pl.ds(0, tiles)]),
            (ob.at[top], lambda l: o_h.at[l, top]),
            (ub.at[top], lambda l: u_h.at[l, top]),
            (zb.at[top], lambda l: z_h.at[l, top]),
        ]

        def save(i, l):
            src, dst = saves[i]
            return pltpu.make_async_copy(src, dst(l), s_sem.at[i])

        def settle(i, l):
            @pl.when(l > 0)
            def _():
                save(i, l - 1).wait()

        def use(i, l):
            weight_copy(i, l).wait()

        def next_weight(i, l):
            @pl.when(l + 1 < layers)
            def _():
                weight_copy(i, l + 1).start()

        kvb[pl.ds(0, BLK), :] = jnp.zeros((BLK, 2 * D), BF)
        kvb[pl.ds(rows + BLK, BLK), :] = jnp.zeros((BLK, 2 * D), BF)
        gp[:, pl.ds(0, 8), :] = jnp.zeros((PAIRS, 8, 128), F32)
        gp[:, pl.ds(rows + 8, 8), :] = jnp.zeros((PAIRS, 8, 128), F32)
        kp[pl.ds(0, BLK), :] = jnp.full((BLK, 128), -1.0, F32)
        kp[pl.ds(rows + BLK, BLK), :] = jnp.full((BLK, 128), -1.0, F32)

        def fill(i, at, carry):
            kp[pl.ds(pl.multiple_of(i * BLK + BLK, BLK), BLK), :] = kb_ref[at, :]
            xb[0, at, :] = x0_ref[at, :]
            return carry

        blocks(rows, fill)

        def feed(l, k, src, dst, gain, wi, early=lambda: None):
            settle(5 + k, l)
            settle(dst, l)

            def first(i, at, carry):
                x = xb[src, at, :]
                xhat, _ = normalise(x)
                a_s[at, :] = (xhat * gain).astype(BF)
                xb[dst, at, :] = x
                return carry

            blocks(rows, first)
            use(wi, l)
            use(wi + 1, l)
            early()

            def chunk(c):
                cols = cut(c, 512)
                h = dot_nn(a_s[top, :], fin[k, :, cols])
                hb[k, top, cols] = h.astype(BF)
                s = (h * sigmoid(h)).astype(BF)
                xb[dst, top, :] = xb[dst, top, :] + 0.5 * dot_nn(s, fout[k, cols, :])

            each(FF // 512, rows, chunk)
            next_weight(wi, l)
            next_weight(wi + 1, l)
            save(5 + k, l).start()
            save(dst, l).start()

        def first_weights(l, which):
            @pl.when(l == 0)
            def _():
                for i in which:
                    weight_copy(i, 0).start()

        def layer(l, carry):
            gains = [gains_ref[l, pl.ds(i, 1), :] for i in range(5)]
            save(0, l).start()
            feed(l, 0, 0, 1, gains[0], 0, lambda: first_weights(l, (2, 3)))
            first_weights(l, (4, 5, 6, 7))

            norm_into(xb.at[1], gains[1], a_s, rows)
            settle(7, l)
            settle(8, l)
            settle(9, l)
            settle(10, l)
            use(2, l)
            for part in range(3):
                proj = dot_nn(a_s[top, :], ain[:, part * D : (part + 1) * D])
                for p in range(PAIRS):
                    lanes = slice(p * 128, (p + 1) * 128)
                    v = proj[:, lanes]
                    if part < 2:
                        v = v * cos_ref[top, :] + swap_halves(v) * sin_ref[top, :]
                    if part == 0:
                        qb[top, lanes] = (v * HD**-0.5).astype(BF)
                    elif part == 1:
                        kvb[pl.ds(BLK, rows), lanes] = v.astype(BF)
                    else:
                        kvb[pl.ds(BLK, rows), D + p * 128 : D + (p + 1) * 128] = v.astype(BF)
            next_weight(2, l)

            def tile(t, at, c):
                near = pl.ds(pl.multiple_of(t * BLK, BLK), 3 * BLK)
                same = kp[near, :] == kr_ref[0:1, pl.ds(pl.multiple_of(t * BLK + BLK, BLK), BLK)]
                same = jnp.concatenate([same, same], axis=1)
                for p in range(PAIRS):
                    lanes = slice(p * 128, (p + 1) * 128)
                    s = dot_nt(kvb[near, lanes], stacked(qb[at, lanes]))
                    s = jnp.where(same, s, MASKED)
                    e = jnp.exp(s - jnp.max(s, axis=0, keepdims=True))
                    low = (e * (1.0 / jnp.sum(e, axis=0, keepdims=True))).astype(BF)
                    ab[t, p] = low
                    o = dot_tn(low, kvb[near, D + p * 128 : D + (p + 1) * 128])
                    ob[at, lanes] = unstacked(o).astype(BF)
                return c

            blocks(rows, tile)
            settle(2, l)
            use(3, l)
            xb[2, top, :] = xb[1, top, :] + dot_nn(ob[top, :], aout[...])
            next_weight(3, l)
            for i in (7, 8, 9, 10, 2):
                save(i, l).start()

            norm_into(xb.at[2], gains[2], a_s, rows)
            settle(11, l)
            settle(12, l)
            use(4, l)
            for half in range(2):
                lanes = slice(half * 256, (half + 1) * 256)
                up1 = dot_nn(a_s[top, :], pin[:, half * 256 : (half + 1) * 256])
                up2 = dot_nn(a_s[top, :], pin[:, D + half * 256 : D + (half + 1) * 256])
                ub[top, lanes] = up1.astype(BF)
                ub[top, D + half * 256 : D + (half + 1) * 256] = up2.astype(BF)
                gated = (up1 * sigmoid(up2)).astype(BF).astype(F32)
                for q in range(2):
                    gp[2 * half + q, pl.ds(8, rows), :] = gated[:, q * 128 : (q + 1) * 128]
            next_weight(4, l)
            rs = lax.rsqrt(var_ref[pl.ds(l, 1), :] + EPSILON)
            mean = mean_ref[pl.ds(l, 1), :]
            scale = scale_ref[pl.ds(l, 1), :]
            shift = shift_ref[pl.ds(l, 1), :]

            def conv(t, at, c):
                near = [pl.ds(t * BLK + 4 + o, BLK) for o in range(KERNEL)]
                own = kb_ref[at, :]
                masks = [kp[pl.ds(t * BLK + BLK - HALO + o, BLK), :] == own for o in range(KERNEL)]
                for p in range(PAIRS):
                    lanes = slice(p * 128, (p + 1) * 128)
                    z = jnp.zeros((BLK, 128), F32)
                    for o in range(KERNEL):
                        w = taps_ref[l, o : o + 1, lanes]
                        z = z + jnp.where(masks[o], w * gp[p, near[o], :], 0.0)
                    zb[at, lanes] = z
                    b = (z - mean[:, lanes]) * rs[:, lanes] * scale[:, lanes] + shift[:, lanes]
                    a_s[at, lanes] = (b * sigmoid(b)).astype(BF)
                return c

            blocks(rows, conv)
            settle(3, l)
            use(5, l)
            xb[3, top, :] = xb[2, top, :] + dot_nn(a_s[top, :], pout[...])
            next_weight(5, l)
            for i in (11, 12, 3):
                save(i, l).start()

            feed(l, 1, 3, 4, gains[3], 6)
            save(0, l).wait()

            def last(i, at, c):
                xhat, _ = normalise(xb[4, at, :])
                y = xhat * gains[4]
                xb[0, at, :] = y
                act_ref[at, :] = y.astype(BF)
                return c

            blocks(rows, last)
            return carry

        lax.fori_loop(0, layers, layer, jnp.int32(0))
        for i in range(1, len(saves)):
            save(i, layers - 1).wait()
        if rows < CAP:
            act_ref[pl.ds(rows, CAP - rows), :] = jnp.zeros((CAP - rows, D), BF)

    by_rows(n_ref, run)


def forward(n, x0, cos, sin, kb, kr, small, mats):
    layers = small[0].shape[0]
    outs = [
        (struct((CAP, D), BF), VMEM),
        (struct((layers, 5, CAP, D), F32), ANY),
        (struct((layers, 2, CAP, FF), BF), ANY),
        (struct((layers, CAP, D), BF), ANY),
        (struct((layers, CAP + 2 * BLK, 2 * D), BF), ANY),
        (struct((layers, CAP // BLK, PAIRS, 3 * BLK, 2 * BLK), BF), ANY),
        (struct((layers, CAP, D), BF), ANY),
        (struct((layers, CAP, 2 * D), BF), ANY),
        (struct((layers, CAP, D), F32), ANY),
    ]
    vm = pltpu.VMEM
    scratch = [
        vm((2, D, FF), BF), vm((2, FF, D), BF), vm((D, 3 * D), BF), vm((D, D), BF), vm((D, 2 * D), BF), vm((D, D), BF),
        vm((5, CAP, D), F32), vm((2, CAP, FF), BF), vm((CAP, D), BF), vm((CAP + 2 * BLK, 2 * D), BF),
        vm((CAP // BLK, PAIRS, 3 * BLK, 2 * BLK), BF), vm((CAP, D), BF), vm((CAP, 2 * D), BF), vm((CAP, D), F32),
        vm((CAP, D), BF), vm((PAIRS, CAP + 16, 128), F32), vm((CAP + 2 * BLK, 128), F32),
        pltpu.SemaphoreType.DMA((8,)), pltpu.SemaphoreType.DMA((13,)),
    ]
    return call(
        forward_body,
        [SMEM] + [VMEM] * 11 + [ANY] * 6,
        outs,
        scratch,
        (n, x0, cos, sin, kb, kr, *small, *mats),
        flops=2 * 640 * 12e6,
        moved=60 * 2**20,
        name="forward",
    )


class Out:
    def __init__(self, core, buf, kept_h, sent_h, sem):
        self.core = core
        self.buf = buf
        self.homes = (kept_h, sent_h)
        self.sem = sem

    def put(self, at, pair):
        self.buf[(self.core,) + at] = pair[0].astype(BF)
        self.buf[(1 - self.core,) + at] = pair[1].astype(BF)

    def copies(self, slot, at):
        return [
            pltpu.make_async_copy(self.buf.at[(i,) + at], home.at[at], self.sem.at[2 * slot + i])
            for i, home in enumerate(self.homes)
        ]

    def send(self, slot, at):
        for c in self.copies(slot, at):
            c.start()

    def wait(self, slot, at):
        for c in self.copies(slot, at):
            c.wait()


def transposed_out(out, dwo, first):
    for z in range(4):
        for b in range(dwo.shape[1] // LANES):
            pair = [dwo[z * 128 + q * 64 : z * 128 + q * 64 + 64, b * LANES : (b + 1) * LANES] for q in range(2)]
            out.put((z, first(b), slice(None)), pair)


def feed_part(l, k, what, core_ref, g_s, ins, outs, scratch):
    final = k == 1
    do_out, do_in = what != "in", what != "out"
    base = D if do_in else 0
    gains_ref, xs_h, hs_h, fin_h, fout_h, *small_refs = ins
    others = len(small_refs)
    keep_h, send_h, small_ref = outs
    x_s, x4_s, h_s, fin, fout, gl_s, a_s, da_s, buf, sem, osem = scratch
    gain = gains_ref[l, pl.ds(3 if final else 0, 1), :]
    gain4 = gains_ref[l, pl.ds(4, 1), :]
    out = Out(core_ref[0], buf, keep_h, send_h, osem)
    every = pl.ds(0, 4)
    high = base + FF * D // (8 * LANES) if do_out else D

    def run(rows):
        top = pl.ds(0, rows)

        def chunk_in(c):
            cols = cut(c, 512)
            made = [pltpu.make_async_copy(hs_h.at[l, k, top, cols], h_s.at[top, cols], sem.at[3 + 3 * c])]
            if do_in:
                made += [
                    pltpu.make_async_copy(fout_h.at[l, k, cols], fout.at[cols], sem.at[4 + 3 * c]),
                    pltpu.make_async_copy(fin_h.at[l, k, :, cols], fin.at[:, cols], sem.at[5 + 3 * c]),
                ]
            return made

        starts = []
        if do_in:
            starts.append(pltpu.make_async_copy(xs_h.at[l, 3 if final else 0, top], x_s.at[top], sem.at[1]))
        if final:
            starts.insert(0, pltpu.make_async_copy(xs_h.at[l, 4, top], x4_s.at[top], sem.at[2]))

        def start():
            for c in starts + chunk_in(0):
                c.start()

        def first(i, at, carry):
            g = g_s[at, :]
            if final:
                xhat, inv = normalise(x4_s[at, :])
                carry = carry + fold(g * xhat)
                g = norm_back(g, xhat, inv, gain4)
                g_s[at, :] = g
            gl_s[at, :] = (0.5 * g).astype(BF)
            if do_in:
                xhat, _ = normalise(x_s[at, :])
                a_s[at, :] = (xhat * gain).astype(BF)
                da_s[at, :] = jnp.zeros((BLK, D), F32)
            return carry

        def low_rows(c):
            low = base + c * 128
            return pl.ds(low, 128) if isinstance(c, int) else pl.ds(pl.multiple_of(low, 128), 128)

        def spots(c):
            return [(c, pl.ds(0, D))] * do_in + [(every, low_rows(c))] * do_out

        def chunk(c):
            cols = cut(c, 512)
            for copy in chunk_in(c):
                copy.wait()
            if isinstance(c, int):
                for copy in chunk_in(c + 2) if c < 2 else []:
                    copy.start()
            else:

                @pl.when(c < 2)
                def _():
                    for copy in chunk_in(c + 2):
                        copy.start()

            h = h_s[top, cols].astype(F32)
            sig = sigmoid(h)
            if do_in:
                ds = dot_nt(gl_s[top, :], fout[cols, :])
                dh = (ds * (sig * (1.0 + h * (1.0 - sig)))).astype(BF)
                dwi = dot_tn(a_s[top, :], dh)
                out.put((c, pl.ds(0, D), slice(None)), (dwi[:, :LANES], dwi[:, LANES:]))
            if do_out:
                dwo = dot_tn(gl_s[top, :], (h * sig).astype(BF))
                step = lambda b: (base + (2 * c + b) * 64)
                transposed_out(
                    out, dwo,
                    lambda b: pl.ds(step(b), 64) if isinstance(c, int) else pl.ds(pl.multiple_of(step(b), 64), 64),
                )
            for i, at in enumerate(spots(c)):
                out.send(2 * c + i, at)
            if do_in:
                da_s[top, :] = da_s[top, :] + dot_nt(dh, fin[:, cols])

        def last(i, at, carry):
            xhat, inv = normalise(x_s[at, :])
            da = da_s[at, :]
            g_s[at, :] = g_s[at, :] + norm_back(da, xhat, inv, gain)
            return carry + fold(da * xhat)

        def small_chunks():
            buf[:, :, pl.ds(high, SMALL_ROWS), :] = jnp.zeros((2, 4, SMALL_ROWS, LANES), BF)
            rows_all = jnp.concatenate([small_ref[...]] + [ref[...] for ref in small_refs], axis=0)
            lines = SMALL_ROWS // 4
            rows_all = jnp.concatenate([rows_all, jnp.zeros((4 * lines - rows_all.shape[0], D), F32)], axis=0)
            for z in range(4):
                pair = []
                for q in range(2):
                    own = rows_all[:, z * 128 + q * 64 : z * 128 + q * 64 + 64]
                    pair.append(jnp.concatenate([own[i * lines : (i + 1) * lines] for i in range(4)], axis=1))
                out.put((z, pl.ds(high, lines), slice(None)), pair)

        low_spot = (every, pl.ds(high, SMALL_ROWS))

        def main(midway):
            for c in starts:
                c.wait()
            for c in chunk_in(1):
                c.start()
            midway()
            gain4_grad = blocks(rows, first, jnp.zeros((8, D), F32))
            each(FF // 512, rows, chunk)
            small_ref[...] = jnp.zeros(small_ref.shape, F32)
            if do_in:
                small_ref[0:1, :] = total(blocks(rows, last, jnp.zeros((8, D), F32)))
            small_ref[1:2, :] = total(gain4_grad)
            if others:
                small_chunks()
                out.send(8, low_spot)

        def finish():
            if others:
                out.wait(8, low_spot)
            for c in range(4):
                for i, at in enumerate(spots(c)):
                    out.wait(2 * c + i, at)

        return start, main, finish

    return run


def feed_spec(l, k, what, smalls, gains, xs, hs, fin, fout):
    vm = pltpu.VMEM
    do_out, do_in = what != "in", what != "out"
    lines = D * do_in + D * do_out + (SMALL_ROWS if smalls else 0)
    none = (8, D)
    return (
        functools.partial(feed_part, l, k, what),
        [(gains, VMEM), (xs, ANY), (hs, ANY), (fin, ANY), (fout, ANY)] + [(v, VMEM) for v in smalls],
        [
            (struct((4, lines, LANES), BF), ANY),
            (struct((4, lines, LANES), BF), ANY),
            (struct((8, D), F32), VMEM),
        ],
        [
            vm((CAP, D) if do_in else none, F32), vm((CAP, D) if k == 1 else none, F32), vm((CAP, FF), BF),
            vm((D, FF) if do_in else none, BF), vm((FF, D) if do_in else none, BF), vm((CAP, D), BF),
            vm((CAP, D) if do_in else none, BF), vm((CAP, D) if do_in else none, F32),
            vm((2, 4, lines, LANES), BF),
            pltpu.SemaphoreType.DMA((15,)), pltpu.SemaphoreType.DMA((18,)),
        ],
        (2 * do_out + 6 * do_in) * 640 * D * FF,
    )


def conv_part(l, core_ref, g_s, ins, outs, scratch):
    kb_ref, gains_ref, taps_ref, mean_ref, var_ref, scale_ref, shift_ref, xs_h, u_h, z_h, pin_h, pout_h = ins
    keep_h, send_h, small_ref = outs
    x_s, u_s, z_s, pin, pout, gl_s, a_s, e_s, de_s, gp, dzp, kp, du_s, buf, sem, osem = scratch
    gain = gains_ref[l, pl.ds(2, 1), :]
    rs = lax.rsqrt(var_ref[pl.ds(l, 1), :] + EPSILON)
    mean = mean_ref[pl.ds(l, 1), :]
    scale = scale_ref[pl.ds(l, 1), :]
    shift = shift_ref[pl.ds(l, 1), :]
    out = Out(core_ref[0], buf, keep_h, send_h, osem)
    every = pl.ds(0, 4)

    def run(rows):
        top = pl.ds(0, rows)
        copies = [
            None,
            pltpu.make_async_copy(pout_h.at[l], pout, sem.at[1]),
            pltpu.make_async_copy(z_h.at[l, top], z_s.at[top], sem.at[2]),
            pltpu.make_async_copy(u_h.at[l, top], u_s.at[top], sem.at[3]),
            pltpu.make_async_copy(xs_h.at[l, 2, top], x_s.at[top], sem.at[4]),
            pltpu.make_async_copy(pin_h.at[l], pin, sem.at[5]),
        ]
        low_spot = (every, pl.ds(256, 128))
        high_spot = (every, pl.ds(0, 256))

        def start():
            for c in copies[1:4]:
                c.start()

        def finish():
            out.wait(0, low_spot)
            out.wait(1, high_spot)

        return start, functools.partial(conv_work, rows, copies), finish

    def conv_work(rows, copies, midway):
        top = pl.ds(0, rows)
        low_spot = (every, pl.ds(256, 128))
        high_spot = (every, pl.ds(0, 256))
        for ref in (gp, dzp):
            ref[:, pl.ds(0, 8), :] = jnp.zeros((PAIRS, 8, 128), F32)
            ref[:, pl.ds(rows + 8, 8), :] = jnp.zeros((PAIRS, 8, 128), F32)
        kp[pl.ds(0, 8), :] = jnp.full((8, 128), -1.0, F32)
        kp[pl.ds(rows + 8, 8), :] = jnp.full((8, 128), -1.0, F32)

        def low(i, at, carry):
            gl_s[at, :] = g_s[at, :].astype(BF)
            kp[pl.ds(pl.multiple_of(i * BLK + 8, 8), BLK), :] = kb_ref[at, :]
            return carry

        blocks(rows, low)
        for c in copies[1:4]:
            c.wait()
        for c in copies[4:]:
            c.start()
        midway()
        de_s[top, :] = dot_nt(gl_s[top, :], pout[...])
        copies[4].wait()

        def first(i, at, carry):
            scale_grad, shift_grad = carry
            inner = pl.ds(pl.multiple_of(i * BLK + 8, 8), BLK)
            hat = (z_s[at, :] - mean) * rs
            b = hat * scale + shift
            sig = sigmoid(b)
            e_s[at, :] = (b * sig).astype(BF)
            db = de_s[at, :] * (sig * (1.0 + b * (1.0 - sig)))
            dz = (db * scale * rs).astype(BF).astype(F32)
            u1 = u_s[at, pl.ds(0, D)].astype(F32)
            u2 = u_s[at, pl.ds(D, D)].astype(F32)
            gated = (u1 * sigmoid(u2)).astype(BF).astype(F32)
            for p in range(PAIRS):
                dzp[p, inner, :] = dz[:, p * 128 : (p + 1) * 128]
                gp[p, inner, :] = gated[:, p * 128 : (p + 1) * 128]
            xhat, _ = normalise(x_s[at, :])
            a_s[at, :] = (xhat * gain).astype(BF)
            return (scale_grad + fold(db * hat), shift_grad + fold(db))

        zero = jnp.zeros((8, D), F32)
        scale_grad, shift_grad = blocks(rows, first, (zero, zero))
        small_ref[...] = jnp.zeros(small_ref.shape, F32)
        small_ref[1:2, :] = total(scale_grad)
        small_ref[2:3, :] = total(shift_grad)
        dwo = dot_tn(gl_s[top, :], e_s[top, :])
        transposed_out(out, dwo, lambda b: pl.ds(256 + b * 64, 64))
        out.send(0, low_spot)

        for p in range(PAIRS):
            lanes = slice(p * 128, (p + 1) * 128)

            def taps(t, at, carry, lanes=lanes, p=p):
                own = kb_ref[at, :]
                dz_own = dzp[p, pl.ds(pl.multiple_of(t * BLK + 8, 8), BLK), :]
                dg = jnp.zeros((BLK, 128), F32)
                sums = []
                for o in range(KERNEL):
                    near = pl.ds(t * BLK + 4 + o, BLK)
                    mask = kp[near, :] == own
                    sums.append(carry[o] + fold(jnp.where(mask, dz_own * gp[p, near, :], 0.0)))
                    w = taps_ref[l, KERNEL - 1 - o : KERNEL - o, lanes]
                    dg = dg + jnp.where(mask, w * dzp[p, near, :], 0.0)
                u1 = u_s[at, lanes].astype(F32)
                sig = sigmoid(u_s[at, D + p * 128 : D + (p + 1) * 128].astype(F32))
                du_s[at, lanes] = (dg * sig).astype(BF)
                du_s[at, D + p * 128 : D + (p + 1) * 128] = (dg * u1 * sig * (1.0 - sig)).astype(BF)
                return tuple(sums)

            sums = blocks(rows, taps, tuple(jnp.zeros((8, 128), F32) for _ in range(KERNEL)))
            for o in range(KERNEL):
                small_ref[8 + o : 9 + o, lanes] = total(sums[o])

        for half in range(2):
            dwi = dot_tn(a_s[top, :], du_s[top, half * 512 : (half + 1) * 512])
            for q in range(2):
                pair = [
                    jnp.concatenate([dwi[: D // 2, at : at + 128], dwi[D // 2 :, at : at + 128]], axis=1)
                    for at in (q * 256, q * 256 + 128)
                ]
                out.put((2 * half + q, pl.ds(0, 256), slice(None)), pair)
        out.send(1, high_spot)
        copies[5].wait()
        de_s[top, :] = dot_nt(du_s[top, :], pin[...])

        def last(i, at, carry):
            xhat, inv = normalise(x_s[at, :])
            da = de_s[at, :]
            g_s[at, :] = g_s[at, :] + norm_back(da, xhat, inv, gain)
            return carry + fold(da * xhat)

        small_ref[0:1, :] = total(blocks(rows, last, zero))

    return run


def conv_spec(l, kb, small, xs, u, z, pin, pout):
    vm = pltpu.VMEM
    return (
        functools.partial(conv_part, l),
        [(kb, VMEM)] + [(v, VMEM) for v in small] + [(v, ANY) for v in (xs, u, z, pin, pout)],
        [
            (struct((4, 384, LANES), BF), ANY),
            (struct((4, 384, LANES), BF), ANY),
            (struct((24, D), F32), VMEM),
        ],
        [
            vm((CAP, D), F32), vm((CAP, 2 * D), BF), vm((CAP, D), F32), vm((D, 2 * D), BF),
            vm((D, D), BF), vm((CAP, D), BF), vm((CAP, D), BF), vm((CAP, D), BF), vm((CAP, D), F32),
            vm((PAIRS, CAP + 16, 128), F32), vm((PAIRS, CAP + 16, 128), F32), vm((CAP + 16, 128), F32),
            vm((CAP, 2 * D), BF), vm((2, 4, 384, LANES), BF),
            pltpu.SemaphoreType.DMA((6,)), pltpu.SemaphoreType.DMA((4,)),
        ],
        12 * 640 * D * D,
    )


def attend_part(l, core_ref, g_s, ins, outs, scratch):
    cos_ref, sin_ref, gains_ref, xs_h, q_h, kv_h, at_h, o_h, ain_h, aout_h = ins
    keep_h, send_h, small_ref = outs
    x_s, q_s, kv_s, at_s, o_s, ain, aout, gl_s, a_s, do_s, dq_s, dkv_s, dp_s, da_s, buf, sem, osem = scratch
    out = Out(core_ref[0], buf, keep_h, send_h, osem)
    every = pl.ds(0, 4)
    gain = gains_ref[l, pl.ds(1, 1), :]

    def run(rows):
        tiles = rows // BLK
        top = pl.ds(0, rows)
        wide = pl.ds(0, rows + 2 * BLK)
        copies = [
            pltpu.make_async_copy(aout_h.at[l], aout, sem.at[0]),
            pltpu.make_async_copy(o_h.at[l, top], o_s.at[top], sem.at[1]),
            pltpu.make_async_copy(q_h.at[l, top], q_s.at[top], sem.at[2]),
            pltpu.make_async_copy(kv_h.at[l, wide], kv_s.at[wide], sem.at[3]),
            pltpu.make_async_copy(xs_h.at[l, 1, top], x_s.at[top], sem.at[5]),
            pltpu.make_async_copy(ain_h.at[l], ain, sem.at[6]),
        ]
        copies = [None] + copies

        def weights_in(t):
            return pltpu.make_async_copy(at_h.at[l, t], at_s.at[t], sem.at[8 + t])

        low_spot = (every, pl.ds(384, 128))
        high_spot = (every, pl.ds(0, 384))

        def start():
            for c in copies[1:5]:
                c.start()
            weights_in(0).start()

        def finish():
            out.wait(0, low_spot)
            out.wait(1, high_spot)

        return start, functools.partial(attend_work, rows, copies, weights_in), finish

    def attend_work(rows, copies, weights_in, midway):
        tiles = rows // BLK
        top = pl.ds(0, rows)
        low_spot = (every, pl.ds(384, 128))
        high_spot = (every, pl.ds(0, 384))

        def low(i, at, carry):
            gl_s[at, :] = g_s[at, :].astype(BF)
            return carry

        blocks(rows, low)

        def clear(i, at, carry):
            dkv_s[at, :] = jnp.zeros((BLK, 2 * D), F32)
            return carry

        blocks(rows + 2 * BLK, clear)
        copies[1].wait()
        do_s[top, :] = dot_nt(gl_s[top, :], aout[...]).astype(BF)
        for c in copies[2:5]:
            c.wait()
        for c in copies[5:]:
            c.start()
        midway()

        def tile(t, at, carry):
            near = pl.ds(pl.multiple_of(t * BLK, BLK), 3 * BLK)
            weights_in(t).wait()

            @pl.when(t + 1 < tiles)
            def _():
                weights_in(t + 1).start()

            for p in range(PAIRS):
                lanes = slice(p * 128, (p + 1) * 128)
                vlanes = slice(D + p * 128, D + (p + 1) * 128)
                do = stacked(do_s[at, lanes])
                low = at_s[t, p]
                weights = low.astype(F32)
                da = dot_nt(kv_s[near, vlanes], do)
                delta = jnp.sum(weights * da, axis=0, keepdims=True)
                ds = (weights * (da - delta)).astype(BF)
                dq_s[at, lanes] = unstacked(dot_tn(ds, kv_s[near, lanes])) * HD**-0.5
                dkv_s[near, lanes] = dkv_s[near, lanes] + dot_nn(ds, stacked(q_s[at, lanes]))
                dkv_s[near, vlanes] = dkv_s[near, vlanes] + dot_nn(low, do)
            return carry

        blocks(rows, tile)
        copies[5].wait()

        def turn(i, at, carry):
            inner = pl.ds(pl.multiple_of(i * BLK + BLK, BLK), BLK)
            cos, sin = cos_ref[at, :], sin_ref[at, :]
            for p in range(PAIRS):
                lanes = slice(p * 128, (p + 1) * 128)
                dq = dq_s[at, lanes]
                dk = dkv_s[inner, lanes]
                dp_s[at, lanes] = (dq * cos - swap_halves(dq) * sin).astype(BF)
                dp_s[at, D + p * 128 : D + (p + 1) * 128] = (dk * cos - swap_halves(dk) * sin).astype(BF)
                dp_s[at, 2 * D + p * 128 : 2 * D + (p + 1) * 128] = dkv_s[
                    inner, D + p * 128 : D + (p + 1) * 128
                ].astype(BF)
            xhat, _ = normalise(x_s[at, :])
            a_s[at, :] = (xhat * gain).astype(BF)
            return carry

        blocks(rows, turn)

        dwo = dot_tn(gl_s[top, :], o_s[top, :])
        transposed_out(out, dwo, lambda b: pl.ds(384 + b * 64, 64))
        out.send(0, low_spot)
        for half in range(2):
            dwi = dot_tn(dp_s[top, half * 768 : (half + 1) * 768], a_s[top, :])
            for q in range(2):
                for b in range(2):
                    pair = [
                        dwi[q * 384 + r * 192 : q * 384 + (r + 1) * 192, b * LANES : (b + 1) * LANES] for r in range(2)
                    ]
                    out.put((2 * half + q, pl.ds(b * 192, 192), slice(None)), pair)
        out.send(1, high_spot)
        copies[6].wait()
        da_s[top, :] = dot_nt(dp_s[top, :], ain[...])

        def last(i, at, carry):
            xhat, inv = normalise(x_s[at, :])
            da = da_s[at, :]
            g_s[at, :] = g_s[at, :] + norm_back(da, xhat, inv, gain)
            return carry + fold(da * xhat)

        small_ref[0:1, :] = total(blocks(rows, last, jnp.zeros((8, D), F32)))

    return run


def attend_spec(l, cos, sin, gains, xs, q, kv, at, o, ain, aout):
    vm = pltpu.VMEM
    return (
        functools.partial(attend_part, l),
        [(v, VMEM) for v in (cos, sin, gains)] + [(v, ANY) for v in (xs, q, kv, at, o, ain, aout)],
        [
            (struct((4, 512, LANES), BF), ANY),
            (struct((4, 512, LANES), BF), ANY),
            (struct((8, D), F32), VMEM),
        ],
        [
            vm((CAP, D), F32), vm((CAP, D), BF), vm((CAP + 2 * BLK, 2 * D), BF),
            vm((CAP // BLK, PAIRS, 3 * BLK, 2 * BLK), BF), vm((CAP, D), BF), vm((D, 3 * D), BF), vm((D, D), BF),
            vm((CAP, D), BF), vm((CAP, D), BF), vm((CAP, D), BF), vm((CAP, D), F32),
            vm((CAP + 2 * BLK, 2 * D), F32), vm((CAP, 3 * D), BF), vm((CAP, D), F32),
            vm((2, 4, 512, LANES), BF),
            pltpu.SemaphoreType.DMA((8 + CAP // BLK,)), pltpu.SemaphoreType.DMA((4,)),
        ],
        16 * 640 * D * D,
    )


def run_parts(name, n, core, g, specs, deps):
    in_counts = [len(spec[1]) for spec in specs]
    out_counts = [len(spec[2]) for spec in specs]
    scratch_counts = [len(spec[3]) for spec in specs]

    def taken(refs, counts):
        pieces, off = [], 0
        for count in counts:
            pieces.append(refs[off : off + count])
            off += count
        return pieces

    def body(n_ref, core_ref, g_h, *refs):
        ins, refs = refs[: sum(in_counts)], refs[sum(in_counts) :]
        out_h, *outs = refs[: 1 + sum(out_counts)]
        g_s, g_sem, *scratch = refs[1 + sum(out_counts) :]
        parts = [
            spec[0](core_ref, g_s, *piece)
            for spec, *piece in zip(
                specs, taken(ins, in_counts), taken(outs, out_counts), taken(scratch, scratch_counts)
            )
        ]

        def run(rows):
            top = pl.ds(0, rows)
            steps = [part(rows) for part in parts]
            g_in = pltpu.make_async_copy(g_h.at[top], g_s.at[top], g_sem)
            g_in.start()
            steps[0][0]()
            g_in.wait()
            for i, (_, main, _) in enumerate(steps):
                main(steps[i + 1][0] if i + 1 < len(steps) else lambda: None)
            g_out = pltpu.make_async_copy(g_s.at[top], out_h.at[top], g_sem)
            g_out.start()
            for _, _, finish in steps:
                finish()
            g_out.wait()

        by_rows(n_ref, run)

    outs = [(struct((CAP, D), F32), ANY)] + [out for spec in specs for out in spec[2]]
    g, *rest = call(
        body,
        [SMEM, SMEM, ANY] + [where for spec in specs for _, where in spec[1]],
        outs,
        [pltpu.VMEM((CAP, D), F32), pltpu.SemaphoreType.DMA] + [v for spec in specs for v in spec[3]],
        (n, core, g, *(v for spec in specs for v, _ in spec[1])),
        flops=sum(spec[4] for spec in specs),
        moved=16 * 2**20,
        name=name,
        deps=deps,
    )
    return g, taken(rest, out_counts)


def add(*terms):
    acc = terms[0].astype(F32)
    for term in terms[1:]:
        acc = acc + term.astype(F32)
    return acc.astype(BF)


def spot_of(place_ref):
    x, y, core = place_ref[0], place_ref[1], place_ref[3]
    even = core == 0
    return jnp.where(even, x, y), jnp.where(even, y, x), 1 + core, 2 - core


def split_first_body(sizes, place_ref, *refs):
    count = len(sizes)
    keeps, gots = refs[:count], refs[count : 2 * count]
    kept, sent = refs[2 * count :]
    first, _, by_first, by_second = spot_of(place_ref)
    off = 0
    for keep, got, n in zip(keeps, gots, sizes):
        at = pl.ds(off, n)

        def one(z, carry, keep=keep, got=got, at=at):
            for j in range(2):
                own = first * by_first + j * by_second
                other = (1 - first) * by_first + j * by_second
                kept[z, j, at] = add(keep[z, own], got[z, own])
                sent[z, j, at] = add(keep[z, other], got[z, other])
            return carry

        lax.fori_loop(0, 4, one, jnp.int32(0))
        off += n


def split_second_body(place_ref, keep, got, kept, sent):
    _, second, _, _ = spot_of(place_ref)

    def one(z, carry):
        kept[z] = add(keep[z, second], got[z, second])
        sent[z] = add(keep[z, 1 - second], got[z, 1 - second])
        return carry

    lax.fori_loop(0, 4, one, jnp.int32(0))


def split_z_body(plan, place_ref, *refs):
    ins, outs = refs[:-4], refs[-4:]
    z = place_ref[2]
    for k, ref in enumerate(outs):
        at = lax.rem(z + k, 4)
        off = used = 0
        for count, n in plan:
            terms = [r[at] for r in ins[used : used + count]]
            ref[pl.ds(off, n), :] = add(*terms) if count > 1 else terms[0]
            used += count
            off += n


def row_pairs(bit):
    return [(i, i ^ bit) for i in range(4)]


def along(axis):
    return [(r * 8 + t, (r ^ (1 << ((t + axis) % 2))) * 8 + t) for r in range(4) for t in range(8)]


def sum_cores_body(sizes, *refs):
    count = len(sizes)
    keeps, gots, out = refs[:count], refs[count : 2 * count], refs[2 * count]
    off = 0
    for keep, got, n in zip(keeps, gots, sizes):
        at = pl.ds(off, n)

        def one(z, carry, keep=keep, got=got, at=at):
            for j in range(4):
                out[j, z, at] = add(keep[z, j], got[z, j])
            return carry

        lax.fori_loop(0, 4, one, jnp.int32(0))
        off += n


class Group:
    def __init__(self, spot, members):
        self.spot = spot
        self.keeps = [keep for _, keep, _ in members]
        self.sizes = [keep.shape[1] // 4 for keep in self.keeps]
        self.names = [name for name, _, _ in members]
        self.n = sum(self.sizes)
        self.bytes = 16 * self.n * LANES * 2
        self.gots = [got for _, _, got in members]

    def cores(self):
        shaped = lambda v: v.reshape(4, 4, v.shape[1] // 4, LANES)
        return (*map(shaped, self.keeps), *map(shaped, self.gots))

    def offload(self, deps):
        both = call(
            functools.partial(sum_cores_body, self.sizes),
            [VMEM] * (2 * len(self.sizes)),
            [(struct((4, 4, self.n, LANES), BF), VMEM)],
            [],
            self.cores(),
            moved=3 * self.bytes,
            name="sum_cores",
            vmem=VMEM_SMALL,
            deps=deps,
        )[0]
        part = lax.psum_scatter(both, "rows", scatter_dimension=0, tiled=True)
        self.terms = [part.reshape(4, self.n, LANES)]
        return [both]

    def first(self, deps, work=0):
        self.kept, sent = call(
            functools.partial(split_first_body, self.sizes),
            [SMEM] + [VMEM] * (2 * len(self.sizes)),
            [(struct((4, 2, self.n, LANES), BF), VMEM)] * 2,
            [],
            (self.spot, *self.cores()),
            moved=3 * self.bytes,
            name="split_first",
            vmem=VMEM_SMALL,
            flops=work,
            deps=deps,
        )
        self.got = lax.ppermute(sent, ("rows", "tm"), along(0))
        return [self.kept]

    def second(self, deps, work=0):
        self.kept, sent = call(
            split_second_body,
            [SMEM] + [VMEM] * 2,
            [(struct((4, self.n, LANES), BF), VMEM)] * 2,
            [],
            (self.spot, self.kept, self.got),
            moved=3 * self.bytes // 2,
            name="split_second",
            vmem=VMEM_SMALL,
            flops=work,
            deps=deps,
        )
        self.terms = [self.kept, lax.ppermute(sent, ("rows", "tm"), along(1))]
        return [self.kept]


def merge_body(*refs):
    *ins, out = refs
    off = 0
    for ref in ins:
        n = ref.shape[1]
        out[:, pl.ds(off, n), :] = ref[...]
        off += n


def offloaded_rest(groups, deps):
    n = sum(group.n for group in groups)
    part = call(
        merge_body,
        [VMEM] * len(groups),
        [(struct((4, n, LANES), BF), VMEM)],
        [],
        [group.terms[0] for group in groups],
        moved=16 * n * LANES,
        name="merge",
        vmem=VMEM_SMALL,
        deps=deps,
    )[0]
    mine = lax.psum_scatter(
        part, "tm", scatter_dimension=0, tiled=True, axis_index_groups=[[0, 2, 4, 6], [1, 3, 5, 7]]
    )
    mine = mine.reshape(part.shape[1:])
    return mine, lax.all_gather(mine, "rows", axis=0, tiled=True)


def along_z(spot, groups, deps, work=0):
    ins = [term for group in groups for term in group.terms]
    n = sum(group.n for group in groups)
    own, *others = call(
        functools.partial(split_z_body, [(len(group.terms), group.n) for group in groups]),
        [SMEM] + [VMEM] * len(ins),
        [(struct((n, LANES), BF), VMEM)] * 4,
        [],
        (spot, *ins),
        moved=16 * n * LANES * 2,
        name="split_z",
        vmem=VMEM_SMALL,
        flops=work,
        deps=deps,
    )
    return [own] + [
        lax.ppermute(v, "tm", [(i, (i + 2 * k) % 8) for i in range(8)]) for k, v in zip((1, 2, 3), others)
    ]


def join_body(plan, *refs):
    *ins, out = refs
    off = at = 0
    for count, n in plan:
        out[pl.ds(at, n), :] = add(*(ref[...] for ref in ins[off : off + count])) if count > 1 else ins[off][...]
        off += count
        at += n


def gathered(lists, deps):
    ins = [term for terms in lists for term in terms]
    plan = [(len(terms), terms[0].shape[0]) for terms in lists]
    n = sum(rows for _, rows in plan)
    mine = call(
        functools.partial(join_body, plan),
        [VMEM] * len(ins),
        [(struct((n, LANES), BF), VMEM)],
        [],
        ins,
        moved=6 * n * LANES,
        name="join",
        vmem=VMEM_SMALL,
        deps=deps,
    )[0]
    return [mine] + [lax.ppermute(mine, "rows", row_pairs(bit)) for bit in (1, 2, 3)]


def finish_body(members, by_bit, me_ref, *refs):
    count = 4 if by_bit else 1
    chunks = refs[:count]
    fin_h, fout_h, ain_h, aout_h, pin_h, pout_h, small_h = refs[-13:-6]
    whole, fout, ain, pin, narrow, sem = refs[-6:]
    me = me_ref[0]
    rows = sum(n for _, _, n in members)
    off = 0
    waits = []
    for i, (l, name, n) in enumerate(members):
        for j in range(4):
            if by_bit:
                owner = pl.multiple_of(jnp.bitwise_xor(me, j) * n, n)
                whole[i, pl.ds(owner, n), :] = chunks[j][pl.ds(off, n), :].astype(F32)
            else:
                whole[i, pl.ds(j * n, n), :] = chunks[0][pl.ds(j * rows + off, n), :].astype(F32)
        off += n
        if name in ("f0", "f1", "f0in", "f0out"):
            k = int(name == "f1")
            jobs = []
            if name != "f0out":
                jobs.append((whole.at[i, pl.ds(0, D)], fin_h.at[l, k]))
            if name != "f0in":
                base = 0 if name == "f0out" else D
                for b in range(FF // LANES):
                    fout[i, :, pl.ds(b * LANES, LANES)] = whole[i, pl.ds(base + b * 64, 64), :]
                jobs.append((fout.at[i], fout_h.at[l, k]))
            else:
                jobs.append((whole.at[i, pl.ds(D, SMALL_ROWS // 4)], small_h))
        elif name == "c":
            pin[i, pl.ds(0, 256), :] = whole[i, pl.ds(0, 256), 0:128]
            pin[i, pl.ds(256, 256), :] = whole[i, pl.ds(0, 256), 128:256]
            for b in range(2):
                narrow[i, :, pl.ds(b * LANES, LANES)] = whole[i, pl.ds(256 + b * 64, 64), :]
            jobs = [(pin.at[i], pin_h.at[l]), (narrow.at[i], pout_h.at[l])]
        else:
            for b in range(2):
                ain[i, :, pl.ds(b * LANES, LANES)] = whole[i, pl.ds(b * 192, 192), :]
                narrow[i, :, pl.ds(b * LANES, LANES)] = whole[i, pl.ds(384 + b * 64, 64), :]
            jobs = [(ain.at[i], ain_h.at[l]), (narrow.at[i], aout_h.at[l])]
        for j, (src, dst) in enumerate(jobs):
            c = pltpu.make_async_copy(src, dst, sem.at[3 * i + j])
            c.start()
            waits.append(c)
    for c in waits:
        c.wait()


def finish(layers, me, groups, chunks, before, deps=()):
    members = [(*name, size) for group in groups for name, size in zip(group.names, group.sizes)]
    count = len(members)
    shapes = [
        (layers, 2, D, FF // 8), (layers, 2, D // 8, FF), (layers, 3 * D // 8, D), (layers, D // 8, D),
        (layers, D, 2 * D // 8), (layers, D // 8, D), (SMALL_ROWS // 4, LANES),
    ]
    vm = pltpu.VMEM

    def body(*refs):
        finish_body(members, len(chunks) == 4, *refs)

    return pl.pallas_call(
        body,
        out_shape=[struct(shape, F32) for shape in shapes],
        in_specs=[SMEM] + [VMEM] * len(chunks) + [ANY] * (len(before) + len(deps)),
        out_specs=[ANY] * 7,
        scratch_shapes=[
            vm((count, 1024 + SMALL_ROWS, LANES), F32), vm((count, 64, FF), F32), vm((count, 192, D), F32),
            vm((count, D, 128), F32), vm((count, 64, D), F32), pltpu.SemaphoreType.DMA((3 * count,)),
        ],
        input_output_aliases={1 + len(chunks) + i: i for i in range(len(before))},
        compiler_params=pltpu.CompilerParams(vmem_limit_bytes=VMEM_LIMIT),
        name="finish",
    )(me, *chunks, *before, *deps)


def per_device(
    frames, segment_ids, norm_gains, feed_in, feed_out, attend_in, attend_out, point_in, depthwise, stat_mean,
    stat_var, batch_scale, batch_shift, point_out, cotangent,
):
    batches, row_count, frame_count, model_dim = frames.shape
    layers = norm_gains.shape[0]
    tm_size = lax.axis_size("tm")
    rows_size = lax.axis_size("rows")
    tm = lax.axis_index("tm")
    row = lax.axis_index("rows")
    fast = tm_size == 8 and rows_size == 4
    half = batches // 2

    ids = segment_ids[:, 0] + 1
    id_rows = jnp.broadcast_to(ids.reshape(1, -1).astype(BF), (16, batches * frame_count))
    parts_of = lambda v, odd: v.reshape(half, 2, frame_count, model_dim)[:, odd].reshape(-1, model_dim)
    message = lambda odd: jnp.concatenate([parts_of(frames, odd), parts_of(cotangent, odd), id_rows], axis=0)
    above = shifted(message(0), "tm", -1)
    below = shifted(message(1), "tm", 1)
    flat = lambda v: v.reshape(batches * frame_count, model_dim)
    x0, g, chooser, cos, sin, kb, kr, n = pack(ids.astype(F32), flat(frames), flat(cotangent), below, above)
    small = (norm_gains, depthwise, stat_mean, stat_var, batch_scale, batch_shift)
    mats = (feed_in, feed_out, attend_in, attend_out, point_in, point_out)
    act, xs, hs, q, kv, at, o, u, z = forward(n, x0, cos, sin, kb, kr, small, mats)

    def unpacked(packed):
        spread = lax.dot_general(
            chooser, packed, (((0,), (0,)), ((), ())), preferred_element_type=F32
        ).astype(BF).reshape(half, 2, 2, frame_count, model_dim)
        from_below = shifted(spread[:, 0, 1], "tm", 1)
        from_above = shifted(spread[:, 1, 0], "tm", -1)
        even = spread[:, 0, 0] + from_below
        odd = spread[:, 1, 1] + from_above
        return jnp.stack([even, odd], axis=1).reshape(batches, 1, frame_count, model_dim)

    activations = unpacked(act)

    if fast:
        spot = jnp.stack([row % 2, row // 2, tm // 2, tm % 2]).astype(jnp.int32)
        core = (tm % 2).astype(jnp.int32).reshape(1)
    else:
        spot = None
        core = jnp.zeros((1,), jnp.int32)

    members = {}
    smalls = {}
    parts = {
        "f1": lambda l: feed_spec(l, 1, "all", (), norm_gains, xs, hs, feed_in, feed_out),
        "c": lambda l: conv_spec(l, kb, small, xs, u, z, point_in, point_out),
        "a": lambda l: attend_spec(l, cos, sin, norm_gains, xs, q, kv, at, o, attend_in, attend_out),
        "f0": lambda l: feed_spec(l, 0, "all", (), norm_gains, xs, hs, feed_in, feed_out),
        "f0out": lambda l: feed_spec(l, 0, "out", (), norm_gains, xs, hs, feed_in, feed_out),
        "f0in": lambda l, rest: feed_spec(l, 0, "in", rest, norm_gains, xs, hs, feed_in, feed_out),
    }
    order = [(l, name) for l in range(layers) for name in ("f0", "a", "c", "f1")]

    def back(l, *names, deps=(), **more):
        nonlocal g
        specs = [parts[name](l, **more) for name in names]
        g, outs = run_parts(f"back_{l}_{'_'.join(names)}", n, core, g, specs, deps)
        for name, (kept, sent, small_grads) in zip(names, outs):
            smalls[l, name] = small_grads
            members[l, name] = ((l, name), kept, sent)

    crossed = {}

    def begin(l, name):
        crossed[l, name] = lax.ppermute(members[l, name][2], "tm", [(i, i ^ 1) for i in range(8)])

    def group(*names):
        for name in names:
            if name not in crossed:
                begin(*name)
        return Group(spot, [(name, members[name][1], crossed[name]) for name in names])

    if fast:
        me = (2 * spot[1] + spot[0]).reshape(1)
        back(1, "f1", "c")
        one = group((1, "f1"), (1, "c"))
        made = one.offload([])
        back(1, "a", "f0", deps=made)
        two = group((1, "a"), (1, "f0"))
        made = two.offload([])
        back(0, "f1", deps=made + one.terms)
        begin(0, "f1")
        back(0, "c")
        begin(0, "c")
        three = group((0, "f1"))
        made = three.first([g])
        mine_early, all_early = offloaded_rest([one, two], made)
        back(0, "a", "f0out", deps=made + two.terms)
        four = group((0, "c"), (0, "a"), (0, "f0out"))
        made = three.second([g])
        made += four.first(made)
        back(0, "f0in", deps=made + [mine_early], rest=[smalls[name] for name in order[1:]])
        five = group((0, "f0in"))
        z_three = along_z(spot, [three], [g], TAIL_WORK)
        made = five.first(z_three[:1])
        made = four.second(made)
        z_four = along_z(spot, [four], made)
        made = five.second(z_four[:1])
        outs = finish(layers, me, [one, two], [all_early], [], made)
        chunks_mid = gathered([z_three, z_four], outs[:1])
        z_five = along_z(spot, [five], chunks_mid[:1])
        outs = finish(layers, me, [three, four], chunks_mid, outs)
        chunks_late = gathered([z_five], outs[:1])
        *mats_out, small_out = finish(layers, me, [five], chunks_late, outs)
        mats_out = [
            v.swapaxes(-1, -2) if turned else v for v, turned in zip(mats_out, (False, True, True, True, False, True))
        ]
        lines = small_out.reshape(-1, 4, 64).swapaxes(0, 1).reshape(-1, 64)
        starts = {name: 0 for name in order}
        at_row = 0
        smalls[0, "f0"] = smalls[0, "f0in"]
        for name in order:
            starts[name] = at_row
            at_row += smalls[name].shape[0]
        pieces = lambda name, first, count: [
            lines[starts[l, name] + first : starts[l, name] + first + count] for l in range(layers)
        ]
    else:
        for l in reversed(range(layers)):
            back(l, "f1", "c")
            back(l, "a", "f0")
        pieces = None
    filled = lax.broadcasted_iota(jnp.int32, g.shape, 0) < n[0]
    frames_grad = unpacked(jnp.where(filled, g, 0.0).astype(BF))

    if not fast:
        mats_out, lines_of = general_sums(layers, members, smalls, order)
        pieces = lambda name, first, count: [lines_of[l, name][first : first + count] for l in range(layers)]
    gains_out = jnp.stack(
        [
            jnp.concatenate(rows, axis=0)
            for rows in zip(
                pieces("f0", 0, 1), pieces("a", 0, 1), pieces("c", 0, 1), pieces("f1", 0, 1), pieces("f1", 1, 1)
            )
        ]
    )
    fin, fout, ain, aout, pin, pout = mats_out
    return (
        activations,
        frames_grad,
        gains_out,
        fin,
        fout,
        ain,
        aout,
        pin,
        jnp.stack(pieces("c", 8, KERNEL)),
        jnp.concatenate(pieces("c", 1, 1), axis=0),
        jnp.concatenate(pieces("c", 2, 1), axis=0),
        pout,
    )


def general_sums(layers, members, smalls, order):
    def natural(l, name):
        _, even, odd = members[l, name]
        return jnp.stack([even, odd], axis=1).astype(F32).reshape(8, -1, LANES)

    def wide(v, count):
        r = v.shape[1] // count
        return jnp.swapaxes(v.reshape(8, count, r, LANES), 1, 2).reshape(8 * r, count * LANES)

    def over_all(v):
        v = lax.psum_scatter(v, "tm", scatter_dimension=v.ndim - 1, tiled=True)
        return lax.psum(v, "rows")

    fin, fout, ain, aout, pin, pout = [], [], [], [], [], []
    for l in range(layers):
        f = [natural(l, "f0"), natural(l, "f1")]
        fin.append(jnp.stack([jnp.moveaxis(v[:, :D], 0, 1).reshape(D, FF) for v in f]))
        fout.append(jnp.stack([wide(v[:, D:], FF // LANES).T for v in f]))
        v = natural(l, "a")
        ain.append(wide(v[:, :384], 2).T)
        aout.append(wide(v[:, 384:], 2).T)
        v = natural(l, "c")
        top = jnp.concatenate([v[:, :256, :128], v[:, :256, 128:]], axis=1)
        pin.append(jnp.moveaxis(top, 0, 1).reshape(D, 2 * D))
        pout.append(wide(v[:, 256:], 2).T)
    mats_out = [over_all(jnp.stack(v)) for v in (fin, fout, ain, aout, pin, pout)]
    small_all = over_all(jnp.concatenate([smalls[name] for name in order], axis=0))
    lines_of = {}
    at = 0
    for name in order:
        rows = smalls[name].shape[0]
        lines_of[name] = small_all[at : at + rows]
        at += rows
    return mats_out, lines_of


def solution(mesh):
    rep = P()
    in_specs = (
        P(None, "rows", "tm", None), P(None, "rows", "tm"), rep, rep, rep, rep, rep, rep, rep, rep, rep, rep, rep, rep,
        P(None, "rows", "tm", None),
    )
    out_specs = (
        P(None, "rows", "tm", None), P(None, "rows", "tm", None), P(None, None, "tm"), P(None, None, None, "tm"),
        P(None, None, None, "tm"), P(None, None, "tm"), P(None, None, "tm"), P(None, None, "tm"),
        P(None, None, "tm"), P(None, "tm"), P(None, "tm"), P(None, None, "tm"),
    )
    return jax.shard_map(per_device, mesh=mesh, in_specs=in_specs, out_specs=out_specs, check_vma=False)
```

```python
import functools

import jax
import jax.numpy as jnp
import numpy as np
from jax import lax
from jax.experimental import pallas as pl
from jax.experimental.pallas import tpu as pltpu
from jax.sharding import PartitionSpec as P

HD = 64
KERNEL = 9
HALO = 4
EPSILON = 1e-05
MASKED = -1e30
BF = jnp.bfloat16
F32 = jnp.float32
D = 512
FF = 2048
BLK = 128
ROW_CHOICES = (640, 1024)
CAP = ROW_CHOICES[-1]
LANES = 256
SMALL_ROWS = 128
TAIL_WORK = 3e10
PAIRS = D // 128
VMEM_LIMIT = 60 * 2**20
VMEM_SMALL = 24 * 2**20
ANY = pl.BlockSpec(memory_space=pl.ANY)
VMEM = pl.BlockSpec(memory_space=pltpu.VMEM)
SMEM = pl.BlockSpec(memory_space=pltpu.SMEM)


def shifted(array, axis, by):
    size = lax.axis_size(axis)
    pairs = [(i, i + by) for i in range(size) if 0 <= i + by < size]
    return lax.ppermute(array, axis, pairs)


def struct(shape, dtype):
    return jax.ShapeDtypeStruct(shape, dtype)


def call(body, ins, outs, scratch, args, flops=0, moved=0, name="kernel", deps=(), vmem=VMEM_LIMIT):
    count = len(ins)

    def inner(*refs):
        body(*refs[:count], *refs[count + len(deps) :])

    return pl.pallas_call(
        inner,
        out_shape=[s for s, _ in outs],
        in_specs=list(ins) + [ANY] * len(deps),
        out_specs=[b for _, b in outs],
        scratch_shapes=scratch,
        compiler_params=pltpu.CompilerParams(vmem_limit_bytes=vmem),
        cost_estimate=pl.CostEstimate(flops=int(flops), bytes_accessed=int(moved), transcendentals=0),
        name=name,
    )(*args, *deps)


def dot_nn(a, b):
    return jnp.dot(a, b, preferred_element_type=F32)


def dot_nt(a, b):
    return lax.dot_general(a, b, (((1,), (1,)), ((), ())), preferred_element_type=F32)


def dot_tn(a, b):
    return lax.dot_general(a, b, (((0,), (0,)), ((), ())), preferred_element_type=F32)


def sigmoid(v):
    return 0.5 + 0.5 * jnp.tanh(0.5 * v)


def normalise(x):
    c = x - jnp.mean(x, axis=-1, keepdims=True)
    inv = lax.rsqrt(jnp.mean(c * c, axis=-1, keepdims=True) + EPSILON)
    return c * inv, inv


def norm_back(grad, xhat, inv, gain):
    w = grad * gain
    return inv * (
        w - jnp.mean(w, axis=-1, keepdims=True) - xhat * jnp.mean(w * xhat, axis=-1, keepdims=True)
    )


def fold(v):
    return jnp.sum(v.reshape(v.shape[0] // 8, 8, v.shape[1]), axis=0)


def total(v):
    return jnp.sum(v, axis=0, keepdims=True)


def by_rows(n_ref, body):
    low = 0
    for rows in ROW_CHOICES:
        n = n_ref[0]
        cond = n > low
        if rows != CAP:
            cond = cond & (n <= rows)

        @pl.when(cond)
        def _(rows=rows):
            body(rows)

        low = rows


def blocks(rows, step, init=None, size=128):
    def wrapped(i, carry):
        at = pl.ds(pl.multiple_of(i * size, size), size)
        return step(i, at, carry)

    start = init if init is not None else jnp.int32(0)
    return lax.fori_loop(0, rows // size, wrapped, start, unroll=rows == ROW_CHOICES[0])


def each(count, rows, step):
    if rows == ROW_CHOICES[0]:
        for i in range(count):
            step(i)
    else:

        def wrapped(i, carry):
            step(i)
            return carry

        lax.fori_loop(0, count, wrapped, jnp.int32(0))


def cut(i, size):
    return pl.ds(i * size, size) if isinstance(i, int) else pl.ds(pl.multiple_of(i * size, size), size)


def rope_tables():
    half = HD // 2
    freq = np.power(np.float32(10000.0), -(np.arange(half).astype(np.float32) / np.float32(half)))
    angle = np.arange(BLK).astype(np.float32)[:, None] * freq.astype(np.float32)[None, :]
    cos = np.cos(angle.astype(np.float64))
    sin = np.sin(angle.astype(np.float64))
    full = (np.concatenate([cos] * 4, axis=1), np.concatenate([-sin, sin] * 2, axis=1))
    parts = []
    for table in full:
        rest = table
        for _ in range(3):
            piece = rest.astype(jnp.bfloat16)
            parts.append(piece)
            rest = rest - piece.astype(np.float64)
    return np.stack(parts)


def pack_body(
    ids_ref, frames_ref, cot_ref, below_ref, above_ref, tab_ref,
    x_ref, g_ref, p_ref, cos_ref, sin_ref, kb_ref, kr_ref, n_ref,
    keep_s, key_s, dest_s, pos_s, win_s, cot_s,
):
    batches = ids_ref.shape[0]
    half = batches // 2
    shown = (8, BLK)
    below_ids = below_ref[pl.ds(4 * BLK, 16), :].astype(F32)[0:1]
    above_ids = above_ref[pl.ds(4 * BLK, 16), :].astype(F32)[0:1]
    for m in range(batches):
        own = ids_ref[m : m + 1, :]
        below = below_ids[:, m * BLK : (m + 1) * BLK]
        above = above_ids[:, m * BLK : (m + 1) * BLK]
        i = m // 2
        mine = pl.ds(m * BLK, BLK)
        theirs = (pl.ds(i * BLK, BLK), pl.ds((half + i) * BLK, BLK))
        if m % 2 == 0:
            pieces = ((own, own != below[:, BLK - 1 : BLK]), (above, above == own[:, BLK - 1 : BLK]))
            frames = ((frames_ref, mine, cot_ref, mine), (above_ref, theirs[0], above_ref, theirs[1]))
        else:
            pieces = ((below, below == own[:, 0:1]), (own, own != above[:, 0:1]))
            frames = ((below_ref, theirs[0], below_ref, theirs[1]), (frames_ref, mine, cot_ref, mine))
        for j in range(2):
            at = pl.ds((2 * m + j) * BLK, BLK)
            key_s[:, at] = jnp.broadcast_to(pieces[j][0] + 4096.0 * m, shown)
            keep_s[:, at] = jnp.broadcast_to(jnp.where(pieces[j][1], 1.0, 0.0), shown)
            src, rows, cot, cot_rows = frames[j]
            win_s[at, :] = src[rows, :]
            cot_s[at, :] = cot[cot_rows, :]
    square = (BLK, BLK)
    earlier = lax.broadcasted_iota(jnp.int32, square, 0) < lax.broadcasted_iota(jnp.int32, square, 1)
    ramp = earlier.astype(F32).astype(BF)
    before = jnp.zeros((8, 1), F32)
    for j in range(2 * batches):
        at = pl.ds(j * BLK, BLK)
        keep = keep_s[:, at]
        dest_s[:, at] = jnp.where(keep > 0.5, before + dot_nn(keep.astype(BF), ramp), -1.0)
        before = before + jnp.sum(keep, axis=1, keepdims=True)
    n = (jnp.sum(before) * 0.125 + 0.5).astype(jnp.int32)
    n_ref[0] = n
    for m in range(batches):
        first, second = pl.ds(2 * m * BLK, BLK), pl.ds((2 * m + 1) * BLK, BLK)
        cols = [jnp.broadcast_to(key_s[0:1, at], square).T for at in (first, second)]
        count = lambda mask: jnp.broadcast_to(jnp.sum(jnp.where(mask, 1.0, 0.0), axis=0, keepdims=True), shown)
        pos_s[:, first] = count((cols[0] == key_s[0:1, first]) & earlier)
        pos_s[:, second] = count(cols[0] == key_s[0:1, second]) + count((cols[1] == key_s[0:1, second]) & earlier)
    kr_ref[...] = jnp.full(kr_ref.shape, -1.0, F32)
    rows_all = 2 * batches * BLK

    def step(i, at):
        row = (lax.broadcasted_iota(jnp.int32, (BLK, rows_all), 0) + i * BLK).astype(F32)
        pick = jnp.where(dest_s[0:1, :] == row, 1.0, 0.0)
        p = pick.astype(BF)
        p_ref[at, :] = p
        x_ref[at, :] = dot_nn(p, win_s[...])
        g_ref[at, :] = dot_nn(p, cot_s[...])
        key = jnp.broadcast_to(jnp.sum(pick * key_s[0:1, :], axis=1, keepdims=True), square)
        kb_ref[at, :] = key
        kr_ref[:, pl.ds(i * BLK + BLK, BLK)] = key.T[0:8]
        pos = jnp.sum(pick * pos_s[0:1, :], axis=1, keepdims=True)
        hot = (lax.broadcasted_iota(jnp.int32, square, 1).astype(F32) == pos).astype(F32).astype(BF)
        cos_ref[at, :] = dot_nn(hot, tab_ref[0]) + dot_nn(hot, tab_ref[1]) + dot_nn(hot, tab_ref[2])
        sin_ref[at, :] = dot_nn(hot, tab_ref[3]) + dot_nn(hot, tab_ref[4]) + dot_nn(hot, tab_ref[5])

    for i in range(rows_all // BLK):
        at = pl.ds(i * BLK, BLK)
        if i * BLK < ROW_CHOICES[0]:
            step(i, at)
        else:

            @pl.when(n > ROW_CHOICES[0])
            def _(i=i, at=at):
                step(i, at)

            @pl.when(n <= ROW_CHOICES[0])
            def _(at=at):
                p_ref[at, :] = jnp.zeros((BLK, rows_all), BF)


def pack(ids, frames, cotangent, below, above):
    vm = pltpu.VMEM
    return call(
        pack_body,
        [VMEM] * 6,
        [
            (struct((CAP, D), F32), VMEM),
            (struct((CAP, D), F32), VMEM),
            (struct((CAP, CAP), BF), VMEM),
            (struct((CAP, 128), F32), VMEM),
            (struct((CAP, 128), F32), VMEM),
            (struct((CAP, 128), F32), VMEM),
            (struct((8, CAP + 2 * BLK), F32), VMEM),
            (struct((1,), jnp.int32), SMEM),
        ],
        [vm((8, CAP), F32), vm((8, CAP), F32), vm((8, CAP), F32), vm((8, CAP), F32), vm((CAP, D), BF), vm((CAP, D), BF)],
        (ids, frames, cotangent, below, above, jnp.asarray(rope_tables(), dtype=BF)),
        flops=4 * CAP * CAP * D,
        moved=12 * 2**20,
        name="pack",
    )


def lane_low(shape):
    return lax.broadcasted_iota(jnp.int32, shape, 1) % HD < HD // 2


def swap_halves(v):
    return jnp.where(lane_low(v.shape), pltpu.roll(v, 128 - HD // 2, 1), pltpu.roll(v, HD // 2, 1))


def stacked(v):
    first = lax.broadcasted_iota(jnp.int32, v.shape, 1) < HD
    zero = jnp.zeros_like(v)
    return jnp.concatenate([jnp.where(first, v, zero), jnp.where(first, zero, v)], axis=0)


def unstacked(v):
    half = v.shape[0] // 2
    first = lax.broadcasted_iota(jnp.int32, (half, 128), 1) < HD
    return jnp.where(first, v[:half], v[half:])


def norm_into(x_ref, gain, a_ref, rows):
    def step(i, at, carry):
        xhat, _ = normalise(x_ref[at, :])
        a_ref[at, :] = (xhat * gain).astype(BF)
        return carry

    blocks(rows, step)


def forward_body(
    n_ref, x0_ref, cos_ref, sin_ref, kb_ref, kr_ref, gains_ref, taps_ref, mean_ref, var_ref, scale_ref, shift_ref,
    fin_h, fout_h, ain_h, aout_h, pin_h, pout_h,
    act_ref, xs_h, hs_h, q_h, kv_h, at_h, o_h, u_h, z_h,
    fin, fout, ain, aout, pin, pout, xb, hb, qb, kvb, ab, ob, ub, zb, a_s, gp, kp, w_sem, s_sem,
):
    layers = gains_ref.shape[0]
    weights = [
        (fin_h, (0,), fin.at[0]), (fout_h, (0,), fout.at[0]), (ain_h, (), ain), (aout_h, (), aout),
        (pin_h, (), pin), (pout_h, (), pout), (fin_h, (1,), fin.at[1]), (fout_h, (1,), fout.at[1]),
    ]

    def weight_copy(i, l):
        src, sub, dst = weights[i]
        return pltpu.make_async_copy(src.at[(l,) + sub], dst, w_sem.at[i])

    for i in (0, 1):
        weight_copy(i, 0).start()

    def run(rows):
        tiles = rows // BLK
        top = pl.ds(0, rows)
        saves = [(xb.at[i, top], lambda l, i=i: xs_h.at[l, i, top]) for i in range(5)]
        saves += [(hb.at[k, top], lambda l, k=k: hs_h.at[l, k, top]) for k in range(2)]
        saves += [
            (qb.at[top], lambda l: q_h.at[l, top]),
            (kvb.at[pl.ds(0, rows + 2 * BLK)], lambda l: kv_h.at[l, pl.ds(0, rows + 2 * BLK)]),
            (ab.at[pl.ds(0, tiles)], lambda l: at_h.at[l, pl.ds(0, tiles)]),
            (ob.at[top], lambda l: o_h.at[l, top]),
            (ub.at[top], lambda l: u_h.at[l, top]),
            (zb.at[top], lambda l: z_h.at[l, top]),
        ]

        def save(i, l):
            src, dst = saves[i]
            return pltpu.make_async_copy(src, dst(l), s_sem.at[i])

        def settle(i, l):
            @pl.when(l > 0)
            def _():
                save(i, l - 1).wait()

        def use(i, l):
            weight_copy(i, l).wait()

        def next_weight(i, l):
            @pl.when(l + 1 < layers)
            def _():
                weight_copy(i, l + 1).start()

        kvb[pl.ds(0, BLK), :] = jnp.zeros((BLK, 2 * D), BF)
        kvb[pl.ds(rows + BLK, BLK), :] = jnp.zeros((BLK, 2 * D), BF)
        gp[:, pl.ds(0, 8), :] = jnp.zeros((PAIRS, 8, 128), F32)
        gp[:, pl.ds(rows + 8, 8), :] = jnp.zeros((PAIRS, 8, 128), F32)
        kp[pl.ds(0, BLK), :] = jnp.full((BLK, 128), -1.0, F32)
        kp[pl.ds(rows + BLK, BLK), :] = jnp.full((BLK, 128), -1.0, F32)

        def fill(i, at, carry):
            kp[pl.ds(pl.multiple_of(i * BLK + BLK, BLK), BLK), :] = kb_ref[at, :]
            xb[0, at, :] = x0_ref[at, :]
            return carry

        blocks(rows, fill)

        def feed(l, k, src, dst, gain, wi, early=lambda: None):
            settle(5 + k, l)
            settle(dst, l)

            def first(i, at, carry):
                x = xb[src, at, :]
                xhat, _ = normalise(x)
                a_s[at, :] = (xhat * gain).astype(BF)
                xb[dst, at, :] = x
                return carry

            blocks(rows, first)
            use(wi, l)
            use(wi + 1, l)
            early()

            def chunk(c):
                cols = cut(c, 512)
                h = dot_nn(a_s[top, :], fin[k, :, cols])
                hb[k, top, cols] = h.astype(BF)
                s = (h * sigmoid(h)).astype(BF)
                xb[dst, top, :] = xb[dst, top, :] + 0.5 * dot_nn(s, fout[k, cols, :])

            each(FF // 512, rows, chunk)
            next_weight(wi, l)
            next_weight(wi + 1, l)
            save(5 + k, l).start()
            save(dst, l).start()

        def first_weights(l, which):
            @pl.when(l == 0)
            def _():
                for i in which:
                    weight_copy(i, 0).start()

        def layer(l, carry):
            gains = [gains_ref[l, pl.ds(i, 1), :] for i in range(5)]
            save(0, l).start()
            feed(l, 0, 0, 1, gains[0], 0, lambda: first_weights(l, (2, 3)))
            first_weights(l, (4, 5, 6, 7))

            norm_into(xb.at[1], gains[1], a_s, rows)
            settle(7, l)
            settle(8, l)
            settle(9, l)
            settle(10, l)
            use(2, l)
            for part in range(3):
                proj = dot_nn(a_s[top, :], ain[:, part * D : (part + 1) * D])
                for p in range(PAIRS):
                    lanes = slice(p * 128, (p + 1) * 128)
                    v = proj[:, lanes]
                    if part < 2:
                        v = v * cos_ref[top, :] + swap_halves(v) * sin_ref[top, :]
                    if part == 0:
                        qb[top, lanes] = (v * HD**-0.5).astype(BF)
                    elif part == 1:
                        kvb[pl.ds(BLK, rows), lanes] = v.astype(BF)
                    else:
                        kvb[pl.ds(BLK, rows), D + p * 128 : D + (p + 1) * 128] = v.astype(BF)
            next_weight(2, l)

            def tile(t, at, c):
                near = pl.ds(pl.multiple_of(t * BLK, BLK), 3 * BLK)
                same = kp[near, :] == kr_ref[0:1, pl.ds(pl.multiple_of(t * BLK + BLK, BLK), BLK)]
                same = jnp.concatenate([same, same], axis=1)
                for p in range(PAIRS):
                    lanes = slice(p * 128, (p + 1) * 128)
                    s = dot_nt(kvb[near, lanes], stacked(qb[at, lanes]))
                    s = jnp.where(same, s, MASKED)
                    e = jnp.exp(s - jnp.max(s, axis=0, keepdims=True))
                    low = (e * (1.0 / jnp.sum(e, axis=0, keepdims=True))).astype(BF)
                    ab[t, p] = low
                    o = dot_tn(low, kvb[near, D + p * 128 : D + (p + 1) * 128])
                    ob[at, lanes] = unstacked(o).astype(BF)
                return c

            blocks(rows, tile)
            settle(2, l)
            use(3, l)
            xb[2, top, :] = xb[1, top, :] + dot_nn(ob[top, :], aout[...])
            next_weight(3, l)
            for i in (7, 8, 9, 10, 2):
                save(i, l).start()

            norm_into(xb.at[2], gains[2], a_s, rows)
            settle(11, l)
            settle(12, l)
            use(4, l)
            for half in range(2):
                lanes = slice(half * 256, (half + 1) * 256)
                up1 = dot_nn(a_s[top, :], pin[:, half * 256 : (half + 1) * 256])
                up2 = dot_nn(a_s[top, :], pin[:, D + half * 256 : D + (half + 1) * 256])
                ub[top, lanes] = up1.astype(BF)
                ub[top, D + half * 256 : D + (half + 1) * 256] = up2.astype(BF)
                gated = (up1 * sigmoid(up2)).astype(BF).astype(F32)
                for q in range(2):
                    gp[2 * half + q, pl.ds(8, rows), :] = gated[:, q * 128 : (q + 1) * 128]
            next_weight(4, l)
            rs = lax.rsqrt(var_ref[pl.ds(l, 1), :] + EPSILON)
            mean = mean_ref[pl.ds(l, 1), :]
            scale = scale_ref[pl.ds(l, 1), :]
            shift = shift_ref[pl.ds(l, 1), :]

            def conv(t, at, c):
                near = [pl.ds(t * BLK + 4 + o, BLK) for o in range(KERNEL)]
                own = kb_ref[at, :]
                masks = [kp[pl.ds(t * BLK + BLK - HALO + o, BLK), :] == own for o in range(KERNEL)]
                for p in range(PAIRS):
                    lanes = slice(p * 128, (p + 1) * 128)
                    z = jnp.zeros((BLK, 128), F32)
                    for o in range(KERNEL):
                        w = taps_ref[l, o : o + 1, lanes]
                        z = z + jnp.where(masks[o], w * gp[p, near[o], :], 0.0)
                    zb[at, lanes] = z
                    b = (z - mean[:, lanes]) * rs[:, lanes] * scale[:, lanes] + shift[:, lanes]
                    a_s[at, lanes] = (b * sigmoid(b)).astype(BF)
                return c

            blocks(rows, conv)
            settle(3, l)
            use(5, l)
            xb[3, top, :] = xb[2, top, :] + dot_nn(a_s[top, :], pout[...])
            next_weight(5, l)
            for i in (11, 12, 3):
                save(i, l).start()

            feed(l, 1, 3, 4, gains[3], 6)
            save(0, l).wait()

            def last(i, at, c):
                xhat, _ = normalise(xb[4, at, :])
                y = xhat * gains[4]
                xb[0, at, :] = y
                act_ref[at, :] = y.astype(BF)
                return c

            blocks(rows, last)
            return carry

        lax.fori_loop(0, layers, layer, jnp.int32(0))
        for i in range(1, len(saves)):
            save(i, layers - 1).wait()
        if rows < CAP:
            act_ref[pl.ds(rows, CAP - rows), :] = jnp.zeros((CAP - rows, D), BF)

    by_rows(n_ref, run)


def forward(n, x0, cos, sin, kb, kr, small, mats):
    layers = small[0].shape[0]
    outs = [
        (struct((CAP, D), BF), VMEM),
        (struct((layers, 5, CAP, D), F32), ANY),
        (struct((layers, 2, CAP, FF), BF), ANY),
        (struct((layers, CAP, D), BF), ANY),
        (struct((layers, CAP + 2 * BLK, 2 * D), BF), ANY),
        (struct((layers, CAP // BLK, PAIRS, 3 * BLK, 2 * BLK), BF), ANY),
        (struct((layers, CAP, D), BF), ANY),
        (struct((layers, CAP, 2 * D), BF), ANY),
        (struct((layers, CAP, D), F32), ANY),
    ]
    vm = pltpu.VMEM
    scratch = [
        vm((2, D, FF), BF), vm((2, FF, D), BF), vm((D, 3 * D), BF), vm((D, D), BF), vm((D, 2 * D), BF), vm((D, D), BF),
        vm((5, CAP, D), F32), vm((2, CAP, FF), BF), vm((CAP, D), BF), vm((CAP + 2 * BLK, 2 * D), BF),
        vm((CAP // BLK, PAIRS, 3 * BLK, 2 * BLK), BF), vm((CAP, D), BF), vm((CAP, 2 * D), BF), vm((CAP, D), F32),
        vm((CAP, D), BF), vm((PAIRS, CAP + 16, 128), F32), vm((CAP + 2 * BLK, 128), F32),
        pltpu.SemaphoreType.DMA((8,)), pltpu.SemaphoreType.DMA((13,)),
    ]
    return call(
        forward_body,
        [SMEM] + [VMEM] * 11 + [ANY] * 6,
        outs,
        scratch,
        (n, x0, cos, sin, kb, kr, *small, *mats),
        flops=2 * 640 * 12e6,
        moved=60 * 2**20,
        name="forward",
    )


class Out:
    def __init__(self, core, buf, kept_h, sent_h, sem):
        self.core = core
        self.buf = buf
        self.homes = (kept_h, sent_h)
        self.sem = sem

    def put(self, at, pair):
        self.buf[(self.core,) + at] = pair[0].astype(BF)
        self.buf[(1 - self.core,) + at] = pair[1].astype(BF)

    def copies(self, slot, at):
        return [
            pltpu.make_async_copy(self.buf.at[(i,) + at], home.at[at], self.sem.at[2 * slot + i])
            for i, home in enumerate(self.homes)
        ]

    def send(self, slot, at):
        for c in self.copies(slot, at):
            c.start()

    def wait(self, slot, at):
        for c in self.copies(slot, at):
            c.wait()


def transposed_out(out, dwo, first):
    for z in range(4):
        for b in range(dwo.shape[1] // LANES):
            pair = [dwo[z * 128 + q * 64 : z * 128 + q * 64 + 64, b * LANES : (b + 1) * LANES] for q in range(2)]
            out.put((z, first(b), slice(None)), pair)


def feed_part(l, k, what, core_ref, g_s, ins, outs, scratch):
    final = k == 1
    do_out, do_in = what != "in", what != "out"
    base = D if do_in else 0
    gains_ref, xs_h, hs_h, fin_h, fout_h, *small_refs = ins
    others = len(small_refs)
    keep_h, send_h, small_ref = outs
    x_s, x4_s, h_s, fin, fout, gl_s, a_s, da_s, buf, sem, osem = scratch
    gain = gains_ref[l, pl.ds(3 if final else 0, 1), :]
    gain4 = gains_ref[l, pl.ds(4, 1), :]
    out = Out(core_ref[0], buf, keep_h, send_h, osem)
    every = pl.ds(0, 4)
    high = base + FF * D // (8 * LANES) if do_out else D

    def run(rows):
        top = pl.ds(0, rows)

        def chunk_in(c):
            cols = cut(c, 512)
            made = [pltpu.make_async_copy(hs_h.at[l, k, top, cols], h_s.at[top, cols], sem.at[3 + 3 * c])]
            if do_in:
                made += [
                    pltpu.make_async_copy(fout_h.at[l, k, cols], fout.at[cols], sem.at[4 + 3 * c]),
                    pltpu.make_async_copy(fin_h.at[l, k, :, cols], fin.at[:, cols], sem.at[5 + 3 * c]),
                ]
            return made

        starts = []
        if do_in:
            starts.append(pltpu.make_async_copy(xs_h.at[l, 3 if final else 0, top], x_s.at[top], sem.at[1]))
        if final:
            starts.insert(0, pltpu.make_async_copy(xs_h.at[l, 4, top], x4_s.at[top], sem.at[2]))

        def start():
            for c in starts + chunk_in(0):
                c.start()

        def first(i, at, carry):
            g = g_s[at, :]
            if final:
                xhat, inv = normalise(x4_s[at, :])
                carry = carry + fold(g * xhat)
                g = norm_back(g, xhat, inv, gain4)
                g_s[at, :] = g
            gl_s[at, :] = (0.5 * g).astype(BF)
            if do_in:
                xhat, _ = normalise(x_s[at, :])
                a_s[at, :] = (xhat * gain).astype(BF)
                da_s[at, :] = jnp.zeros((BLK, D), F32)
            return carry

        def low_rows(c):
            low = base + c * 128
            return pl.ds(low, 128) if isinstance(c, int) else pl.ds(pl.multiple_of(low, 128), 128)

        def spots(c):
            return [(c, pl.ds(0, D))] * do_in + [(every, low_rows(c))] * do_out

        def chunk(c):
            cols = cut(c, 512)
            for copy in chunk_in(c):
                copy.wait()
            if isinstance(c, int):
                for copy in chunk_in(c + 2) if c < 2 else []:
                    copy.start()
            else:

                @pl.when(c < 2)
                def _():
                    for copy in chunk_in(c + 2):
                        copy.start()

            h = h_s[top, cols].astype(F32)
            sig = sigmoid(h)
            if do_in:
                ds = dot_nt(gl_s[top, :], fout[cols, :])
                dh = (ds * (sig * (1.0 + h * (1.0 - sig)))).astype(BF)
                dwi = dot_tn(a_s[top, :], dh)
                out.put((c, pl.ds(0, D), slice(None)), (dwi[:, :LANES], dwi[:, LANES:]))
            if do_out:
                dwo = dot_tn(gl_s[top, :], (h * sig).astype(BF))
                step = lambda b: (base + (2 * c + b) * 64)
                transposed_out(
                    out, dwo,
                    lambda b: pl.ds(step(b), 64) if isinstance(c, int) else pl.ds(pl.multiple_of(step(b), 64), 64),
                )
            for i, at in enumerate(spots(c)):
                out.send(2 * c + i, at)
            if do_in:
                da_s[top, :] = da_s[top, :] + dot_nt(dh, fin[:, cols])

        def last(i, at, carry):
            xhat, inv = normalise(x_s[at, :])
            da = da_s[at, :]
            g_s[at, :] = g_s[at, :] + norm_back(da, xhat, inv, gain)
            return carry + fold(da * xhat)

        def small_chunks():
            buf[:, :, pl.ds(high, SMALL_ROWS), :] = jnp.zeros((2, 4, SMALL_ROWS, LANES), BF)
            rows_all = jnp.concatenate([small_ref[...]] + [ref[...] for ref in small_refs], axis=0)
            lines = SMALL_ROWS // 4
            rows_all = jnp.concatenate([rows_all, jnp.zeros((4 * lines - rows_all.shape[0], D), F32)], axis=0)
            for z in range(4):
                pair = []
                for q in range(2):
                    own = rows_all[:, z * 128 + q * 64 : z * 128 + q * 64 + 64]
                    pair.append(jnp.concatenate([own[i * lines : (i + 1) * lines] for i in range(4)], axis=1))
                out.put((z, pl.ds(high, lines), slice(None)), pair)

        low_spot = (every, pl.ds(high, SMALL_ROWS))

        def main(midway):
            for c in starts:
                c.wait()
            for c in chunk_in(1):
                c.start()
            midway()
            gain4_grad = blocks(rows, first, jnp.zeros((8, D), F32))
            each(FF // 512, rows, chunk)
            small_ref[...] = jnp.zeros(small_ref.shape, F32)
            if do_in:
                small_ref[0:1, :] = total(blocks(rows, last, jnp.zeros((8, D), F32)))
            small_ref[1:2, :] = total(gain4_grad)
            if others:
                small_chunks()
                out.send(8, low_spot)

        def finish():
            if others:
                out.wait(8, low_spot)
            for c in range(4):
                for i, at in enumerate(spots(c)):
                    out.wait(2 * c + i, at)

        return start, main, finish

    return run


def feed_spec(l, k, what, smalls, gains, xs, hs, fin, fout):
    vm = pltpu.VMEM
    do_out, do_in = what != "in", what != "out"
    lines = D * do_in + D * do_out + (SMALL_ROWS if smalls else 0)
    none = (8, D)
    return (
        functools.partial(feed_part, l, k, what),
        [(gains, VMEM), (xs, ANY), (hs, ANY), (fin, ANY), (fout, ANY)] + [(v, VMEM) for v in smalls],
        [
            (struct((4, lines, LANES), BF), ANY),
            (struct((4, lines, LANES), BF), ANY),
            (struct((8, D), F32), VMEM),
        ],
        [
            vm((CAP, D) if do_in else none, F32), vm((CAP, D) if k == 1 else none, F32), vm((CAP, FF), BF),
            vm((D, FF) if do_in else none, BF), vm((FF, D) if do_in else none, BF), vm((CAP, D), BF),
            vm((CAP, D) if do_in else none, BF), vm((CAP, D) if do_in else none, F32),
            vm((2, 4, lines, LANES), BF),
            pltpu.SemaphoreType.DMA((15,)), pltpu.SemaphoreType.DMA((18,)),
        ],
        (2 * do_out + 6 * do_in) * 640 * D * FF,
    )


def conv_part(l, core_ref, g_s, ins, outs, scratch):
    kb_ref, gains_ref, taps_ref, mean_ref, var_ref, scale_ref, shift_ref, xs_h, u_h, z_h, pin_h, pout_h = ins
    keep_h, send_h, small_ref = outs
    x_s, u_s, z_s, pin, pout, gl_s, a_s, e_s, de_s, gp, dzp, kp, du_s, buf, sem, osem = scratch
    gain = gains_ref[l, pl.ds(2, 1), :]
    rs = lax.rsqrt(var_ref[pl.ds(l, 1), :] + EPSILON)
    mean = mean_ref[pl.ds(l, 1), :]
    scale = scale_ref[pl.ds(l, 1), :]
    shift = shift_ref[pl.ds(l, 1), :]
    out = Out(core_ref[0], buf, keep_h, send_h, osem)
    every = pl.ds(0, 4)

    def run(rows):
        top = pl.ds(0, rows)
        copies = [
            None,
            pltpu.make_async_copy(pout_h.at[l], pout, sem.at[1]),
            pltpu.make_async_copy(z_h.at[l, top], z_s.at[top], sem.at[2]),
            pltpu.make_async_copy(u_h.at[l, top], u_s.at[top], sem.at[3]),
            pltpu.make_async_copy(xs_h.at[l, 2, top], x_s.at[top], sem.at[4]),
            pltpu.make_async_copy(pin_h.at[l], pin, sem.at[5]),
        ]
        low_spot = (every, pl.ds(256, 128))
        high_spot = (every, pl.ds(0, 256))

        def start():
            for c in copies[1:4]:
                c.start()

        def finish():
            out.wait(0, low_spot)
            out.wait(1, high_spot)

        return start, functools.partial(conv_work, rows, copies), finish

    def conv_work(rows, copies, midway):
        top = pl.ds(0, rows)
        low_spot = (every, pl.ds(256, 128))
        high_spot = (every, pl.ds(0, 256))
        for ref in (gp, dzp):
            ref[:, pl.ds(0, 8), :] = jnp.zeros((PAIRS, 8, 128), F32)
            ref[:, pl.ds(rows + 8, 8), :] = jnp.zeros((PAIRS, 8, 128), F32)
        kp[pl.ds(0, 8), :] = jnp.full((8, 128), -1.0, F32)
        kp[pl.ds(rows + 8, 8), :] = jnp.full((8, 128), -1.0, F32)

        def low(i, at, carry):
            gl_s[at, :] = g_s[at, :].astype(BF)
            kp[pl.ds(pl.multiple_of(i * BLK + 8, 8), BLK), :] = kb_ref[at, :]
            return carry

        blocks(rows, low)
        for c in copies[1:4]:
            c.wait()
        for c in copies[4:]:
            c.start()
        midway()
        de_s[top, :] = dot_nt(gl_s[top, :], pout[...])
        copies[4].wait()

        def first(i, at, carry):
            scale_grad, shift_grad = carry
            inner = pl.ds(pl.multiple_of(i * BLK + 8, 8), BLK)
            hat = (z_s[at, :] - mean) * rs
            b = hat * scale + shift
            sig = sigmoid(b)
            e_s[at, :] = (b * sig).astype(BF)
            db = de_s[at, :] * (sig * (1.0 + b * (1.0 - sig)))
            dz = (db * scale * rs).astype(BF).astype(F32)
            u1 = u_s[at, pl.ds(0, D)].astype(F32)
            u2 = u_s[at, pl.ds(D, D)].astype(F32)
            gated = (u1 * sigmoid(u2)).astype(BF).astype(F32)
            for p in range(PAIRS):
                dzp[p, inner, :] = dz[:, p * 128 : (p + 1) * 128]
                gp[p, inner, :] = gated[:, p * 128 : (p + 1) * 128]
            xhat, _ = normalise(x_s[at, :])
            a_s[at, :] = (xhat * gain).astype(BF)
            return (scale_grad + fold(db * hat), shift_grad + fold(db))

        zero = jnp.zeros((8, D), F32)
        scale_grad, shift_grad = blocks(rows, first, (zero, zero))
        small_ref[...] = jnp.zeros(small_ref.shape, F32)
        small_ref[1:2, :] = total(scale_grad)
        small_ref[2:3, :] = total(shift_grad)
        dwo = dot_tn(gl_s[top, :], e_s[top, :])
        transposed_out(out, dwo, lambda b: pl.ds(256 + b * 64, 64))
        out.send(0, low_spot)

        for p in range(PAIRS):
            lanes = slice(p * 128, (p + 1) * 128)

            def taps(t, at, carry, lanes=lanes, p=p):
                own = kb_ref[at, :]
                dz_own = dzp[p, pl.ds(pl.multiple_of(t * BLK + 8, 8), BLK), :]
                dg = jnp.zeros((BLK, 128), F32)
                sums = []
                for o in range(KERNEL):
                    near = pl.ds(t * BLK + 4 + o, BLK)
                    mask = kp[near, :] == own
                    sums.append(carry[o] + fold(jnp.where(mask, dz_own * gp[p, near, :], 0.0)))
                    w = taps_ref[l, KERNEL - 1 - o : KERNEL - o, lanes]
                    dg = dg + jnp.where(mask, w * dzp[p, near, :], 0.0)
                u1 = u_s[at, lanes].astype(F32)
                sig = sigmoid(u_s[at, D + p * 128 : D + (p + 1) * 128].astype(F32))
                du_s[at, lanes] = (dg * sig).astype(BF)
                du_s[at, D + p * 128 : D + (p + 1) * 128] = (dg * u1 * sig * (1.0 - sig)).astype(BF)
                return tuple(sums)

            sums = blocks(rows, taps, tuple(jnp.zeros((8, 128), F32) for _ in range(KERNEL)))
            for o in range(KERNEL):
                small_ref[8 + o : 9 + o, lanes] = total(sums[o])

        for half in range(2):
            dwi = dot_tn(a_s[top, :], du_s[top, half * 512 : (half + 1) * 512])
            for q in range(2):
                pair = [
                    jnp.concatenate([dwi[: D // 2, at : at + 128], dwi[D // 2 :, at : at + 128]], axis=1)
                    for at in (q * 256, q * 256 + 128)
                ]
                out.put((2 * half + q, pl.ds(0, 256), slice(None)), pair)
        out.send(1, high_spot)
        copies[5].wait()
        de_s[top, :] = dot_nt(du_s[top, :], pin[...])

        def last(i, at, carry):
            xhat, inv = normalise(x_s[at, :])
            da = de_s[at, :]
            g_s[at, :] = g_s[at, :] + norm_back(da, xhat, inv, gain)
            return carry + fold(da * xhat)

        small_ref[0:1, :] = total(blocks(rows, last, zero))

    return run


def conv_spec(l, kb, small, xs, u, z, pin, pout):
    vm = pltpu.VMEM
    return (
        functools.partial(conv_part, l),
        [(kb, VMEM)] + [(v, VMEM) for v in small] + [(v, ANY) for v in (xs, u, z, pin, pout)],
        [
            (struct((4, 384, LANES), BF), ANY),
            (struct((4, 384, LANES), BF), ANY),
            (struct((24, D), F32), VMEM),
        ],
        [
            vm((CAP, D), F32), vm((CAP, 2 * D), BF), vm((CAP, D), F32), vm((D, 2 * D), BF),
            vm((D, D), BF), vm((CAP, D), BF), vm((CAP, D), BF), vm((CAP, D), BF), vm((CAP, D), F32),
            vm((PAIRS, CAP + 16, 128), F32), vm((PAIRS, CAP + 16, 128), F32), vm((CAP + 16, 128), F32),
            vm((CAP, 2 * D), BF), vm((2, 4, 384, LANES), BF),
            pltpu.SemaphoreType.DMA((6,)), pltpu.SemaphoreType.DMA((4,)),
        ],
        12 * 640 * D * D,
    )


def attend_part(l, core_ref, g_s, ins, outs, scratch):
    cos_ref, sin_ref, gains_ref, xs_h, q_h, kv_h, at_h, o_h, ain_h, aout_h = ins
    keep_h, send_h, small_ref = outs
    x_s, q_s, kv_s, at_s, o_s, ain, aout, gl_s, a_s, do_s, dq_s, dkv_s, dp_s, da_s, buf, sem, osem = scratch
    out = Out(core_ref[0], buf, keep_h, send_h, osem)
    every = pl.ds(0, 4)
    gain = gains_ref[l, pl.ds(1, 1), :]

    def run(rows):
        tiles = rows // BLK
        top = pl.ds(0, rows)
        wide = pl.ds(0, rows + 2 * BLK)
        copies = [
            pltpu.make_async_copy(aout_h.at[l], aout, sem.at[0]),
            pltpu.make_async_copy(o_h.at[l, top], o_s.at[top], sem.at[1]),
            pltpu.make_async_copy(q_h.at[l, top], q_s.at[top], sem.at[2]),
            pltpu.make_async_copy(kv_h.at[l, wide], kv_s.at[wide], sem.at[3]),
            pltpu.make_async_copy(xs_h.at[l, 1, top], x_s.at[top], sem.at[5]),
            pltpu.make_async_copy(ain_h.at[l], ain, sem.at[6]),
        ]
        copies = [None] + copies

        def weights_in(t):
            return pltpu.make_async_copy(at_h.at[l, t], at_s.at[t], sem.at[8 + t])

        low_spot = (every, pl.ds(384, 128))
        high_spot = (every, pl.ds(0, 384))

        def start():
            for c in copies[1:5]:
                c.start()
            weights_in(0).start()

        def finish():
            out.wait(0, low_spot)
            out.wait(1, high_spot)

        return start, functools.partial(attend_work, rows, copies, weights_in), finish

    def attend_work(rows, copies, weights_in, midway):
        tiles = rows // BLK
        top = pl.ds(0, rows)
        low_spot = (every, pl.ds(384, 128))
        high_spot = (every, pl.ds(0, 384))

        def low(i, at, carry):
            gl_s[at, :] = g_s[at, :].astype(BF)
            return carry

        blocks(rows, low)

        def clear(i, at, carry):
            dkv_s[at, :] = jnp.zeros((BLK, 2 * D), F32)
            return carry

        blocks(rows + 2 * BLK, clear)
        copies[1].wait()
        do_s[top, :] = dot_nt(gl_s[top, :], aout[...]).astype(BF)
        for c in copies[2:5]:
            c.wait()
        for c in copies[5:]:
            c.start()
        midway()

        def tile(t, at, carry):
            near = pl.ds(pl.multiple_of(t * BLK, BLK), 3 * BLK)
            weights_in(t).wait()

            @pl.when(t + 1 < tiles)
            def _():
                weights_in(t + 1).start()

            for p in range(PAIRS):
                lanes = slice(p * 128, (p + 1) * 128)
                vlanes = slice(D + p * 128, D + (p + 1) * 128)
                do = stacked(do_s[at, lanes])
                low = at_s[t, p]
                weights = low.astype(F32)
                da = dot_nt(kv_s[near, vlanes], do)
                delta = jnp.sum(weights * da, axis=0, keepdims=True)
                ds = (weights * (da - delta)).astype(BF)
                dq_s[at, lanes] = unstacked(dot_tn(ds, kv_s[near, lanes])) * HD**-0.5
                dkv_s[near, lanes] = dkv_s[near, lanes] + dot_nn(ds, stacked(q_s[at, lanes]))
                dkv_s[near, vlanes] = dkv_s[near, vlanes] + dot_nn(low, do)
            return carry

        blocks(rows, tile)
        copies[5].wait()

        def turn(i, at, carry):
            inner = pl.ds(pl.multiple_of(i * BLK + BLK, BLK), BLK)
            cos, sin = cos_ref[at, :], sin_ref[at, :]
            for p in range(PAIRS):
                lanes = slice(p * 128, (p + 1) * 128)
                dq = dq_s[at, lanes]
                dk = dkv_s[inner, lanes]
                dp_s[at, lanes] = (dq * cos - swap_halves(dq) * sin).astype(BF)
                dp_s[at, D + p * 128 : D + (p + 1) * 128] = (dk * cos - swap_halves(dk) * sin).astype(BF)
                dp_s[at, 2 * D + p * 128 : 2 * D + (p + 1) * 128] = dkv_s[
                    inner, D + p * 128 : D + (p + 1) * 128
                ].astype(BF)
            xhat, _ = normalise(x_s[at, :])
            a_s[at, :] = (xhat * gain).astype(BF)
            return carry

        blocks(rows, turn)

        dwo = dot_tn(gl_s[top, :], o_s[top, :])
        transposed_out(out, dwo, lambda b: pl.ds(384 + b * 64, 64))
        out.send(0, low_spot)
        for half in range(2):
            dwi = dot_tn(dp_s[top, half * 768 : (half + 1) * 768], a_s[top, :])
            for q in range(2):
                for b in range(2):
                    pair = [
                        dwi[q * 384 + r * 192 : q * 384 + (r + 1) * 192, b * LANES : (b + 1) * LANES] for r in range(2)
                    ]
                    out.put((2 * half + q, pl.ds(b * 192, 192), slice(None)), pair)
        out.send(1, high_spot)
        copies[6].wait()
        da_s[top, :] = dot_nt(dp_s[top, :], ain[...])

        def last(i, at, carry):
            xhat, inv = normalise(x_s[at, :])
            da = da_s[at, :]
            g_s[at, :] = g_s[at, :] + norm_back(da, xhat, inv, gain)
            return carry + fold(da * xhat)

        small_ref[0:1, :] = total(blocks(rows, last, jnp.zeros((8, D), F32)))

    return run


def attend_spec(l, cos, sin, gains, xs, q, kv, at, o, ain, aout):
    vm = pltpu.VMEM
    return (
        functools.partial(attend_part, l),
        [(v, VMEM) for v in (cos, sin, gains)] + [(v, ANY) for v in (xs, q, kv, at, o, ain, aout)],
        [
            (struct((4, 512, LANES), BF), ANY),
            (struct((4, 512, LANES), BF), ANY),
            (struct((8, D), F32), VMEM),
        ],
        [
            vm((CAP, D), F32), vm((CAP, D), BF), vm((CAP + 2 * BLK, 2 * D), BF),
            vm((CAP // BLK, PAIRS, 3 * BLK, 2 * BLK), BF), vm((CAP, D), BF), vm((D, 3 * D), BF), vm((D, D), BF),
            vm((CAP, D), BF), vm((CAP, D), BF), vm((CAP, D), BF), vm((CAP, D), F32),
            vm((CAP + 2 * BLK, 2 * D), F32), vm((CAP, 3 * D), BF), vm((CAP, D), F32),
            vm((2, 4, 512, LANES), BF),
            pltpu.SemaphoreType.DMA((8 + CAP // BLK,)), pltpu.SemaphoreType.DMA((4,)),
        ],
        16 * 640 * D * D,
    )


def run_parts(name, n, core, g, specs, deps):
    in_counts = [len(spec[1]) for spec in specs]
    out_counts = [len(spec[2]) for spec in specs]
    scratch_counts = [len(spec[3]) for spec in specs]

    def taken(refs, counts):
        pieces, off = [], 0
        for count in counts:
            pieces.append(refs[off : off + count])
            off += count
        return pieces

    def body(n_ref, core_ref, g_h, *refs):
        ins, refs = refs[: sum(in_counts)], refs[sum(in_counts) :]
        out_h, *outs = refs[: 1 + sum(out_counts)]
        g_s, g_sem, *scratch = refs[1 + sum(out_counts) :]
        parts = [
            spec[0](core_ref, g_s, *piece)
            for spec, *piece in zip(
                specs, taken(ins, in_counts), taken(outs, out_counts), taken(scratch, scratch_counts)
            )
        ]

        def run(rows):
            top = pl.ds(0, rows)
            steps = [part(rows) for part in parts]
            g_in = pltpu.make_async_copy(g_h.at[top], g_s.at[top], g_sem)
            g_in.start()
            steps[0][0]()
            g_in.wait()
            for i, (_, main, _) in enumerate(steps):
                main(steps[i + 1][0] if i + 1 < len(steps) else lambda: None)
            g_out = pltpu.make_async_copy(g_s.at[top], out_h.at[top], g_sem)
            g_out.start()
            for _, _, finish in steps:
                finish()
            g_out.wait()

        by_rows(n_ref, run)

    outs = [(struct((CAP, D), F32), ANY)] + [out for spec in specs for out in spec[2]]
    g, *rest = call(
        body,
        [SMEM, SMEM, ANY] + [where for spec in specs for _, where in spec[1]],
        outs,
        [pltpu.VMEM((CAP, D), F32), pltpu.SemaphoreType.DMA] + [v for spec in specs for v in spec[3]],
        (n, core, g, *(v for spec in specs for v, _ in spec[1])),
        flops=sum(spec[4] for spec in specs),
        moved=16 * 2**20,
        name=name,
        deps=deps,
    )
    return g, taken(rest, out_counts)


def add(*terms):
    acc = terms[0].astype(F32)
    for term in terms[1:]:
        acc = acc + term.astype(F32)
    return acc.astype(BF)


def spot_of(place_ref):
    x, y, core = place_ref[0], place_ref[1], place_ref[3]
    even = core == 0
    return jnp.where(even, x, y), jnp.where(even, y, x), 1 + core, 2 - core


def split_first_body(sizes, place_ref, *refs):
    count = len(sizes)
    keeps, gots = refs[:count], refs[count : 2 * count]
    kept, sent = refs[2 * count :]
    first, _, by_first, by_second = spot_of(place_ref)
    off = 0
    for keep, got, n in zip(keeps, gots, sizes):
        at = pl.ds(off, n)

        def one(z, carry, keep=keep, got=got, at=at):
            for j in range(2):
                own = first * by_first + j * by_second
                other = (1 - first) * by_first + j * by_second
                kept[z, j, at] = add(keep[z, own], got[z, own])
                sent[z, j, at] = add(keep[z, other], got[z, other])
            return carry

        lax.fori_loop(0, 4, one, jnp.int32(0))
        off += n


def split_second_body(sizes, place_ref, *refs):
    *ins, kept, sent = refs
    _, second, _, _ = spot_of(place_ref)
    off = 0
    for i, n in enumerate(sizes):
        keep, got = ins[2 * i : 2 * i + 2]
        at = pl.ds(off, n)

        def one(z, carry, keep=keep, got=got, at=at):
            kept[z, at] = add(keep[z, second], got[z, second])
            sent[z, at] = add(keep[z, 1 - second], got[z, 1 - second])
            return carry

        lax.fori_loop(0, 4, one, jnp.int32(0))
        off += n


def split_z_body(plan, place_ref, *refs):
    ins, outs = refs[:-4], refs[-4:]
    z = place_ref[2]
    for k, ref in enumerate(outs):
        at = lax.rem(z + k, 4)
        off = used = 0
        for count, n in plan:
            terms = [r[at] for r in ins[used : used + count]]
            ref[pl.ds(off, n), :] = add(*terms) if count > 1 else terms[0]
            used += count
            off += n


def along(axis):
    return [(r * 8 + t, (r ^ (1 << ((t + axis) % 2))) * 8 + t) for r in range(4) for t in range(8)]


def sum_cores_body(sizes, *refs):
    count = len(sizes)
    keeps, gots, out = refs[:count], refs[count : 2 * count], refs[2 * count]
    off = 0
    for keep, got, n in zip(keeps, gots, sizes):
        at = pl.ds(off, n)

        def one(z, carry, keep=keep, got=got, at=at):
            for j in range(4):
                out[j, z, at] = add(keep[z, j], got[z, j])
            return carry

        lax.fori_loop(0, 4, one, jnp.int32(0))
        off += n


class Group:
    def __init__(self, spot, members):
        self.spot = spot
        self.keeps = [keep for _, keep, _ in members]
        self.sizes = [keep.shape[1] // 4 for keep in self.keeps]
        self.names = [name for name, _, _ in members]
        self.n = sum(self.sizes)
        self.bytes = 16 * self.n * LANES * 2
        self.gots = [got for _, _, got in members]

    def cores(self):
        shaped = lambda v: v.reshape(4, 4, v.shape[1] // 4, LANES)
        return (*map(shaped, self.keeps), *map(shaped, self.gots))

    def offload(self, deps):
        both = call(
            functools.partial(sum_cores_body, self.sizes),
            [VMEM] * (2 * len(self.sizes)),
            [(struct((4, 4, self.n, LANES), BF), VMEM)],
            [],
            self.cores(),
            moved=3 * self.bytes,
            name="sum_cores",
            vmem=VMEM_SMALL,
            deps=deps,
        )[0]
        part = lax.psum_scatter(both, "rows", scatter_dimension=0, tiled=True)
        self.terms = [part.reshape(4, self.n, LANES)]
        return [both]

    def first(self, deps, work=0):
        self.kept, sent = call(
            functools.partial(split_first_body, self.sizes),
            [SMEM] + [VMEM] * (2 * len(self.sizes)),
            [(struct((4, 2, self.n, LANES), BF), VMEM)] * 2,
            [],
            (self.spot, *self.cores()),
            moved=3 * self.bytes,
            name="split_first",
            vmem=VMEM_SMALL,
            flops=work,
            deps=deps,
        )
        self.got = lax.ppermute(sent, ("rows", "tm"), along(0))
        return [self.kept]


class Second:
    def __init__(self, spot, groups, deps):
        sizes = [group.n for group in groups]
        self.n = sum(sizes)
        kept, sent = call(
            functools.partial(split_second_body, sizes),
            [SMEM] + [VMEM] * (2 * len(groups)),
            [(struct((4, self.n, LANES), BF), VMEM)] * 2,
            [],
            (spot, *(v for group in groups for v in (group.kept, group.got))),
            moved=24 * self.n * LANES * 2,
            name="split_second",
            vmem=VMEM_SMALL,
            deps=deps,
        )
        self.terms = [kept, lax.ppermute(sent, ("rows", "tm"), along(1))]


def merge_body(*refs):
    *ins, out = refs
    off = 0
    for ref in ins:
        n = ref.shape[1]
        out[:, pl.ds(off, n), :] = ref[...]
        off += n


def offloaded_rest(groups, deps):
    n = sum(group.n for group in groups)
    part = call(
        merge_body,
        [VMEM] * len(groups),
        [(struct((4, n, LANES), BF), VMEM)],
        [],
        [group.terms[0] for group in groups],
        moved=16 * n * LANES,
        name="merge",
        vmem=VMEM_SMALL,
        deps=deps,
    )[0]
    mine = lax.psum_scatter(
        part, "tm", scatter_dimension=0, tiled=True, axis_index_groups=[[0, 2, 4, 6], [1, 3, 5, 7]]
    )
    return mine.reshape(part.shape[1:])


def along_z(spot, groups, deps, work=0):
    ins = [term for group in groups for term in group.terms]
    n = sum(group.n for group in groups)
    own, *others = call(
        functools.partial(split_z_body, [(len(group.terms), group.n) for group in groups]),
        [SMEM] + [VMEM] * len(ins),
        [(struct((n, LANES), BF), VMEM)] * 4,
        [],
        (spot, *ins),
        moved=16 * n * LANES * 2,
        name="split_z",
        vmem=VMEM_SMALL,
        flops=work,
        deps=deps,
    )
    return [own] + [
        lax.ppermute(v, "tm", [(i, (i + 2 * k) % 8) for i in range(8)]) for k, v in zip((1, 2, 3), others)
    ]


def join_body(plan, *refs):
    *ins, out = refs
    off = at = 0
    for count, n in plan:
        out[pl.ds(at, n), :] = add(*(ref[...] for ref in ins[off : off + count])) if count > 1 else ins[off][...]
        off += count
        at += n


def gathered(lists, deps):
    ins = [term for terms in lists for term in terms]
    plan = [(len(terms), terms[0].shape[0]) for terms in lists]
    n = sum(rows for _, rows in plan)
    mine = call(
        functools.partial(join_body, plan),
        [VMEM] * len(ins),
        [(struct((n, LANES), BF), VMEM)],
        [],
        ins,
        moved=6 * n * LANES,
        name="join",
        deps=deps,
    )[0]
    one = lax.ppermute(mine, ("rows", "tm"), along(0))
    two = lax.ppermute(mine, ("rows", "tm"), along(1))
    return [mine, one, two, lax.ppermute(one, ("rows", "tm"), along(1))]


def finish_body(members, by_bit, me_ref, *refs):
    count = 4 if by_bit else 1
    chunks = refs[:count]
    fin_h, fout_h, ain_h, aout_h, pin_h, pout_h, small_h = refs[-13:-6]
    whole, fout, ain, pin, narrow, sem = refs[-6:]
    me = me_ref[0]
    rows = sum(n for _, _, n in members)
    off = 0
    waits = []
    for i, (l, name, n) in enumerate(members):
        for j in range(4):
            if by_bit:
                flip = (0, 1 + me_ref[1], 2 - me_ref[1], 3)[j]
                owner = pl.multiple_of(jnp.bitwise_xor(me, flip) * n, n)
                whole[i, pl.ds(owner, n), :] = chunks[j][pl.ds(off, n), :].astype(F32)
            else:
                whole[i, pl.ds(j * n, n), :] = chunks[0][pl.ds(j * rows + off, n), :].astype(F32)
        off += n
        if name in ("f0", "f1", "f0in", "f0out"):
            k = int(name == "f1")
            jobs = []
            if name != "f0out":
                jobs.append((whole.at[i, pl.ds(0, D)], fin_h.at[l, k]))
            if name != "f0in":
                base = 0 if name == "f0out" else D
                for b in range(FF // LANES):
                    fout[i, :, pl.ds(b * LANES, LANES)] = whole[i, pl.ds(base + b * 64, 64), :]
                jobs.append((fout.at[i], fout_h.at[l, k]))
            else:
                jobs.append((whole.at[i, pl.ds(D, SMALL_ROWS // 4)], small_h))
        elif name == "c":
            pin[i, pl.ds(0, 256), :] = whole[i, pl.ds(0, 256), 0:128]
            pin[i, pl.ds(256, 256), :] = whole[i, pl.ds(0, 256), 128:256]
            for b in range(2):
                narrow[i, :, pl.ds(b * LANES, LANES)] = whole[i, pl.ds(256 + b * 64, 64), :]
            jobs = [(pin.at[i], pin_h.at[l]), (narrow.at[i], pout_h.at[l])]
        else:
            for b in range(2):
                ain[i, :, pl.ds(b * LANES, LANES)] = whole[i, pl.ds(b * 192, 192), :]
                narrow[i, :, pl.ds(b * LANES, LANES)] = whole[i, pl.ds(384 + b * 64, 64), :]
            jobs = [(ain.at[i], ain_h.at[l]), (narrow.at[i], aout_h.at[l])]
        for j, (src, dst) in enumerate(jobs):
            c = pltpu.make_async_copy(src, dst, sem.at[3 * i + j])
            c.start()
            waits.append(c)
    for c in waits:
        c.wait()


def finish(layers, me, groups, chunks, before, deps=()):
    members = [(*name, size) for group in groups for name, size in zip(group.names, group.sizes)]
    count = len(members)
    shapes = [
        (layers, 2, D, FF // 8), (layers, 2, D // 8, FF), (layers, 3 * D // 8, D), (layers, D // 8, D),
        (layers, D, 2 * D // 8), (layers, D // 8, D), (SMALL_ROWS // 4, LANES),
    ]
    vm = pltpu.VMEM

    def body(*refs):
        finish_body(members, len(chunks) == 4, *refs)

    return pl.pallas_call(
        body,
        out_shape=[struct(shape, F32) for shape in shapes],
        in_specs=[SMEM] + [VMEM] * len(chunks) + [ANY] * (len(before) + len(deps)),
        out_specs=[ANY] * 7,
        scratch_shapes=[
            vm((count, 1024 + SMALL_ROWS, LANES), F32), vm((count, 64, FF), F32), vm((count, 192, D), F32),
            vm((count, D, 128), F32), vm((count, 64, D), F32), pltpu.SemaphoreType.DMA((3 * count,)),
        ],
        input_output_aliases={1 + len(chunks) + i: i for i in range(len(before))},
        compiler_params=pltpu.CompilerParams(vmem_limit_bytes=VMEM_LIMIT),
        name="finish",
    )(me, *chunks, *before, *deps)


def per_device(
    frames, segment_ids, norm_gains, feed_in, feed_out, attend_in, attend_out, point_in, depthwise, stat_mean,
    stat_var, batch_scale, batch_shift, point_out, cotangent,
):
    batches, row_count, frame_count, model_dim = frames.shape
    layers = norm_gains.shape[0]
    tm_size = lax.axis_size("tm")
    rows_size = lax.axis_size("rows")
    tm = lax.axis_index("tm")
    row = lax.axis_index("rows")
    fast = tm_size == 8 and rows_size == 4
    half = batches // 2

    ids = segment_ids[:, 0] + 1
    id_rows = jnp.broadcast_to(ids.reshape(1, -1).astype(BF), (16, batches * frame_count))
    parts_of = lambda v, odd: v.reshape(half, 2, frame_count, model_dim)[:, odd].reshape(-1, model_dim)
    message = lambda odd: jnp.concatenate([parts_of(frames, odd), parts_of(cotangent, odd), id_rows], axis=0)
    above = shifted(message(0), "tm", -1)
    below = shifted(message(1), "tm", 1)
    flat = lambda v: v.reshape(batches * frame_count, model_dim)
    x0, g, chooser, cos, sin, kb, kr, n = pack(ids.astype(F32), flat(frames), flat(cotangent), below, above)
    small = (norm_gains, depthwise, stat_mean, stat_var, batch_scale, batch_shift)
    mats = (feed_in, feed_out, attend_in, attend_out, point_in, point_out)
    act, xs, hs, q, kv, at, o, u, z = forward(n, x0, cos, sin, kb, kr, small, mats)

    def filled(v):
        return jnp.where(lax.broadcasted_iota(jnp.int32, v.shape, 0) < n[0], v, 0.0).astype(BF)

    def spread(packed):
        wide = jnp.concatenate(packed, axis=1)
        frames_of = lax.dot_general(chooser, wide, (((0,), (0,)), ((), ())), preferred_element_type=F32)
        return frames_of.astype(BF)

    def unpacked(windows_of):
        windows_of = windows_of.reshape(half, 2, 2, frame_count, 2 * model_dim)
        from_below = shifted(windows_of[:, 0, 1], "tm", 1)
        from_above = shifted(windows_of[:, 1, 0], "tm", -1)
        even = windows_of[:, 0, 0] + from_below
        odd = windows_of[:, 1, 1] + from_above
        frames_out = jnp.stack([even, odd], axis=1).reshape(batches, 1, frame_count, 2 * model_dim)
        return jnp.split(frames_out, 2, axis=-1)

    if fast:
        spot = jnp.stack([row % 2, row // 2, tm // 2, tm % 2]).astype(jnp.int32)
        core = (tm % 2).astype(jnp.int32).reshape(1)
    else:
        spot = None
        core = jnp.zeros((1,), jnp.int32)

    members = {}
    smalls = {}
    parts = {
        "f1": lambda l: feed_spec(l, 1, "all", (), norm_gains, xs, hs, feed_in, feed_out),
        "c": lambda l: conv_spec(l, kb, small, xs, u, z, point_in, point_out),
        "a": lambda l: attend_spec(l, cos, sin, norm_gains, xs, q, kv, at, o, attend_in, attend_out),
        "f0": lambda l: feed_spec(l, 0, "all", (), norm_gains, xs, hs, feed_in, feed_out),
        "f0out": lambda l: feed_spec(l, 0, "out", (), norm_gains, xs, hs, feed_in, feed_out),
        "f0in": lambda l, rest: feed_spec(l, 0, "in", rest, norm_gains, xs, hs, feed_in, feed_out),
    }
    order = [(l, name) for l in range(layers) for name in ("f0", "a", "c", "f1")]

    def back(l, *names, deps=(), **more):
        nonlocal g
        specs = [parts[name](l, **more) for name in names]
        g, outs = run_parts(f"back_{l}_{'_'.join(names)}", n, core, g, specs, deps)
        for name, (kept, sent, small_grads) in zip(names, outs):
            smalls[l, name] = small_grads
            members[l, name] = ((l, name), kept, sent)

    crossed = {}

    def begin(l, name):
        crossed[l, name] = lax.ppermute(members[l, name][2], "tm", [(i, i ^ 1) for i in range(8)])

    def group(*names):
        for name in names:
            if name not in crossed:
                begin(*name)
        return Group(spot, [(name, members[name][1], crossed[name]) for name in names])

    if fast:
        me = jnp.stack([2 * spot[1] + spot[0], spot[3]])
        back(1, "f1", "c")
        one = group((1, "f1"), (1, "c"))
        made = one.offload([])
        back(1, "a", "f0", deps=made)
        begin(1, "a")
        begin(1, "f0")
        back(0, "f1")
        begin(0, "f1")
        two = group((1, "a"), (1, "f0"))
        made = two.offload([g])
        back(0, "c", deps=made + one.terms)
        begin(0, "c")
        three = group((0, "f1"))
        made = three.first([g])
        back(0, "a", "f0out", deps=made)
        four = group((0, "c"), (0, "a"), (0, "f0out"))
        three_next = Second(spot, [three], [g])
        made = three_next.terms[:1] + four.first(three_next.terms[:1])
        z_early = offloaded_rest([one, two], made)
        back(0, "f0in", deps=made + two.terms, rest=[smalls[name] for name in order[1:]])
        five = group((0, "f0in"))
        z_three = along_z(spot, [three_next], [g, four.got], TAIL_WORK)
        made = five.first(z_three[:1])
        last = Second(spot, [four, five], made)
        z_last = along_z(spot, [last], z_three[1:])
        home = spread([act, filled(g)])
        chunks = gathered([[z_early], z_three, z_last], [home])
        *mats_out, small_out = finish(layers, me, [one, two, three, four, five], chunks, [])
        mats_out = [
            v.swapaxes(-1, -2) if turned else v for v, turned in zip(mats_out, (False, True, True, True, False, True))
        ]
        lines = small_out.reshape(-1, 4, 64).swapaxes(0, 1).reshape(-1, 64)
        starts = {name: 0 for name in order}
        at_row = 0
        smalls[0, "f0"] = smalls[0, "f0in"]
        for name in order:
            starts[name] = at_row
            at_row += smalls[name].shape[0]
        pieces = lambda name, first, count: [
            lines[starts[l, name] + first : starts[l, name] + first + count] for l in range(layers)
        ]
    else:
        for l in reversed(range(layers)):
            back(l, "f1", "c")
            back(l, "a", "f0")
        pieces = None
        home = spread([act, filled(g)])
    activations, frames_grad = unpacked(home)

    if not fast:
        mats_out, lines_of = general_sums(layers, members, smalls, order)
        pieces = lambda name, first, count: [lines_of[l, name][first : first + count] for l in range(layers)]
    gains_out = jnp.stack(
        [
            jnp.concatenate(rows, axis=0)
            for rows in zip(
                pieces("f0", 0, 1), pieces("a", 0, 1), pieces("c", 0, 1), pieces("f1", 0, 1), pieces("f1", 1, 1)
            )
        ]
    )
    fin, fout, ain, aout, pin, pout = mats_out
    return (
        activations,
        frames_grad,
        gains_out,
        fin,
        fout,
        ain,
        aout,
        pin,
        jnp.stack(pieces("c", 8, KERNEL)),
        jnp.concatenate(pieces("c", 1, 1), axis=0),
        jnp.concatenate(pieces("c", 2, 1), axis=0),
        pout,
    )


def general_sums(layers, members, smalls, order):
    def natural(l, name):
        _, even, odd = members[l, name]
        return jnp.stack([even, odd], axis=1).astype(F32).reshape(8, -1, LANES)

    def wide(v, count):
        r = v.shape[1] // count
        return jnp.swapaxes(v.reshape(8, count, r, LANES), 1, 2).reshape(8 * r, count * LANES)

    def over_all(v):
        v = lax.psum_scatter(v, "tm", scatter_dimension=v.ndim - 1, tiled=True)
        return lax.psum(v, "rows")

    fin, fout, ain, aout, pin, pout = [], [], [], [], [], []
    for l in range(layers):
        f = [natural(l, "f0"), natural(l, "f1")]
        fin.append(jnp.stack([jnp.moveaxis(v[:, :D], 0, 1).reshape(D, FF) for v in f]))
        fout.append(jnp.stack([wide(v[:, D:], FF // LANES).T for v in f]))
        v = natural(l, "a")
        ain.append(wide(v[:, :384], 2).T)
        aout.append(wide(v[:, 384:], 2).T)
        v = natural(l, "c")
        top = jnp.concatenate([v[:, :256, :128], v[:, :256, 128:]], axis=1)
        pin.append(jnp.moveaxis(top, 0, 1).reshape(D, 2 * D))
        pout.append(wide(v[:, 256:], 2).T)
    mats_out = [over_all(jnp.stack(v)) for v in (fin, fout, ain, aout, pin, pout)]
    small_all = over_all(jnp.concatenate([smalls[name] for name in order], axis=0))
    lines_of = {}
    at = 0
    for name in order:
        rows = smalls[name].shape[0]
        lines_of[name] = small_all[at : at + rows]
        at += rows
    return mats_out, lines_of


def solution(mesh):
    rep = P()
    in_specs = (
        P(None, "rows", "tm", None), P(None, "rows", "tm"), rep, rep, rep, rep, rep, rep, rep, rep, rep, rep, rep, rep,
        P(None, "rows", "tm", None),
    )
    out_specs = (
        P(None, "rows", "tm", None), P(None, "rows", "tm", None), P(None, None, "tm"), P(None, None, None, "tm"),
        P(None, None, None, "tm"), P(None, None, "tm"), P(None, None, "tm"), P(None, None, "tm"),
        P(None, None, "tm"), P(None, "tm"), P(None, "tm"), P(None, None, "tm"),
    )
    return jax.shard_map(per_device, mesh=mesh, in_specs=in_specs, out_specs=out_specs, check_vma=False)
```

```python
import functools

import jax
import jax.numpy as jnp
import numpy as np
from jax import lax
from jax.experimental import pallas as pl
from jax.experimental.pallas import tpu as pltpu
from jax.sharding import PartitionSpec as P

HD = 64
KERNEL = 9
HALO = 4
EPSILON = 1e-05
MASKED = -1e30
BF = jnp.bfloat16
F32 = jnp.float32
D = 512
FF = 2048
BLK = 128
ROW_CHOICES = (640, 1024)
CAP = ROW_CHOICES[-1]
LANES = 256
SMALL_ROWS = 128
TAIL_WORK = 3e10
PAIRS = D // 128
VMEM_LIMIT = 60 * 2**20
VMEM_SMALL = 24 * 2**20
ANY = pl.BlockSpec(memory_space=pl.ANY)
VMEM = pl.BlockSpec(memory_space=pltpu.VMEM)
SMEM = pl.BlockSpec(memory_space=pltpu.SMEM)


def shifted(array, axis, by):
    size = lax.axis_size(axis)
    pairs = [(i, i + by) for i in range(size) if 0 <= i + by < size]
    return lax.ppermute(array, axis, pairs)


def struct(shape, dtype):
    return jax.ShapeDtypeStruct(shape, dtype)


def call(body, ins, outs, scratch, args, flops=0, moved=0, name="kernel", deps=(), vmem=VMEM_LIMIT):
    count = len(ins)

    def inner(*refs):
        body(*refs[:count], *refs[count + len(deps) :])

    return pl.pallas_call(
        inner,
        out_shape=[s for s, _ in outs],
        in_specs=list(ins) + [ANY] * len(deps),
        out_specs=[b for _, b in outs],
        scratch_shapes=scratch,
        compiler_params=pltpu.CompilerParams(vmem_limit_bytes=vmem),
        cost_estimate=pl.CostEstimate(flops=int(flops), bytes_accessed=int(moved), transcendentals=0),
        name=name,
    )(*args, *deps)


def dot_nn(a, b):
    return jnp.dot(a, b, preferred_element_type=F32)


def dot_nt(a, b):
    return lax.dot_general(a, b, (((1,), (1,)), ((), ())), preferred_element_type=F32)


def dot_tn(a, b):
    return lax.dot_general(a, b, (((0,), (0,)), ((), ())), preferred_element_type=F32)


def sigmoid(v):
    return 0.5 + 0.5 * jnp.tanh(0.5 * v)


def normalise(x):
    c = x - jnp.mean(x, axis=-1, keepdims=True)
    inv = lax.rsqrt(jnp.mean(c * c, axis=-1, keepdims=True) + EPSILON)
    return c * inv, inv


def norm_back(grad, xhat, inv, gain):
    w = grad * gain
    return inv * (
        w - jnp.mean(w, axis=-1, keepdims=True) - xhat * jnp.mean(w * xhat, axis=-1, keepdims=True)
    )


def fold(v):
    return jnp.sum(v.reshape(v.shape[0] // 8, 8, v.shape[1]), axis=0)


def total(v):
    return jnp.sum(v, axis=0, keepdims=True)


def by_rows(n_ref, body):
    low = 0
    for rows in ROW_CHOICES:
        n = n_ref[0]
        cond = n > low
        if rows != CAP:
            cond = cond & (n <= rows)

        @pl.when(cond)
        def _(rows=rows):
            body(rows)

        low = rows


def blocks(rows, step, init=None, size=128):
    def wrapped(i, carry):
        at = pl.ds(pl.multiple_of(i * size, size), size)
        return step(i, at, carry)

    start = init if init is not None else jnp.int32(0)
    return lax.fori_loop(0, rows // size, wrapped, start, unroll=rows == ROW_CHOICES[0])


def each(count, rows, step):
    if rows == ROW_CHOICES[0]:
        for i in range(count):
            step(i)
    else:

        def wrapped(i, carry):
            step(i)
            return carry

        lax.fori_loop(0, count, wrapped, jnp.int32(0))


def cut(i, size):
    return pl.ds(i * size, size) if isinstance(i, int) else pl.ds(pl.multiple_of(i * size, size), size)


def rope_tables():
    half = HD // 2
    freq = np.power(np.float32(10000.0), -(np.arange(half).astype(np.float32) / np.float32(half)))
    angle = np.arange(BLK).astype(np.float32)[:, None] * freq.astype(np.float32)[None, :]
    cos = np.cos(angle.astype(np.float64))
    sin = np.sin(angle.astype(np.float64))
    full = (np.concatenate([cos] * 4, axis=1), np.concatenate([-sin, sin] * 2, axis=1))
    parts = []
    for table in full:
        rest = table
        for _ in range(3):
            piece = rest.astype(jnp.bfloat16)
            parts.append(piece)
            rest = rest - piece.astype(np.float64)
    return np.stack(parts)


def pack_body(
    ids_ref, frames_ref, cot_ref, below_ref, above_ref, tab_ref,
    x_ref, g_ref, p_ref, cos_ref, sin_ref, kb_ref, kr_ref, n_ref,
    keep_s, key_s, dest_s, pos_s, win_s, cot_s,
):
    batches = ids_ref.shape[0]
    half = batches // 2
    shown = (8, BLK)
    below_ids = below_ref[pl.ds(4 * BLK, 16), :].astype(F32)[0:1]
    above_ids = above_ref[pl.ds(4 * BLK, 16), :].astype(F32)[0:1]
    for m in range(batches):
        own = ids_ref[m : m + 1, :]
        below = below_ids[:, m * BLK : (m + 1) * BLK]
        above = above_ids[:, m * BLK : (m + 1) * BLK]
        i = m // 2
        mine = pl.ds(m * BLK, BLK)
        theirs = (pl.ds(i * BLK, BLK), pl.ds((half + i) * BLK, BLK))
        if m % 2 == 0:
            pieces = ((own, own != below[:, BLK - 1 : BLK]), (above, above == own[:, BLK - 1 : BLK]))
            frames = ((frames_ref, mine, cot_ref, mine), (above_ref, theirs[0], above_ref, theirs[1]))
        else:
            pieces = ((below, below == own[:, 0:1]), (own, own != above[:, 0:1]))
            frames = ((below_ref, theirs[0], below_ref, theirs[1]), (frames_ref, mine, cot_ref, mine))
        for j in range(2):
            at = pl.ds((2 * m + j) * BLK, BLK)
            key_s[:, at] = jnp.broadcast_to(pieces[j][0] + 4096.0 * m, shown)
            keep_s[:, at] = jnp.broadcast_to(jnp.where(pieces[j][1], 1.0, 0.0), shown)
            src, rows, cot, cot_rows = frames[j]
            win_s[at, :] = src[rows, :]
            cot_s[at, :] = cot[cot_rows, :]
    square = (BLK, BLK)
    earlier = lax.broadcasted_iota(jnp.int32, square, 0) < lax.broadcasted_iota(jnp.int32, square, 1)
    ramp = earlier.astype(F32).astype(BF)
    before = jnp.zeros((8, 1), F32)
    for j in range(2 * batches):
        at = pl.ds(j * BLK, BLK)
        keep = keep_s[:, at]
        dest_s[:, at] = jnp.where(keep > 0.5, before + dot_nn(keep.astype(BF), ramp), -1.0)
        before = before + jnp.sum(keep, axis=1, keepdims=True)
    n = (jnp.sum(before) * 0.125 + 0.5).astype(jnp.int32)
    n_ref[0] = n
    for m in range(batches):
        first, second = pl.ds(2 * m * BLK, BLK), pl.ds((2 * m + 1) * BLK, BLK)
        cols = [jnp.broadcast_to(key_s[0:1, at], square).T for at in (first, second)]
        count = lambda mask: jnp.broadcast_to(jnp.sum(jnp.where(mask, 1.0, 0.0), axis=0, keepdims=True), shown)
        pos_s[:, first] = count((cols[0] == key_s[0:1, first]) & earlier)
        pos_s[:, second] = count(cols[0] == key_s[0:1, second]) + count((cols[1] == key_s[0:1, second]) & earlier)
    kr_ref[...] = jnp.full(kr_ref.shape, -1.0, F32)
    rows_all = 2 * batches * BLK

    def step(i, at):
        row = (lax.broadcasted_iota(jnp.int32, (BLK, rows_all), 0) + i * BLK).astype(F32)
        pick = jnp.where(dest_s[0:1, :] == row, 1.0, 0.0)
        p = pick.astype(BF)
        p_ref[at, :] = p
        x_ref[at, :] = dot_nn(p, win_s[...])
        g_ref[at, :] = dot_nn(p, cot_s[...])
        key = jnp.broadcast_to(jnp.sum(pick * key_s[0:1, :], axis=1, keepdims=True), square)
        kb_ref[at, :] = key
        kr_ref[:, pl.ds(i * BLK + BLK, BLK)] = key.T[0:8]
        pos = jnp.sum(pick * pos_s[0:1, :], axis=1, keepdims=True)
        hot = (lax.broadcasted_iota(jnp.int32, square, 1).astype(F32) == pos).astype(F32).astype(BF)
        cos_ref[at, :] = dot_nn(hot, tab_ref[0]) + dot_nn(hot, tab_ref[1]) + dot_nn(hot, tab_ref[2])
        sin_ref[at, :] = dot_nn(hot, tab_ref[3]) + dot_nn(hot, tab_ref[4]) + dot_nn(hot, tab_ref[5])

    for i in range(rows_all // BLK):
        at = pl.ds(i * BLK, BLK)
        if i * BLK < ROW_CHOICES[0]:
            step(i, at)
        else:

            @pl.when(n > ROW_CHOICES[0])
            def _(i=i, at=at):
                step(i, at)

            @pl.when(n <= ROW_CHOICES[0])
            def _(at=at):
                p_ref[at, :] = jnp.zeros((BLK, rows_all), BF)


def pack(ids, frames, cotangent, below, above):
    vm = pltpu.VMEM
    return call(
        pack_body,
        [VMEM] * 6,
        [
            (struct((CAP, D), F32), VMEM),
            (struct((CAP, D), F32), VMEM),
            (struct((CAP, CAP), BF), VMEM),
            (struct((CAP, 128), F32), VMEM),
            (struct((CAP, 128), F32), VMEM),
            (struct((CAP, 128), F32), VMEM),
            (struct((8, CAP + 2 * BLK), F32), VMEM),
            (struct((1,), jnp.int32), SMEM),
        ],
        [vm((8, CAP), F32), vm((8, CAP), F32), vm((8, CAP), F32), vm((8, CAP), F32), vm((CAP, D), BF), vm((CAP, D), BF)],
        (ids, frames, cotangent, below, above, jnp.asarray(rope_tables(), dtype=BF)),
        flops=4 * CAP * CAP * D,
        moved=12 * 2**20,
        name="pack",
    )


def lane_low(shape):
    return lax.broadcasted_iota(jnp.int32, shape, 1) % HD < HD // 2


def swap_halves(v):
    return jnp.where(lane_low(v.shape), pltpu.roll(v, 128 - HD // 2, 1), pltpu.roll(v, HD // 2, 1))


def stacked(v):
    first = lax.broadcasted_iota(jnp.int32, v.shape, 1) < HD
    zero = jnp.zeros_like(v)
    return jnp.concatenate([jnp.where(first, v, zero), jnp.where(first, zero, v)], axis=0)


def unstacked(v):
    half = v.shape[0] // 2
    first = lax.broadcasted_iota(jnp.int32, (half, 128), 1) < HD
    return jnp.where(first, v[:half], v[half:])


def norm_into(x_ref, gain, a_ref, rows):
    def step(i, at, carry):
        xhat, _ = normalise(x_ref[at, :])
        a_ref[at, :] = (xhat * gain).astype(BF)
        return carry

    blocks(rows, step)


def forward_body(
    n_ref, x0_ref, cos_ref, sin_ref, kb_ref, kr_ref, gains_ref, taps_ref, mean_ref, var_ref, scale_ref, shift_ref,
    fin_h, fout_h, ain_h, aout_h, pin_h, pout_h,
    act_ref, xs_h, hs_h, q_h, kv_h, at_h, o_h, u_h, z_h,
    fin, fout, ain, aout, pin, pout, xb, hb, qb, kvb, ab, ob, ub, zb, a_s, gp, kp, w_sem, s_sem,
):
    layers = gains_ref.shape[0]
    weights = [
        (fin_h, (0,), fin.at[0]), (fout_h, (0,), fout.at[0]), (ain_h, (), ain), (aout_h, (), aout),
        (pin_h, (), pin), (pout_h, (), pout), (fin_h, (1,), fin.at[1]), (fout_h, (1,), fout.at[1]),
    ]

    def weight_copy(i, l):
        src, sub, dst = weights[i]
        return pltpu.make_async_copy(src.at[(l,) + sub], dst, w_sem.at[i])

    for i in (0, 1):
        weight_copy(i, 0).start()

    def run(rows):
        tiles = rows // BLK
        top = pl.ds(0, rows)
        saves = [(xb.at[i, top], lambda l, i=i: xs_h.at[l, i, top]) for i in range(5)]
        saves += [(hb.at[k, top], lambda l, k=k: hs_h.at[l, k, top]) for k in range(2)]
        saves += [
            (qb.at[top], lambda l: q_h.at[l, top]),
            (kvb.at[pl.ds(0, rows + 2 * BLK)], lambda l: kv_h.at[l, pl.ds(0, rows + 2 * BLK)]),
            (ab.at[pl.ds(0, tiles)], lambda l: at_h.at[l, pl.ds(0, tiles)]),
            (ob.at[top], lambda l: o_h.at[l, top]),
            (ub.at[top], lambda l: u_h.at[l, top]),
            (zb.at[top], lambda l: z_h.at[l, top]),
        ]

        def save(i, l):
            src, dst = saves[i]
            return pltpu.make_async_copy(src, dst(l), s_sem.at[i])

        def settle(i, l):
            @pl.when(l > 0)
            def _():
                save(i, l - 1).wait()

        def use(i, l):
            weight_copy(i, l).wait()

        def next_weight(i, l):
            @pl.when(l + 1 < layers)
            def _():
                weight_copy(i, l + 1).start()

        kvb[pl.ds(0, BLK), :] = jnp.zeros((BLK, 2 * D), BF)
        kvb[pl.ds(rows + BLK, BLK), :] = jnp.zeros((BLK, 2 * D), BF)
        gp[:, pl.ds(0, 8), :] = jnp.zeros((PAIRS, 8, 128), F32)
        gp[:, pl.ds(rows + 8, 8), :] = jnp.zeros((PAIRS, 8, 128), F32)
        kp[pl.ds(0, BLK), :] = jnp.full((BLK, 128), -1.0, F32)
        kp[pl.ds(rows + BLK, BLK), :] = jnp.full((BLK, 128), -1.0, F32)

        def fill(i, at, carry):
            kp[pl.ds(pl.multiple_of(i * BLK + BLK, BLK), BLK), :] = kb_ref[at, :]
            xb[0, at, :] = x0_ref[at, :]
            return carry

        blocks(rows, fill)

        def feed(l, k, src, dst, gain, wi, early=lambda: None):
            settle(5 + k, l)
            settle(dst, l)

            def first(i, at, carry):
                x = xb[src, at, :]
                xhat, _ = normalise(x)
                a_s[at, :] = (xhat * gain).astype(BF)
                xb[dst, at, :] = x
                return carry

            blocks(rows, first)
            use(wi, l)
            use(wi + 1, l)
            early()

            def chunk(c):
                cols = cut(c, 512)
                h = dot_nn(a_s[top, :], fin[k, :, cols])
                hb[k, top, cols] = h.astype(BF)
                s = (h * sigmoid(h)).astype(BF)
                xb[dst, top, :] = xb[dst, top, :] + 0.5 * dot_nn(s, fout[k, cols, :])

            each(FF // 512, rows, chunk)
            next_weight(wi, l)
            next_weight(wi + 1, l)
            save(5 + k, l).start()
            save(dst, l).start()

        def first_weights(l, which):
            @pl.when(l == 0)
            def _():
                for i in which:
                    weight_copy(i, 0).start()

        def layer(l, carry):
            gains = [gains_ref[l, pl.ds(i, 1), :] for i in range(5)]
            save(0, l).start()
            feed(l, 0, 0, 1, gains[0], 0, lambda: first_weights(l, (2, 3)))
            first_weights(l, (4, 5, 6, 7))

            norm_into(xb.at[1], gains[1], a_s, rows)
            settle(7, l)
            settle(8, l)
            settle(9, l)
            settle(10, l)
            use(2, l)
            for part in range(3):
                proj = dot_nn(a_s[top, :], ain[:, part * D : (part + 1) * D])
                for p in range(PAIRS):
                    lanes = slice(p * 128, (p + 1) * 128)
                    v = proj[:, lanes]
                    if part < 2:
                        v = v * cos_ref[top, :] + swap_halves(v) * sin_ref[top, :]
                    if part == 0:
                        qb[top, lanes] = (v * HD**-0.5).astype(BF)
                    elif part == 1:
                        kvb[pl.ds(BLK, rows), lanes] = v.astype(BF)
                    else:
                        kvb[pl.ds(BLK, rows), D + p * 128 : D + (p + 1) * 128] = v.astype(BF)
            next_weight(2, l)

            def tile(t, at, c):
                near = pl.ds(pl.multiple_of(t * BLK, BLK), 3 * BLK)
                same = kp[near, :] == kr_ref[0:1, pl.ds(pl.multiple_of(t * BLK + BLK, BLK), BLK)]
                same = jnp.concatenate([same, same], axis=1)
                for p in range(PAIRS):
                    lanes = slice(p * 128, (p + 1) * 128)
                    s = dot_nt(kvb[near, lanes], stacked(qb[at, lanes]))
                    s = jnp.where(same, s, MASKED)
                    e = jnp.exp(s - jnp.max(s, axis=0, keepdims=True))
                    low = (e * (1.0 / jnp.sum(e, axis=0, keepdims=True))).astype(BF)
                    ab[t, p] = low
                    o = dot_tn(low, kvb[near, D + p * 128 : D + (p + 1) * 128])
                    ob[at, lanes] = unstacked(o).astype(BF)
                return c

            blocks(rows, tile)
            settle(2, l)
            use(3, l)
            xb[2, top, :] = xb[1, top, :] + dot_nn(ob[top, :], aout[...])
            next_weight(3, l)
            for i in (7, 8, 9, 10, 2):
                save(i, l).start()

            norm_into(xb.at[2], gains[2], a_s, rows)
            settle(11, l)
            settle(12, l)
            use(4, l)
            for half in range(2):
                lanes = slice(half * 256, (half + 1) * 256)
                up1 = dot_nn(a_s[top, :], pin[:, half * 256 : (half + 1) * 256])
                up2 = dot_nn(a_s[top, :], pin[:, D + half * 256 : D + (half + 1) * 256])
                ub[top, lanes] = up1.astype(BF)
                ub[top, D + half * 256 : D + (half + 1) * 256] = up2.astype(BF)
                gated = (up1 * sigmoid(up2)).astype(BF).astype(F32)
                for q in range(2):
                    gp[2 * half + q, pl.ds(8, rows), :] = gated[:, q * 128 : (q + 1) * 128]
            next_weight(4, l)
            rs = lax.rsqrt(var_ref[pl.ds(l, 1), :] + EPSILON)
            mean = mean_ref[pl.ds(l, 1), :]
            scale = scale_ref[pl.ds(l, 1), :]
            shift = shift_ref[pl.ds(l, 1), :]

            def conv(t, at, c):
                near = [pl.ds(t * BLK + 4 + o, BLK) for o in range(KERNEL)]
                own = kb_ref[at, :]
                masks = [kp[pl.ds(t * BLK + BLK - HALO + o, BLK), :] == own for o in range(KERNEL)]
                for p in range(PAIRS):
                    lanes = slice(p * 128, (p + 1) * 128)
                    z = jnp.zeros((BLK, 128), F32)
                    for o in range(KERNEL):
                        w = taps_ref[l, o : o + 1, lanes]
                        z = z + jnp.where(masks[o], w * gp[p, near[o], :], 0.0)
                    zb[at, lanes] = z
                    b = (z - mean[:, lanes]) * rs[:, lanes] * scale[:, lanes] + shift[:, lanes]
                    a_s[at, lanes] = (b * sigmoid(b)).astype(BF)
                return c

            blocks(rows, conv)
            settle(3, l)
            use(5, l)
            xb[3, top, :] = xb[2, top, :] + dot_nn(a_s[top, :], pout[...])
            next_weight(5, l)
            for i in (11, 12, 3):
                save(i, l).start()

            feed(l, 1, 3, 4, gains[3], 6)
            save(0, l).wait()

            def last(i, at, c):
                xhat, _ = normalise(xb[4, at, :])
                y = xhat * gains[4]
                xb[0, at, :] = y
                act_ref[at, :] = y.astype(BF)
                return c

            blocks(rows, last)
            return carry

        lax.fori_loop(0, layers, layer, jnp.int32(0))
        for i in range(1, len(saves)):
            save(i, layers - 1).wait()
        if rows < CAP:
            act_ref[pl.ds(rows, CAP - rows), :] = jnp.zeros((CAP - rows, D), BF)

    by_rows(n_ref, run)


def forward(n, x0, cos, sin, kb, kr, small, mats):
    layers = small[0].shape[0]
    outs = [
        (struct((CAP, D), BF), VMEM),
        (struct((layers, 5, CAP, D), F32), ANY),
        (struct((layers, 2, CAP, FF), BF), ANY),
        (struct((layers, CAP, D), BF), ANY),
        (struct((layers, CAP + 2 * BLK, 2 * D), BF), ANY),
        (struct((layers, CAP // BLK, PAIRS, 3 * BLK, 2 * BLK), BF), ANY),
        (struct((layers, CAP, D), BF), ANY),
        (struct((layers, CAP, 2 * D), BF), ANY),
        (struct((layers, CAP, D), F32), ANY),
    ]
    vm = pltpu.VMEM
    scratch = [
        vm((2, D, FF), BF), vm((2, FF, D), BF), vm((D, 3 * D), BF), vm((D, D), BF), vm((D, 2 * D), BF), vm((D, D), BF),
        vm((5, CAP, D), F32), vm((2, CAP, FF), BF), vm((CAP, D), BF), vm((CAP + 2 * BLK, 2 * D), BF),
        vm((CAP // BLK, PAIRS, 3 * BLK, 2 * BLK), BF), vm((CAP, D), BF), vm((CAP, 2 * D), BF), vm((CAP, D), F32),
        vm((CAP, D), BF), vm((PAIRS, CAP + 16, 128), F32), vm((CAP + 2 * BLK, 128), F32),
        pltpu.SemaphoreType.DMA((8,)), pltpu.SemaphoreType.DMA((13,)),
    ]
    return call(
        forward_body,
        [SMEM] + [VMEM] * 11 + [ANY] * 6,
        outs,
        scratch,
        (n, x0, cos, sin, kb, kr, *small, *mats),
        flops=2 * 640 * 12e6,
        moved=60 * 2**20,
        name="forward",
    )


class Out:
    def __init__(self, core, buf, kept_h, sent_h, sem):
        self.core = core
        self.buf = buf
        self.homes = (kept_h, sent_h)
        self.sem = sem

    def put(self, at, pair):
        self.buf[(self.core,) + at] = pair[0].astype(BF)
        self.buf[(1 - self.core,) + at] = pair[1].astype(BF)

    def copies(self, slot, at):
        return [
            pltpu.make_async_copy(self.buf.at[(i,) + at], home.at[at], self.sem.at[2 * slot + i])
            for i, home in enumerate(self.homes)
        ]

    def send(self, slot, at):
        for c in self.copies(slot, at):
            c.start()

    def wait(self, slot, at):
        for c in self.copies(slot, at):
            c.wait()


def transposed_out(out, dwo, first):
    for z in range(4):
        for b in range(dwo.shape[1] // LANES):
            pair = [dwo[z * 128 + q * 64 : z * 128 + q * 64 + 64, b * LANES : (b + 1) * LANES] for q in range(2)]
            out.put((z, first(b), slice(None)), pair)


def feed_part(l, k, what, core_ref, g_s, ins, outs, scratch):
    final = k == 1
    do_out, do_in = what != "in", what != "out"
    base = D if do_in else 0
    gains_ref, xs_h, hs_h, fin_h, fout_h, *small_refs = ins
    others = len(small_refs)
    keep_h, send_h, small_ref = outs
    x_s, x4_s, h_s, fin, fout, gl_s, a_s, da_s, buf, sem, osem = scratch
    gain = gains_ref[l, pl.ds(3 if final else 0, 1), :]
    gain4 = gains_ref[l, pl.ds(4, 1), :]
    out = Out(core_ref[0], buf, keep_h, send_h, osem)
    every = pl.ds(0, 4)
    high = base + FF * D // (8 * LANES) if do_out else D

    def run(rows):
        top = pl.ds(0, rows)

        def chunk_in(c):
            cols = cut(c, 512)
            made = [pltpu.make_async_copy(hs_h.at[l, k, top, cols], h_s.at[top, cols], sem.at[3 + 3 * c])]
            if do_in:
                made += [
                    pltpu.make_async_copy(fout_h.at[l, k, cols], fout.at[cols], sem.at[4 + 3 * c]),
                    pltpu.make_async_copy(fin_h.at[l, k, :, cols], fin.at[:, cols], sem.at[5 + 3 * c]),
                ]
            return made

        starts = []
        if do_in:
            starts.append(pltpu.make_async_copy(xs_h.at[l, 3 if final else 0, top], x_s.at[top], sem.at[1]))
        if final:
            starts.insert(0, pltpu.make_async_copy(xs_h.at[l, 4, top], x4_s.at[top], sem.at[2]))

        def start():
            for c in starts + chunk_in(0):
                c.start()

        def first(i, at, carry):
            g = g_s[at, :]
            if final:
                xhat, inv = normalise(x4_s[at, :])
                carry = carry + fold(g * xhat)
                g = norm_back(g, xhat, inv, gain4)
                g_s[at, :] = g
            gl_s[at, :] = (0.5 * g).astype(BF)
            if do_in:
                xhat, _ = normalise(x_s[at, :])
                a_s[at, :] = (xhat * gain).astype(BF)
                da_s[at, :] = jnp.zeros((BLK, D), F32)
            return carry

        def low_rows(c):
            low = base + c * 128
            return pl.ds(low, 128) if isinstance(c, int) else pl.ds(pl.multiple_of(low, 128), 128)

        def spots(c):
            return [(c, pl.ds(0, D))] * do_in + [(every, low_rows(c))] * do_out

        def chunk(c):
            cols = cut(c, 512)
            for copy in chunk_in(c):
                copy.wait()
            if isinstance(c, int):
                for copy in chunk_in(c + 2) if c < 2 else []:
                    copy.start()
            else:

                @pl.when(c < 2)
                def _():
                    for copy in chunk_in(c + 2):
                        copy.start()

            h = h_s[top, cols].astype(F32)
            sig = sigmoid(h)
            if do_in:
                ds = dot_nt(gl_s[top, :], fout[cols, :])
                dh = (ds * (sig * (1.0 + h * (1.0 - sig)))).astype(BF)
                dwi = dot_tn(a_s[top, :], dh)
                out.put((c, pl.ds(0, D), slice(None)), (dwi[:, :LANES], dwi[:, LANES:]))
            if do_out:
                dwo = dot_tn(gl_s[top, :], (h * sig).astype(BF))
                step = lambda b: (base + (2 * c + b) * 64)
                transposed_out(
                    out, dwo,
                    lambda b: pl.ds(step(b), 64) if isinstance(c, int) else pl.ds(pl.multiple_of(step(b), 64), 64),
                )
            for i, at in enumerate(spots(c)):
                out.send(2 * c + i, at)
            if do_in:
                da_s[top, :] = da_s[top, :] + dot_nt(dh, fin[:, cols])

        def last(i, at, carry):
            xhat, inv = normalise(x_s[at, :])
            da = da_s[at, :]
            g_s[at, :] = g_s[at, :] + norm_back(da, xhat, inv, gain)
            return carry + fold(da * xhat)

        def small_chunks():
            buf[:, :, pl.ds(high, SMALL_ROWS), :] = jnp.zeros((2, 4, SMALL_ROWS, LANES), BF)
            rows_all = jnp.concatenate([small_ref[...]] + [ref[...] for ref in small_refs], axis=0)
            lines = SMALL_ROWS // 4
            rows_all = jnp.concatenate([rows_all, jnp.zeros((4 * lines - rows_all.shape[0], D), F32)], axis=0)
            for z in range(4):
                pair = []
                for q in range(2):
                    own = rows_all[:, z * 128 + q * 64 : z * 128 + q * 64 + 64]
                    pair.append(jnp.concatenate([own[i * lines : (i + 1) * lines] for i in range(4)], axis=1))
                out.put((z, pl.ds(high, lines), slice(None)), pair)

        low_spot = (every, pl.ds(high, SMALL_ROWS))

        def main(midway):
            for c in starts:
                c.wait()
            for c in chunk_in(1):
                c.start()
            midway()
            gain4_grad = blocks(rows, first, jnp.zeros((8, D), F32))
            each(FF // 512, rows, chunk)
            small_ref[...] = jnp.zeros(small_ref.shape, F32)
            if do_in:
                small_ref[0:1, :] = total(blocks(rows, last, jnp.zeros((8, D), F32)))
            small_ref[1:2, :] = total(gain4_grad)
            if others:
                small_chunks()
                out.send(8, low_spot)

        def finish():
            if others:
                out.wait(8, low_spot)
            for c in range(4):
                for i, at in enumerate(spots(c)):
                    out.wait(2 * c + i, at)

        return start, main, finish

    return run


def feed_spec(l, k, what, smalls, gains, xs, hs, fin, fout):
    vm = pltpu.VMEM
    do_out, do_in = what != "in", what != "out"
    lines = D * do_in + D * do_out + (SMALL_ROWS if smalls else 0)
    none = (8, D)
    return (
        functools.partial(feed_part, l, k, what),
        [(gains, VMEM), (xs, ANY), (hs, ANY), (fin, ANY), (fout, ANY)] + [(v, VMEM) for v in smalls],
        [
            (struct((4, lines, LANES), BF), ANY),
            (struct((4, lines, LANES), BF), ANY),
            (struct((8, D), F32), VMEM),
        ],
        [
            vm((CAP, D) if do_in else none, F32), vm((CAP, D) if k == 1 else none, F32), vm((CAP, FF), BF),
            vm((D, FF) if do_in else none, BF), vm((FF, D) if do_in else none, BF), vm((CAP, D), BF),
            vm((CAP, D) if do_in else none, BF), vm((CAP, D) if do_in else none, F32),
            vm((2, 4, lines, LANES), BF),
            pltpu.SemaphoreType.DMA((15,)), pltpu.SemaphoreType.DMA((18,)),
        ],
        (2 * do_out + 6 * do_in) * 640 * D * FF,
    )


def conv_part(l, core_ref, g_s, ins, outs, scratch):
    kb_ref, gains_ref, taps_ref, mean_ref, var_ref, scale_ref, shift_ref, xs_h, u_h, z_h, pin_h, pout_h = ins
    keep_h, send_h, small_ref = outs
    x_s, u_s, z_s, pin, pout, gl_s, a_s, e_s, de_s, gp, dzp, kp, du_s, buf, sem, osem = scratch
    gain = gains_ref[l, pl.ds(2, 1), :]
    rs = lax.rsqrt(var_ref[pl.ds(l, 1), :] + EPSILON)
    mean = mean_ref[pl.ds(l, 1), :]
    scale = scale_ref[pl.ds(l, 1), :]
    shift = shift_ref[pl.ds(l, 1), :]
    out = Out(core_ref[0], buf, keep_h, send_h, osem)
    every = pl.ds(0, 4)

    def run(rows):
        top = pl.ds(0, rows)
        copies = [
            None,
            pltpu.make_async_copy(pout_h.at[l], pout, sem.at[1]),
            pltpu.make_async_copy(z_h.at[l, top], z_s.at[top], sem.at[2]),
            pltpu.make_async_copy(u_h.at[l, top], u_s.at[top], sem.at[3]),
            pltpu.make_async_copy(xs_h.at[l, 2, top], x_s.at[top], sem.at[4]),
            pltpu.make_async_copy(pin_h.at[l], pin, sem.at[5]),
        ]
        low_spot = (every, pl.ds(256, 128))
        high_spot = (every, pl.ds(0, 256))

        def start():
            for c in copies[1:4]:
                c.start()

        def finish():
            out.wait(0, low_spot)
            out.wait(1, high_spot)

        return start, functools.partial(conv_work, rows, copies), finish

    def conv_work(rows, copies, midway):
        top = pl.ds(0, rows)
        low_spot = (every, pl.ds(256, 128))
        high_spot = (every, pl.ds(0, 256))
        for ref in (gp, dzp):
            ref[:, pl.ds(0, 8), :] = jnp.zeros((PAIRS, 8, 128), F32)
            ref[:, pl.ds(rows + 8, 8), :] = jnp.zeros((PAIRS, 8, 128), F32)
        kp[pl.ds(0, 8), :] = jnp.full((8, 128), -1.0, F32)
        kp[pl.ds(rows + 8, 8), :] = jnp.full((8, 128), -1.0, F32)

        def low(i, at, carry):
            gl_s[at, :] = g_s[at, :].astype(BF)
            kp[pl.ds(pl.multiple_of(i * BLK + 8, 8), BLK), :] = kb_ref[at, :]
            return carry

        blocks(rows, low)
        for c in copies[1:4]:
            c.wait()
        for c in copies[4:]:
            c.start()
        midway()
        de_s[top, :] = dot_nt(gl_s[top, :], pout[...])
        copies[4].wait()

        def first(i, at, carry):
            scale_grad, shift_grad = carry
            inner = pl.ds(pl.multiple_of(i * BLK + 8, 8), BLK)
            hat = (z_s[at, :] - mean) * rs
            b = hat * scale + shift
            sig = sigmoid(b)
            e_s[at, :] = (b * sig).astype(BF)
            db = de_s[at, :] * (sig * (1.0 + b * (1.0 - sig)))
            dz = (db * scale * rs).astype(BF).astype(F32)
            u1 = u_s[at, pl.ds(0, D)].astype(F32)
            u2 = u_s[at, pl.ds(D, D)].astype(F32)
            gated = (u1 * sigmoid(u2)).astype(BF).astype(F32)
            for p in range(PAIRS):
                dzp[p, inner, :] = dz[:, p * 128 : (p + 1) * 128]
                gp[p, inner, :] = gated[:, p * 128 : (p + 1) * 128]
            xhat, _ = normalise(x_s[at, :])
            a_s[at, :] = (xhat * gain).astype(BF)
            return (scale_grad + fold(db * hat), shift_grad + fold(db))

        zero = jnp.zeros((8, D), F32)
        scale_grad, shift_grad = blocks(rows, first, (zero, zero))
        small_ref[...] = jnp.zeros(small_ref.shape, F32)
        small_ref[1:2, :] = total(scale_grad)
        small_ref[2:3, :] = total(shift_grad)
        dwo = dot_tn(gl_s[top, :], e_s[top, :])
        transposed_out(out, dwo, lambda b: pl.ds(256 + b * 64, 64))
        out.send(0, low_spot)

        for p in range(PAIRS):
            lanes = slice(p * 128, (p + 1) * 128)

            def taps(t, at, carry, lanes=lanes, p=p):
                own = kb_ref[at, :]
                dz_own = dzp[p, pl.ds(pl.multiple_of(t * BLK + 8, 8), BLK), :]
                dg = jnp.zeros((BLK, 128), F32)
                sums = []
                for o in range(KERNEL):
                    near = pl.ds(t * BLK + 4 + o, BLK)
                    mask = kp[near, :] == own
                    sums.append(carry[o] + fold(jnp.where(mask, dz_own * gp[p, near, :], 0.0)))
                    w = taps_ref[l, KERNEL - 1 - o : KERNEL - o, lanes]
                    dg = dg + jnp.where(mask, w * dzp[p, near, :], 0.0)
                u1 = u_s[at, lanes].astype(F32)
                sig = sigmoid(u_s[at, D + p * 128 : D + (p + 1) * 128].astype(F32))
                du_s[at, lanes] = (dg * sig).astype(BF)
                du_s[at, D + p * 128 : D + (p + 1) * 128] = (dg * u1 * sig * (1.0 - sig)).astype(BF)
                return tuple(sums)

            sums = blocks(rows, taps, tuple(jnp.zeros((8, 128), F32) for _ in range(KERNEL)))
            for o in range(KERNEL):
                small_ref[8 + o : 9 + o, lanes] = total(sums[o])

        for half in range(2):
            dwi = dot_tn(a_s[top, :], du_s[top, half * 512 : (half + 1) * 512])
            for q in range(2):
                pair = [
                    jnp.concatenate([dwi[: D // 2, at : at + 128], dwi[D // 2 :, at : at + 128]], axis=1)
                    for at in (q * 256, q * 256 + 128)
                ]
                out.put((2 * half + q, pl.ds(0, 256), slice(None)), pair)
        out.send(1, high_spot)
        copies[5].wait()
        de_s[top, :] = dot_nt(du_s[top, :], pin[...])

        def last(i, at, carry):
            xhat, inv = normalise(x_s[at, :])
            da = de_s[at, :]
            g_s[at, :] = g_s[at, :] + norm_back(da, xhat, inv, gain)
            return carry + fold(da * xhat)

        small_ref[0:1, :] = total(blocks(rows, last, zero))

    return run


def conv_spec(l, kb, small, xs, u, z, pin, pout):
    vm = pltpu.VMEM
    return (
        functools.partial(conv_part, l),
        [(kb, VMEM)] + [(v, VMEM) for v in small] + [(v, ANY) for v in (xs, u, z, pin, pout)],
        [
            (struct((4, 384, LANES), BF), ANY),
            (struct((4, 384, LANES), BF), ANY),
            (struct((24, D), F32), VMEM),
        ],
        [
            vm((CAP, D), F32), vm((CAP, 2 * D), BF), vm((CAP, D), F32), vm((D, 2 * D), BF),
            vm((D, D), BF), vm((CAP, D), BF), vm((CAP, D), BF), vm((CAP, D), BF), vm((CAP, D), F32),
            vm((PAIRS, CAP + 16, 128), F32), vm((PAIRS, CAP + 16, 128), F32), vm((CAP + 16, 128), F32),
            vm((CAP, 2 * D), BF), vm((2, 4, 384, LANES), BF),
            pltpu.SemaphoreType.DMA((6,)), pltpu.SemaphoreType.DMA((4,)),
        ],
        12 * 640 * D * D,
    )


def attend_part(l, core_ref, g_s, ins, outs, scratch):
    cos_ref, sin_ref, gains_ref, xs_h, q_h, kv_h, at_h, o_h, ain_h, aout_h = ins
    keep_h, send_h, small_ref = outs
    x_s, q_s, kv_s, at_s, o_s, ain, aout, gl_s, a_s, do_s, dq_s, dkv_s, dp_s, da_s, buf, sem, osem = scratch
    out = Out(core_ref[0], buf, keep_h, send_h, osem)
    every = pl.ds(0, 4)
    gain = gains_ref[l, pl.ds(1, 1), :]

    def run(rows):
        tiles = rows // BLK
        top = pl.ds(0, rows)
        wide = pl.ds(0, rows + 2 * BLK)
        copies = [
            pltpu.make_async_copy(aout_h.at[l], aout, sem.at[0]),
            pltpu.make_async_copy(o_h.at[l, top], o_s.at[top], sem.at[1]),
            pltpu.make_async_copy(q_h.at[l, top], q_s.at[top], sem.at[2]),
            pltpu.make_async_copy(kv_h.at[l, wide], kv_s.at[wide], sem.at[3]),
            pltpu.make_async_copy(xs_h.at[l, 1, top], x_s.at[top], sem.at[5]),
            pltpu.make_async_copy(ain_h.at[l], ain, sem.at[6]),
        ]
        copies = [None] + copies

        def weights_in(t):
            return pltpu.make_async_copy(at_h.at[l, t], at_s.at[t], sem.at[8 + t])

        low_spot = (every, pl.ds(384, 128))
        high_spot = (every, pl.ds(0, 384))

        def start():
            for c in copies[1:5]:
                c.start()
            weights_in(0).start()

        def finish():
            out.wait(0, low_spot)
            out.wait(1, high_spot)

        return start, functools.partial(attend_work, rows, copies, weights_in), finish

    def attend_work(rows, copies, weights_in, midway):
        tiles = rows // BLK
        top = pl.ds(0, rows)
        low_spot = (every, pl.ds(384, 128))
        high_spot = (every, pl.ds(0, 384))

        def low(i, at, carry):
            gl_s[at, :] = g_s[at, :].astype(BF)
            return carry

        blocks(rows, low)

        def clear(i, at, carry):
            dkv_s[at, :] = jnp.zeros((BLK, 2 * D), F32)
            return carry

        blocks(rows + 2 * BLK, clear)
        copies[1].wait()
        do_s[top, :] = dot_nt(gl_s[top, :], aout[...]).astype(BF)
        for c in copies[2:5]:
            c.wait()
        for c in copies[5:]:
            c.start()
        midway()

        def tile(t, at, carry):
            near = pl.ds(pl.multiple_of(t * BLK, BLK), 3 * BLK)
            weights_in(t).wait()

            @pl.when(t + 1 < tiles)
            def _():
                weights_in(t + 1).start()

            for p in range(PAIRS):
                lanes = slice(p * 128, (p + 1) * 128)
                vlanes = slice(D + p * 128, D + (p + 1) * 128)
                do = stacked(do_s[at, lanes])
                low = at_s[t, p]
                weights = low.astype(F32)
                da = dot_nt(kv_s[near, vlanes], do)
                delta = jnp.sum(weights * da, axis=0, keepdims=True)
                ds = (weights * (da - delta)).astype(BF)
                dq_s[at, lanes] = unstacked(dot_tn(ds, kv_s[near, lanes])) * HD**-0.5
                dkv_s[near, lanes] = dkv_s[near, lanes] + dot_nn(ds, stacked(q_s[at, lanes]))
                dkv_s[near, vlanes] = dkv_s[near, vlanes] + dot_nn(low, do)
            return carry

        blocks(rows, tile)
        copies[5].wait()

        def turn(i, at, carry):
            inner = pl.ds(pl.multiple_of(i * BLK + BLK, BLK), BLK)
            cos, sin = cos_ref[at, :], sin_ref[at, :]
            for p in range(PAIRS):
                lanes = slice(p * 128, (p + 1) * 128)
                dq = dq_s[at, lanes]
                dk = dkv_s[inner, lanes]
                dp_s[at, lanes] = (dq * cos - swap_halves(dq) * sin).astype(BF)
                dp_s[at, D + p * 128 : D + (p + 1) * 128] = (dk * cos - swap_halves(dk) * sin).astype(BF)
                dp_s[at, 2 * D + p * 128 : 2 * D + (p + 1) * 128] = dkv_s[
                    inner, D + p * 128 : D + (p + 1) * 128
                ].astype(BF)
            xhat, _ = normalise(x_s[at, :])
            a_s[at, :] = (xhat * gain).astype(BF)
            return carry

        blocks(rows, turn)

        dwo = dot_tn(gl_s[top, :], o_s[top, :])
        transposed_out(out, dwo, lambda b: pl.ds(384 + b * 64, 64))
        out.send(0, low_spot)
        for half in range(2):
            dwi = dot_tn(dp_s[top, half * 768 : (half + 1) * 768], a_s[top, :])
            for q in range(2):
                for b in range(2):
                    pair = [
                        dwi[q * 384 + r * 192 : q * 384 + (r + 1) * 192, b * LANES : (b + 1) * LANES] for r in range(2)
                    ]
                    out.put((2 * half + q, pl.ds(b * 192, 192), slice(None)), pair)
        out.send(1, high_spot)
        copies[6].wait()
        da_s[top, :] = dot_nt(dp_s[top, :], ain[...])

        def last(i, at, carry):
            xhat, inv = normalise(x_s[at, :])
            da = da_s[at, :]
            g_s[at, :] = g_s[at, :] + norm_back(da, xhat, inv, gain)
            return carry + fold(da * xhat)

        small_ref[0:1, :] = total(blocks(rows, last, jnp.zeros((8, D), F32)))

    return run


def attend_spec(l, cos, sin, gains, xs, q, kv, at, o, ain, aout):
    vm = pltpu.VMEM
    return (
        functools.partial(attend_part, l),
        [(v, VMEM) for v in (cos, sin, gains)] + [(v, ANY) for v in (xs, q, kv, at, o, ain, aout)],
        [
            (struct((4, 512, LANES), BF), ANY),
            (struct((4, 512, LANES), BF), ANY),
            (struct((8, D), F32), VMEM),
        ],
        [
            vm((CAP, D), F32), vm((CAP, D), BF), vm((CAP + 2 * BLK, 2 * D), BF),
            vm((CAP // BLK, PAIRS, 3 * BLK, 2 * BLK), BF), vm((CAP, D), BF), vm((D, 3 * D), BF), vm((D, D), BF),
            vm((CAP, D), BF), vm((CAP, D), BF), vm((CAP, D), BF), vm((CAP, D), F32),
            vm((CAP + 2 * BLK, 2 * D), F32), vm((CAP, 3 * D), BF), vm((CAP, D), F32),
            vm((2, 4, 512, LANES), BF),
            pltpu.SemaphoreType.DMA((8 + CAP // BLK,)), pltpu.SemaphoreType.DMA((4,)),
        ],
        16 * 640 * D * D,
    )


def run_parts(name, n, core, g, specs, deps):
    in_counts = [len(spec[1]) for spec in specs]
    out_counts = [len(spec[2]) for spec in specs]
    scratch_counts = [len(spec[3]) for spec in specs]

    def taken(refs, counts):
        pieces, off = [], 0
        for count in counts:
            pieces.append(refs[off : off + count])
            off += count
        return pieces

    def body(n_ref, core_ref, g_h, *refs):
        ins, refs = refs[: sum(in_counts)], refs[sum(in_counts) :]
        out_h, *outs = refs[: 1 + sum(out_counts)]
        g_s, g_sem, *scratch = refs[1 + sum(out_counts) :]
        parts = [
            spec[0](core_ref, g_s, *piece)
            for spec, *piece in zip(
                specs, taken(ins, in_counts), taken(outs, out_counts), taken(scratch, scratch_counts)
            )
        ]

        def run(rows):
            top = pl.ds(0, rows)
            steps = [part(rows) for part in parts]
            g_in = pltpu.make_async_copy(g_h.at[top], g_s.at[top], g_sem)
            g_in.start()
            steps[0][0]()
            g_in.wait()
            for i, (_, main, _) in enumerate(steps):
                main(steps[i + 1][0] if i + 1 < len(steps) else lambda: None)
            g_out = pltpu.make_async_copy(g_s.at[top], out_h.at[top], g_sem)
            g_out.start()
            for _, _, finish in steps:
                finish()
            g_out.wait()

        by_rows(n_ref, run)

    outs = [(struct((CAP, D), F32), ANY)] + [out for spec in specs for out in spec[2]]
    g, *rest = call(
        body,
        [SMEM, SMEM, ANY] + [where for spec in specs for _, where in spec[1]],
        outs,
        [pltpu.VMEM((CAP, D), F32), pltpu.SemaphoreType.DMA] + [v for spec in specs for v in spec[3]],
        (n, core, g, *(v for spec in specs for v, _ in spec[1])),
        flops=sum(spec[4] for spec in specs),
        moved=16 * 2**20,
        name=name,
        deps=deps,
    )
    return g, taken(rest, out_counts)


def add(*terms):
    acc = terms[0].astype(F32)
    for term in terms[1:]:
        acc = acc + term.astype(F32)
    return acc.astype(BF)


def spot_of(place_ref):
    x, y, core = place_ref[0], place_ref[1], place_ref[3]
    even = core == 0
    return jnp.where(even, x, y), jnp.where(even, y, x), 1 + core, 2 - core


def split_first_body(sizes, place_ref, *refs):
    count = len(sizes)
    keeps, gots = refs[:count], refs[count : 2 * count]
    kept, sent = refs[2 * count :]
    first, _, by_first, by_second = spot_of(place_ref)
    off = 0
    for keep, got, n in zip(keeps, gots, sizes):
        at = pl.ds(off, n)

        def one(z, carry, keep=keep, got=got, at=at):
            for j in range(2):
                own = first * by_first + j * by_second
                other = (1 - first) * by_first + j * by_second
                kept[z, j, at] = add(keep[z, own], got[z, own])
                sent[z, j, at] = add(keep[z, other], got[z, other])
            return carry

        lax.fori_loop(0, 4, one, jnp.int32(0))
        off += n


def split_second_body(sizes, place_ref, *refs):
    *ins, kept, sent = refs
    _, second, _, _ = spot_of(place_ref)
    off = 0
    for i, n in enumerate(sizes):
        keep, got = ins[2 * i : 2 * i + 2]
        at = pl.ds(off, n)

        def one(z, carry, keep=keep, got=got, at=at):
            kept[z, at] = add(keep[z, second], got[z, second])
            sent[z, at] = add(keep[z, 1 - second], got[z, 1 - second])
            return carry

        lax.fori_loop(0, 4, one, jnp.int32(0))
        off += n


def split_z_body(plan, place_ref, *refs):
    ins, outs = refs[:-4], refs[-4:]
    z = place_ref[2]
    for k, ref in enumerate(outs):
        at = lax.rem(z + k, 4)
        off = used = 0
        for count, n in plan:
            terms = [r[at] for r in ins[used : used + count]]
            ref[pl.ds(off, n), :] = add(*terms) if count > 1 else terms[0]
            used += count
            off += n


def along(axis):
    return [(r * 8 + t, (r ^ (1 << ((t + axis) % 2))) * 8 + t) for r in range(4) for t in range(8)]


def sum_cores_body(sizes, *refs):
    count = len(sizes)
    keeps, gots, out = refs[:count], refs[count : 2 * count], refs[2 * count]
    off = 0
    for keep, got, n in zip(keeps, gots, sizes):
        at = pl.ds(off, n)

        def one(z, carry, keep=keep, got=got, at=at):
            for j in range(4):
                out[j, z, at] = add(keep[z, j], got[z, j])
            return carry

        lax.fori_loop(0, 4, one, jnp.int32(0))
        off += n


class Group:
    def __init__(self, spot, members):
        self.spot = spot
        self.keeps = [keep for _, keep, _ in members]
        self.sizes = [keep.shape[1] // 4 for keep in self.keeps]
        self.names = [name for name, _, _ in members]
        self.n = sum(self.sizes)
        self.bytes = 16 * self.n * LANES * 2
        self.gots = [got for _, _, got in members]

    def cores(self):
        shaped = lambda v: v.reshape(4, 4, v.shape[1] // 4, LANES)
        return (*map(shaped, self.keeps), *map(shaped, self.gots))

    def offload(self, deps):
        both = call(
            functools.partial(sum_cores_body, self.sizes),
            [VMEM] * (2 * len(self.sizes)),
            [(struct((4, 4, self.n, LANES), BF), VMEM)],
            [],
            self.cores(),
            moved=3 * self.bytes,
            name="sum_cores",
            vmem=VMEM_SMALL,
            deps=deps,
        )[0]
        part = lax.psum_scatter(both, "rows", scatter_dimension=0, tiled=True)
        self.terms = [part.reshape(4, self.n, LANES)]
        return [both]

    def first(self, deps, work=0):
        self.kept, sent = call(
            functools.partial(split_first_body, self.sizes),
            [SMEM] + [VMEM] * (2 * len(self.sizes)),
            [(struct((4, 2, self.n, LANES), BF), VMEM)] * 2,
            [],
            (self.spot, *self.cores()),
            moved=3 * self.bytes,
            name="split_first",
            vmem=VMEM_SMALL,
            flops=work,
            deps=deps,
        )
        self.got = lax.ppermute(sent, ("rows", "tm"), along(0))
        return [self.kept]


class Second:
    def __init__(self, spot, groups, deps):
        sizes = [group.n for group in groups]
        self.n = sum(sizes)
        kept, sent = call(
            functools.partial(split_second_body, sizes),
            [SMEM] + [VMEM] * (2 * len(groups)),
            [(struct((4, self.n, LANES), BF), VMEM)] * 2,
            [],
            (spot, *(v for group in groups for v in (group.kept, group.got))),
            moved=24 * self.n * LANES * 2,
            name="split_second",
            vmem=VMEM_SMALL,
            deps=deps,
        )
        self.terms = [kept, lax.ppermute(sent, ("rows", "tm"), along(1))]


def merge_body(*refs):
    *ins, out = refs
    off = 0
    for ref in ins:
        n = ref.shape[1]
        out[:, pl.ds(off, n), :] = ref[...]
        off += n


def offloaded_rest(groups, deps):
    n = sum(group.n for group in groups)
    part = call(
        merge_body,
        [VMEM] * len(groups),
        [(struct((4, n, LANES), BF), VMEM)],
        [],
        [group.terms[0] for group in groups],
        moved=16 * n * LANES,
        name="merge",
        vmem=VMEM_SMALL,
        deps=deps,
    )[0]
    mine = lax.psum_scatter(
        part, "tm", scatter_dimension=0, tiled=True, axis_index_groups=[[0, 2, 4, 6], [1, 3, 5, 7]]
    )
    return mine.reshape(part.shape[1:])


def along_z(spot, groups, deps, work=0):
    ins = [term for group in groups for term in group.terms]
    n = sum(group.n for group in groups)
    own, *others = call(
        functools.partial(split_z_body, [(len(group.terms), group.n) for group in groups]),
        [SMEM] + [VMEM] * len(ins),
        [(struct((n, LANES), BF), VMEM)] * 4,
        [],
        (spot, *ins),
        moved=16 * n * LANES * 2,
        name="split_z",
        vmem=VMEM_SMALL,
        flops=work,
        deps=deps,
    )
    return [own] + [
        lax.ppermute(v, "tm", [(i, (i + 2 * k) % 8) for i in range(8)]) for k, v in zip((1, 2, 3), others)
    ]


def join_body(plan, *refs):
    *ins, out = refs
    off = at = 0
    for count, n in plan:
        out[pl.ds(at, n), :] = add(*(ref[...] for ref in ins[off : off + count])) if count > 1 else ins[off][...]
        off += count
        at += n


def gathered(lists, deps):
    ins = [term for terms in lists for term in terms]
    plan = [(len(terms), terms[0].shape[0]) for terms in lists]
    n = sum(rows for _, rows in plan)
    mine = call(
        functools.partial(join_body, plan),
        [VMEM] * len(ins),
        [(struct((n, LANES), BF), VMEM)],
        [],
        ins,
        moved=6 * n * LANES,
        name="join",
        deps=deps,
    )[0]
    one = lax.ppermute(mine, ("rows", "tm"), along(0))
    two = lax.ppermute(mine, ("rows", "tm"), along(1))
    return [mine, one, two, lax.ppermute(one, ("rows", "tm"), along(1))]


def finish_body(members, by_bit, me_ref, *refs):
    count = 4 if by_bit else 1
    chunks = refs[:count]
    fin_h, fout_h, ain_h, aout_h, pin_h, pout_h, small_h = refs[-13:-6]
    whole, fout, ain, pin, narrow, sem = refs[-6:]
    me = me_ref[0]
    rows = sum(n for _, _, n in members)
    off = 0
    waits = []
    for i, (l, name, n) in enumerate(members):
        for j in range(4):
            if by_bit:
                flip = (0, 1 + me_ref[1], 2 - me_ref[1], 3)[j]
                owner = pl.multiple_of(jnp.bitwise_xor(me, flip) * n, n)
                whole[i, pl.ds(owner, n), :] = chunks[j][pl.ds(off, n), :].astype(F32)
            else:
                whole[i, pl.ds(j * n, n), :] = chunks[0][pl.ds(j * rows + off, n), :].astype(F32)
        off += n
        if name in ("f0", "f1", "f0in", "f0out"):
            k = int(name == "f1")
            jobs = []
            if name != "f0out":
                jobs.append((whole.at[i, pl.ds(0, D)], fin_h.at[l, k]))
            if name != "f0in":
                base = 0 if name == "f0out" else D
                for b in range(FF // LANES):
                    fout[i, :, pl.ds(b * LANES, LANES)] = whole[i, pl.ds(base + b * 64, 64), :]
                jobs.append((fout.at[i], fout_h.at[l, k]))
            else:
                jobs.append((whole.at[i, pl.ds(D, SMALL_ROWS // 4)], small_h))
        elif name == "c":
            pin[i, pl.ds(0, 256), :] = whole[i, pl.ds(0, 256), 0:128]
            pin[i, pl.ds(256, 256), :] = whole[i, pl.ds(0, 256), 128:256]
            for b in range(2):
                narrow[i, :, pl.ds(b * LANES, LANES)] = whole[i, pl.ds(256 + b * 64, 64), :]
            jobs = [(pin.at[i], pin_h.at[l]), (narrow.at[i], pout_h.at[l])]
        else:
            for b in range(2):
                ain[i, :, pl.ds(b * LANES, LANES)] = whole[i, pl.ds(b * 192, 192), :]
                narrow[i, :, pl.ds(b * LANES, LANES)] = whole[i, pl.ds(384 + b * 64, 64), :]
            jobs = [(ain.at[i], ain_h.at[l]), (narrow.at[i], aout_h.at[l])]
        for j, (src, dst) in enumerate(jobs):
            c = pltpu.make_async_copy(src, dst, sem.at[3 * i + j])
            c.start()
            waits.append(c)
    for c in waits:
        c.wait()


def finish(layers, me, groups, chunks, before, deps=()):
    members = [(*name, size) for group in groups for name, size in zip(group.names, group.sizes)]
    count = len(members)
    shapes = [
        (layers, 2, D, FF // 8), (layers, 2, D // 8, FF), (layers, 3 * D // 8, D), (layers, D // 8, D),
        (layers, D, 2 * D // 8), (layers, D // 8, D), (SMALL_ROWS // 4, LANES),
    ]
    vm = pltpu.VMEM

    def body(*refs):
        finish_body(members, len(chunks) == 4, *refs)

    return pl.pallas_call(
        body,
        out_shape=[struct(shape, F32) for shape in shapes],
        in_specs=[SMEM] + [VMEM] * len(chunks) + [ANY] * (len(before) + len(deps)),
        out_specs=[ANY] * 7,
        scratch_shapes=[
            vm((count, 1024 + SMALL_ROWS, LANES), F32), vm((count, 64, FF), F32), vm((count, 192, D), F32),
            vm((count, D, 128), F32), vm((count, 64, D), F32), pltpu.SemaphoreType.DMA((3 * count,)),
        ],
        input_output_aliases={1 + len(chunks) + i: i for i in range(len(before))},
        compiler_params=pltpu.CompilerParams(vmem_limit_bytes=VMEM_LIMIT),
        name="finish",
    )(me, *chunks, *before, *deps)


def per_device(
    frames, segment_ids, norm_gains, feed_in, feed_out, attend_in, attend_out, point_in, depthwise, stat_mean,
    stat_var, batch_scale, batch_shift, point_out, cotangent,
):
    batches, row_count, frame_count, model_dim = frames.shape
    layers = norm_gains.shape[0]
    tm_size = lax.axis_size("tm")
    rows_size = lax.axis_size("rows")
    tm = lax.axis_index("tm")
    row = lax.axis_index("rows")
    fast = tm_size == 8 and rows_size == 4
    half = batches // 2

    ids = segment_ids[:, 0] + 1
    id_rows = jnp.broadcast_to(ids.reshape(1, -1).astype(BF), (16, batches * frame_count))
    parts_of = lambda v, odd: v.reshape(half, 2, frame_count, model_dim)[:, odd].reshape(-1, model_dim)
    message = lambda odd: jnp.concatenate([parts_of(frames, odd), parts_of(cotangent, odd), id_rows], axis=0)
    above = shifted(message(0), "tm", -1)
    below = shifted(message(1), "tm", 1)
    flat = lambda v: v.reshape(batches * frame_count, model_dim)
    x0, g, chooser, cos, sin, kb, kr, n = pack(ids.astype(F32), flat(frames), flat(cotangent), below, above)
    small = (norm_gains, depthwise, stat_mean, stat_var, batch_scale, batch_shift)
    mats = (feed_in, feed_out, attend_in, attend_out, point_in, point_out)
    act, xs, hs, q, kv, at, o, u, z = forward(n, x0, cos, sin, kb, kr, small, mats)

    def filled(v):
        return jnp.where(lax.broadcasted_iota(jnp.int32, v.shape, 0) < n[0], v, 0.0).astype(BF)

    def spread(packed):
        wide = jnp.concatenate(packed, axis=1)
        frames_of = lax.dot_general(chooser, wide, (((0,), (0,)), ((), ())), preferred_element_type=F32)
        return frames_of.astype(BF)

    def crossing(windows_of):
        windows_of = windows_of.reshape(half, 2, 2, frame_count, 2 * model_dim)
        return [shifted(windows_of[:, 0, 1], "tm", 1), shifted(windows_of[:, 1, 0], "tm", -1)]

    def unpacked(windows_of, from_below, from_above):
        windows_of = windows_of.reshape(half, 2, 2, frame_count, 2 * model_dim)
        even = windows_of[:, 0, 0] + from_below
        odd = windows_of[:, 1, 1] + from_above
        frames_out = jnp.stack([even, odd], axis=1).reshape(batches, 1, frame_count, 2 * model_dim)
        return jnp.split(frames_out, 2, axis=-1)

    if fast:
        spot = jnp.stack([row % 2, row // 2, tm // 2, tm % 2]).astype(jnp.int32)
        core = (tm % 2).astype(jnp.int32).reshape(1)
    else:
        spot = None
        core = jnp.zeros((1,), jnp.int32)

    members = {}
    smalls = {}
    parts = {
        "f1": lambda l: feed_spec(l, 1, "all", (), norm_gains, xs, hs, feed_in, feed_out),
        "c": lambda l: conv_spec(l, kb, small, xs, u, z, point_in, point_out),
        "a": lambda l: attend_spec(l, cos, sin, norm_gains, xs, q, kv, at, o, attend_in, attend_out),
        "f0": lambda l: feed_spec(l, 0, "all", (), norm_gains, xs, hs, feed_in, feed_out),
        "f0out": lambda l: feed_spec(l, 0, "out", (), norm_gains, xs, hs, feed_in, feed_out),
        "f0in": lambda l, rest: feed_spec(l, 0, "in", rest, norm_gains, xs, hs, feed_in, feed_out),
    }
    order = [(l, name) for l in range(layers) for name in ("f0", "a", "c", "f1")]

    def back(l, *names, deps=(), **more):
        nonlocal g
        specs = [parts[name](l, **more) for name in names]
        g, outs = run_parts(f"back_{l}_{'_'.join(names)}", n, core, g, specs, deps)
        for name, (kept, sent, small_grads) in zip(names, outs):
            smalls[l, name] = small_grads
            members[l, name] = ((l, name), kept, sent)

    crossed = {}

    def begin(l, name):
        crossed[l, name] = lax.ppermute(members[l, name][2], "tm", [(i, i ^ 1) for i in range(8)])

    def group(*names):
        for name in names:
            if name not in crossed:
                begin(*name)
        return Group(spot, [(name, members[name][1], crossed[name]) for name in names])

    if fast:
        me = jnp.stack([2 * spot[1] + spot[0], spot[3]])
        back(1, "f1", "c")
        one = group((1, "f1"), (1, "c"))
        made = one.offload([])
        back(1, "a", "f0", deps=made)
        begin(1, "a")
        begin(1, "f0")
        back(0, "f1")
        begin(0, "f1")
        two = group((1, "a"), (1, "f0"))
        made = two.offload([g])
        back(0, "c", deps=made + one.terms)
        begin(0, "c")
        three = group((0, "f1"))
        made = three.first([g])
        back(0, "a", "f0out", deps=made)
        four = group((0, "c"), (0, "a"), (0, "f0out"))
        three_next = Second(spot, [three], [g])
        made = three_next.terms[:1] + four.first(three_next.terms[:1])
        z_early = offloaded_rest([one, two], made)
        back(0, "f0in", deps=made + two.terms, rest=[smalls[name] for name in order[1:]])
        five = group((0, "f0in"))
        z_three = along_z(spot, [three_next], [g, four.got], TAIL_WORK)
        made = five.first(z_three[:1])
        home = spread([act, filled(g)])
        crossed_home = crossing(home)
        last = Second(spot, [four, five], made + crossed_home)
        z_last = along_z(spot, [last], z_three[1:])
        chunks_early = gathered([[z_early], z_three], z_last[:1])
        chunks_late = gathered([z_last], chunks_early[1:])
        outs = finish(layers, me, [one, two, three], chunks_early, [], chunks_late[:1])
        *mats_out, small_out = finish(layers, me, [four, five], chunks_late, outs)
        mats_out = [
            v.swapaxes(-1, -2) if turned else v for v, turned in zip(mats_out, (False, True, True, True, False, True))
        ]
        lines = small_out.reshape(-1, 4, 64).swapaxes(0, 1).reshape(-1, 64)
        starts = {name: 0 for name in order}
        at_row = 0
        smalls[0, "f0"] = smalls[0, "f0in"]
        for name in order:
            starts[name] = at_row
            at_row += smalls[name].shape[0]
        pieces = lambda name, first, count: [
            lines[starts[l, name] + first : starts[l, name] + first + count] for l in range(layers)
        ]
    else:
        for l in reversed(range(layers)):
            back(l, "f1", "c")
            back(l, "a", "f0")
        pieces = None
        home = spread([act, filled(g)])
        crossed_home = crossing(home)
    activations, frames_grad = unpacked(home, *crossed_home)

    if not fast:
        mats_out, lines_of = general_sums(layers, members, smalls, order)
        pieces = lambda name, first, count: [lines_of[l, name][first : first + count] for l in range(layers)]
    gains_out = jnp.stack(
        [
            jnp.concatenate(rows, axis=0)
            for rows in zip(
                pieces("f0", 0, 1), pieces("a", 0, 1), pieces("c", 0, 1), pieces("f1", 0, 1), pieces("f1", 1, 1)
            )
        ]
    )
    fin, fout, ain, aout, pin, pout = mats_out
    return (
        activations,
        frames_grad,
        gains_out,
        fin,
        fout,
        ain,
        aout,
        pin,
        jnp.stack(pieces("c", 8, KERNEL)),
        jnp.concatenate(pieces("c", 1, 1), axis=0),
        jnp.concatenate(pieces("c", 2, 1), axis=0),
        pout,
    )


def general_sums(layers, members, smalls, order):
    def natural(l, name):
        _, even, odd = members[l, name]
        return jnp.stack([even, odd], axis=1).astype(F32).reshape(8, -1, LANES)

    def wide(v, count):
        r = v.shape[1] // count
        return jnp.swapaxes(v.reshape(8, count, r, LANES), 1, 2).reshape(8 * r, count * LANES)

    def over_all(v):
        v = lax.psum_scatter(v, "tm", scatter_dimension=v.ndim - 1, tiled=True)
        return lax.psum(v, "rows")

    fin, fout, ain, aout, pin, pout = [], [], [], [], [], []
    for l in range(layers):
        f = [natural(l, "f0"), natural(l, "f1")]
        fin.append(jnp.stack([jnp.moveaxis(v[:, :D], 0, 1).reshape(D, FF) for v in f]))
        fout.append(jnp.stack([wide(v[:, D:], FF // LANES).T for v in f]))
        v = natural(l, "a")
        ain.append(wide(v[:, :384], 2).T)
        aout.append(wide(v[:, 384:], 2).T)
        v = natural(l, "c")
        top = jnp.concatenate([v[:, :256, :128], v[:, :256, 128:]], axis=1)
        pin.append(jnp.moveaxis(top, 0, 1).reshape(D, 2 * D))
        pout.append(wide(v[:, 256:], 2).T)
    mats_out = [over_all(jnp.stack(v)) for v in (fin, fout, ain, aout, pin, pout)]
    small_all = over_all(jnp.concatenate([smalls[name] for name in order], axis=0))
    lines_of = {}
    at = 0
    for name in order:
        rows = smalls[name].shape[0]
        lines_of[name] = small_all[at : at + rows]
        at += rows
    return mats_out, lines_of


def solution(mesh):
    rep = P()
    in_specs = (
        P(None, "rows", "tm", None), P(None, "rows", "tm"), rep, rep, rep, rep, rep, rep, rep, rep, rep, rep, rep, rep,
        P(None, "rows", "tm", None),
    )
    out_specs = (
        P(None, "rows", "tm", None), P(None, "rows", "tm", None), P(None, None, "tm"), P(None, None, None, "tm"),
        P(None, None, None, "tm"), P(None, None, "tm"), P(None, None, "tm"), P(None, None, "tm"),
        P(None, None, "tm"), P(None, "tm"), P(None, "tm"), P(None, None, "tm"),
    )
    return jax.shard_map(per_device, mesh=mesh, in_specs=in_specs, out_specs=out_specs, check_vma=False)
```
